32 devices in a mesh: dp: 8 (over z, x), hst: 4 (over y, core).
Axes of the slice: x: 2, y: 2, z: 4, core: 2. Of those that a mesh axis runs over, the one named last changes fastest.
Arguments:
- tokens: bfloat16 [128, 7168], P('dp', 'hst'), may hold values from -6 to 6
- cotangent: bfloat16 [128, 7168], P('dp', 'hst'), may hold values from -6 to 6
- expert_ids: int32 [128, 2], P('dp'), may hold values from 0 to 7, all different within a row; in each aligned block of 16 rows (0 to 15, 16 to 31, ...) at most 4 rows name the same one
- gate_values: float32 [128, 2], P('dp'), may hold values from 0.2 to 1
- w_gate: bfloat16 [8, 4864, 7168], P('hst', 'dp'), may hold values from -0.0625 to 0.0625
- w_up: bfloat16 [8, 4864, 7168], P('hst', 'dp'), may hold values from -0.0625 to 0.0625
- w_down: bfloat16 [8, 4864, 7168], P('hst', 'dp'), may hold values from -0.078125 to 0.078125
Outputs:
- mixed: bfloat16 [128, 7168], P('dp', 'hst')
- grad_tokens: bfloat16 [128, 7168], P('dp', 'hst')
- grad_gate: bfloat16 [8, 4864, 7168], P('hst', 'dp')
- grad_up: bfloat16 [8, 4864, 7168], P('hst', 'dp')
- grad_down: bfloat16 [8, 4864, 7168], P('hst', 'dp')
The draws below stay inside these ranges and needn't reach their ends.
Inputs may be any that keep to these rules, and one draw needn't show every extreme that they name: `expert_ids`: within each block of 16 rows (the rows of one index of dp), a token names two different experts, and no expert is named by more than 4 routes; since a block has 8 routes and 8 slots, every expert fills all 4 of its slots in every block.
All inputs are finite; a program needn't handle non-finite values.
Results may differ from the reference program's by a relative error of at most 0.023.
Values may be sent and summed in bfloat16 or wider, within the bound.
No kernel may reach another device: no remote copies, remote signals or barrier semaphores. Data moves between devices by JAX's collectives and lax.ppermute only.
A program may use at most 192 MiB of HBM per device.

```python
import math
import jax
import jax.numpy as jnp
import numpy as np
from jax import lax

D = 7168
FF_E = 4864
EXPERTS = 8
TOK_DEV = 16
CAP = 4
TOKENS = 128
N_DP = 8


def levels(rng, dims, cuts, least, largest):
    factor_of, own = 1.0, jax.random.fold_in(rng, 6)
    for dim, shards_of in cuts:
        heights = jnp.exp(jax.random.uniform(jax.random.fold_in(own, dim), (shards_of,), jnp.float32, least / len(cuts), largest / len(cuts)))
        factor_of = factor_of * jnp.repeat(heights, dims[dim] // shards_of).reshape([-1 if axis == dim else 1 for axis in range(len(dims))])
    return factor_of


def assign_block(rng, own, number, rows, number_of, top, reach, skew):
    sequence = jax.random.permutation(rng, number_of)
    packed, common = portions_of(number_of, rows * top, reach, skew, True), portions_of(number_of, rows * top, reach, skew, False)
    places = jnp.arange(number_of)

    def named(sizes, rotation):
        used = int((sizes > 0).sum())
        fixed = max(1, used // 4)
        passed = fixed + (places - fixed + rotation * (used - fixed)) % max(1, number_of - fixed)
        return jnp.zeros((number_of,), jnp.int32).at[sequence[jnp.where(places < fixed, places, passed)]].set(jnp.asarray(sizes, jnp.int32))

    sizes = jnp.where(number % 4 == 0, named(packed, number // 4), named(common, number - number // 4 - 1))
    mixed = jax.random.permutation(jax.random.fold_in(own, 3), number_of)
    donor, sink = mixed[0:number_of // 2 * 2:2], mixed[1:number_of // 2 * 2:2]
    slack = jnp.minimum(sizes[donor] - 1, reach - sizes[sink]) // 2
    slack = jnp.where((donor == sequence[0]) | (sink == sequence[0]) | (sizes[sink] == 0), 0, jnp.maximum(slack, 0))
    passed = jax.random.randint(jax.random.fold_in(own, 4), (number_of // 2,), 0, 1 << 20) % (slack + 1)
    sizes = sizes.at[donor].add(-passed).at[sink].add(passed)
    items = jnp.searchsorted(jnp.cumsum(sizes), jnp.arange(rows * top), side="right").astype(jnp.int32)
    grid = items.reshape(top, rows).T
    grid = grid[jax.random.permutation(jax.random.fold_in(own, 1), rows)]
    rotation = jax.random.randint(jax.random.fold_in(own, 2), (rows, 1), 0, top)
    return jnp.take_along_axis(grid, (jnp.arange(top)[None, :] + rotation) % top, axis=1)


def portions_of(number_of, total, limit, skew, full):
    loads = [(1 << 20) // math.isqrt(grade ** skew) + 1 for grade in range(1, number_of + 1)]
    largest = limit if full else min(limit, max(-(-total // number_of), total * loads[0] // sum(loads)))
    least = 1 if total - largest >= number_of - 1 else 0
    given, rest = [largest] + [least] * (number_of - 1), total - largest - least * (number_of - 1)
    while rest > 0:
        candidates = [i for i in range(1, number_of) if given[i] < largest] or [i for i in range(1, number_of) if given[i] < limit]
        pool, left = sum([loads[i] for i in candidates]), rest
        for i in candidates:
            addition = min(limit - given[i], max(1, left * loads[i] // pool), rest)
            given[i] = given[i] + addition
            rest = rest - addition
    return np.array(given)


def noise(key, shape, scale, reach, cuts=(), kind=jnp.bfloat16):
    result = jax.random.normal(key, shape, jnp.float32) * scale
    if len(cuts) > 0:
        result = levels(key, shape, cuts, -0.22, 0.18) * result
    return jnp.clip(result, min=-reach, max=reach).astype(kind)


def setup_inputs(seed: int = 0) -> dict:
    streams_of = jax.random.split(jax.random.key(seed), 8)
    tokens = noise(streams_of[0], (TOKENS, D), 1.0, 6.0, ((0, 8), (1, 4)))
    cotangent = noise(streams_of[1], (TOKENS, D), 1.0, 6.0, ((0, 8), (1, 4)))
    expert_ids_keys = jax.random.split(jax.random.fold_in(streams_of[2], 1), TOKENS // TOK_DEV)
    expert_ids_turns = jax.random.permutation(jax.random.fold_in(streams_of[2], 3), TOKENS // TOK_DEV)
    expert_ids = jax.vmap(lambda own, number: assign_block(jax.random.fold_in(streams_of[2], 2), own, number, TOK_DEV, EXPERTS, 2, CAP, 1))(expert_ids_keys, expert_ids_turns).reshape((TOKENS, 2))
    gate_values = jnp.clip(0.2 + 0.8 * jax.random.uniform(streams_of[3], (TOKENS, 2), jnp.float32) ** levels(streams_of[3], (TOKENS, 2), ((0, 8),), -0.2, 0.2), 0.2, 1.0)
    w_gate = noise(streams_of[4], (EXPERTS, FF_E, D), D ** -0.5, 0.0625, ((0, 4), (1, 8)))
    w_up = noise(streams_of[5], (EXPERTS, FF_E, D), D ** -0.5, 0.0625, ((0, 4), (1, 8)))
    w_down = noise(streams_of[6], (EXPERTS, FF_E, D), FF_E ** -0.5, 0.078125, ((0, 4), (1, 8)))
    return dict(tokens=tokens, cotangent=cotangent, expert_ids=expert_ids, gate_values=gate_values, w_gate=w_gate, w_up=w_up, w_down=w_down)


def route_tables(expert_ids, gate_values, experts, cap):
    count = expert_ids.shape[0]
    flat = expert_ids.reshape(-1)
    labels = jnp.arange(experts, dtype=jnp.int32)
    onehot = (flat[:, None] == labels[None, :]).astype(jnp.int32)
    position = jnp.cumsum(onehot, axis=0) - onehot
    slot = jnp.sum(position * onehot, axis=1)
    slots = jnp.arange(cap, dtype=jnp.int32)
    hit = (flat[:, None, None] == labels[None, :, None]) & (slot[:, None, None] == slots[None, None, :])
    hit = hit.astype(jnp.float32).reshape(count, 2, experts, cap)
    select = jnp.transpose(jnp.sum(hit, axis=1), (1, 2, 0))
    weigh = jnp.transpose(jnp.sum(hit * gate_values[:, :, None, None], axis=1), (1, 2, 0))
    return select, weigh


def sliced_sum(left, right, width, pieces, rows):
    def add_slice(index, total):
        part = jnp.dot(lax.dynamic_slice_in_dim(left, index * width, width, 1),
                       lax.dynamic_slice_in_dim(right, index * width, width, 0),
                       preferred_element_type=jnp.float32)
        rounded = lax.optimization_barrier(part.astype(jnp.bfloat16))
        return total + rounded.astype(jnp.float32)
    return lax.fori_loop(0, pieces, add_slice, jnp.zeros((rows, right.shape[1]), jnp.float32))


def reference(tokens, cotangent, expert_ids, gate_values, w_gate, w_up, w_down):
    hp = lax.Precision.HIGHEST
    blocks = N_DP
    rows = blocks * CAP
    width = FF_E // N_DP
    x_blocks = tokens.reshape(blocks, TOK_DEV, D).astype(jnp.float32)
    d_blocks = cotangent.reshape(blocks, TOK_DEV, D).astype(jnp.float32)
    select, weigh = jax.vmap(lambda a, b: route_tables(a, b, EXPERTS, CAP))(
        expert_ids.reshape(blocks, TOK_DEV, 2), gate_values.reshape(blocks, TOK_DEV, 2))
    x_rows = jnp.einsum('becT,bTd->ebcd', select, x_blocks, precision=hp).astype(jnp.bfloat16).reshape(EXPERTS, rows, D)
    d_rows = jnp.einsum('becT,bTd->ebcd', weigh, d_blocks, precision=hp).astype(jnp.bfloat16).reshape(EXPERTS, rows, D)

    def one_expert(pack):
        xr, dr, wg, wu, wd = pack
        g = jnp.dot(xr, wg.T, preferred_element_type=jnp.float32)
        u = jnp.dot(xr, wu.T, preferred_element_type=jnp.float32)
        sig = jax.nn.sigmoid(g)
        act = (g * sig * u).astype(jnp.bfloat16)
        out = sliced_sum(act, wd, width, N_DP, rows)
        da = jnp.dot(dr, wd.T, preferred_element_type=jnp.float32)
        dg = (da * u * sig * (1.0 + g * (1.0 - sig))).astype(jnp.bfloat16)
        du = (da * g * sig).astype(jnp.bfloat16)
        gdown = jnp.dot(act.T, dr, preferred_element_type=jnp.float32).astype(jnp.bfloat16)
        ggate = jnp.dot(dg.T, xr, preferred_element_type=jnp.float32).astype(jnp.bfloat16)
        gup = jnp.dot(du.T, xr, preferred_element_type=jnp.float32).astype(jnp.bfloat16)

        def add_slice(index, total):
            dgs = lax.dynamic_slice_in_dim(dg, index * width, width, 1)
            dus = lax.dynamic_slice_in_dim(du, index * width, width, 1)
            wgs = lax.dynamic_slice_in_dim(wg, index * width, width, 0)
            wus = lax.dynamic_slice_in_dim(wu, index * width, width, 0)
            part = jnp.dot(dgs, wgs, preferred_element_type=jnp.float32) + jnp.dot(dus, wus, preferred_element_type=jnp.float32)
            rounded = lax.optimization_barrier(part.astype(jnp.bfloat16))
            return total + rounded.astype(jnp.float32)
        back = lax.fori_loop(0, N_DP, add_slice, jnp.zeros((rows, D), jnp.float32))
        return out, back, ggate, gup, gdown

    outs, backs, grad_gate, grad_up, grad_down = lax.map(one_expert, (x_rows, d_rows, w_gate, w_up, w_down))
    outs = outs.reshape(EXPERTS, blocks, CAP, D)
    backs = backs.reshape(EXPERTS, blocks, CAP, D)
    mixed = jnp.einsum('becT,ebcd->bTd', weigh, outs, precision=hp).astype(jnp.bfloat16).reshape(TOKENS, D)
    grad_tokens = jnp.einsum('becT,ebcd->bTd', select, backs, precision=hp).astype(jnp.bfloat16).reshape(TOKENS, D)
    return mixed, grad_tokens, grad_gate, grad_up, grad_down
```

```python
import functools

import jax
import jax.numpy as jnp
from jax import lax
from jax.experimental import pallas as pl
from jax.experimental.pallas import tpu as pltpu
from jax.sharding import PartitionSpec as P

CAP = 4
LANES = 128
MIB = 1 << 20
F32 = jnp.float32
BF16 = jnp.bfloat16
AXES = ("dp", "hst")


def dot(a, b):
    return lax.dot_general(a, b, (((1,), (0,)), ((), ())), preferred_element_type=F32)


def dot_t(a, b):
    return lax.dot_general(a, b, (((1,), (1,)), ((), ())), preferred_element_type=F32)


def log2(n):
    assert n & (n - 1) == 0
    return n.bit_length() - 1


class Grid:
    def __init__(self, dp, hst):
        self.dp, self.hst = dp, hst
        self.nc = 2 if hst % 2 == 0 else 1
        self.ny = hst // self.nc
        self.nx = self.ny if dp % self.ny == 0 else 1
        self.nz = dp // self.nx
        self.square = [(a, b) for a in range(self.nx) for b in range(self.ny)]

    def shift(self, value, dz=0, dx=0, dy=0, dc=0):
        pairs = []
        for z in range(self.nz):
            for x in range(self.nx):
                for y in range(self.ny):
                    for c in range(self.nc):
                        to_dp = (z + dz) % self.nz * self.nx + (x + dx) % self.nx
                        to_hst = (y + dy) % self.ny * self.nc + (c + dc) % self.nc
                        here = (z * self.nx + x) * self.hst + y * self.nc + c
                        pairs.append((here, to_dp * self.hst + to_hst))
        return lax.ppermute(value, AXES, pairs)


def gather(grid, mine):
    parts = [mine] + [grid.shift(mine, dz=k) for k in range(1, grid.nz)]
    column = jnp.concatenate(parts, axis=0)
    plane = {
        (a, b): column if (a, b) == (0, 0) else grid.shift(column, dx=a, dy=b)
        for a, b in grid.square
    }
    planes = [plane]
    for c in range(1, grid.nc):
        planes.append({at: grid.shift(block, dc=c) for at, block in plane.items()})
    return planes


def scatter_sum(grid, parts, rows):
    kept = parts[0].astype(F32)
    for c in range(1, grid.nc):
        kept = kept + grid.shift(parts[c], dc=-c).astype(F32)
    kept = kept.astype(BF16)
    total = kept[0, 0].astype(F32)
    for a, b in grid.square[1:]:
        total = total + grid.shift(kept[a, b], dx=-a, dy=-b).astype(F32)
    total = total.astype(BF16)
    result = total[:rows].astype(F32)
    for k in range(1, grid.nz):
        block = lax.slice_in_dim(total, k * rows, (k + 1) * rows, axis=0)
        result = result + grid.shift(block, dz=-k).astype(F32)
    return result.astype(BF16)


def tables(aux, first, rows, local, block):
    tokens = aux.shape[0]
    across = jnp.transpose(aux.astype(F32))
    ids = [across[k : k + 1] for k in range(2)]
    gates = [across[2 + k : 3 + k] + across[4 + k : 5 + k] + across[6 + k : 7 + k] for k in range(2)]
    total = local * rows
    r = lax.broadcasted_iota(jnp.int32, (total, tokens), 0)
    j = lax.broadcasted_iota(jnp.int32, (total, tokens), 1)
    expert = ((r >> log2(rows)) + first).astype(F32)
    own_block = ((r & (rows - 1)) >> log2(CAP)) == (j >> log2(block))
    slot = (r & (CAP - 1)).astype(F32)
    hits = [(ids[k] == expert).astype(F32) for k in range(2)]
    hit = hits[0] + hits[1]
    up = lax.broadcasted_iota(jnp.int32, (tokens, tokens), 0)
    to = lax.broadcasted_iota(jnp.int32, (tokens, tokens), 1)
    earlier = ((up >> log2(block)) == (to >> log2(block))) & (up < to)
    position = dot(hit.astype(BF16), jnp.where(earlier, 1.0, 0.0).astype(BF16))
    select = jnp.where(own_block & (position == slot), hit, 0.0)
    gate = jnp.sum(select * (hits[0] * gates[0] + hits[1] * gates[1]), axis=1, keepdims=True)
    return select, gate


def route(blocks, select, out_ref, width, chunk):
    index = 0
    for plane in blocks:
        for group in plane:
            whole = jnp.concatenate([ref[:, :width] for ref in group], axis=0)
            picked = dot(select, whole)
            for at in range(0, width, chunk):
                yield index, picked[:, at : at + chunk]
                index += 1


def first_kernel(shape, place_ref, *refs):
    grid, local, rows, block, width, chunk, chunks = shape
    count = grid.nc * grid.ny * grid.nx
    it = iter(refs[:count])
    blocks = [[[next(it) for _ in range(grid.nx)] for _ in range(grid.ny)] for _ in range(grid.nc)]
    (wg_ref, wu_ref, x_ref, select_ref, back_ref, gate_ref, act_ref, p_ref, q_ref, g_acc, u_acc) = refs[count:]
    step = pl.program_id(0)

    @pl.when(step == 0)
    def _():
        aux = jnp.concatenate([ref[:, width : width + LANES] for ref in blocks[0][0]], axis=0)
        select, gate = tables(aux, place_ref[chunks], rows, local, block)
        gate_ref[...] = jnp.broadcast_to(gate, gate_ref.shape)
        select_ref[...] = select.astype(BF16)
        back_ref[...] = jnp.transpose(select).astype(BF16)
        for index, picked in route(blocks, select.astype(BF16), x_ref, width, chunk):
            x_ref[index] = picked.astype(BF16)
        g_acc[...] = jnp.zeros_like(g_acc)
        u_acc[...] = jnp.zeros_like(u_acc)

    x = x_ref[step]
    for e in range(local):
        mine = x[e * rows : (e + 1) * rows]
        g_acc[e] += dot_t(mine, wg_ref[e])
        u_acc[e] += dot_t(mine, wu_ref[e])

    @pl.when(step == chunks - 1)
    def _():
        g, u = g_acc[...], u_acc[...]
        sigma = jax.nn.sigmoid(g)
        act_ref[...] = (g * sigma * u).astype(BF16)
        p_ref[...] = u * sigma * (1.0 + g * (1.0 - sigma))
        q_ref[...] = g * sigma


def forward_kernel(local, rows, half, place_ref, act_ref, gate_ref, back_ref, w_ref, own_ref, other_ref, o_rows):
    step = pl.program_id(0)
    for e in range(local):
        at = slice(e * rows, (e + 1) * rows)
        o_rows[at] = (dot(act_ref[e], w_ref[e]) * gate_ref[at, :1]).astype(BF16)
    put(step, half, dot(back_ref[...], o_rows[...]).astype(BF16), own_ref, other_ref)


def put(step, half, value, own_ref, other_ref):
    @pl.when(step < half)
    def _():
        own_ref[...] = value.reshape(own_ref.shape)

    @pl.when(step >= half)
    def _():
        other_ref[...] = value.reshape(other_ref.shape)


def second_kernel(shape, place_ref, *refs):
    grid, local, rows, block, width, chunk, chunks = shape
    count = grid.nc * grid.ny * grid.nx
    it = iter(refs[:count])
    blocks = [[[next(it) for _ in range(grid.nx)] for _ in range(grid.ny)] for _ in range(grid.nc)]
    (select_ref, gate_ref, p_ref, q_ref, w_ref, d_ref, dg_ref, du_ref, acc) = refs[count:]
    step = pl.program_id(0)

    @pl.when(step == 0)
    def _():
        for index, picked in route(blocks, select_ref[...], d_ref, width, chunk):
            d_ref[index] = (picked * gate_ref[:, :1]).astype(BF16)
        acc[...] = jnp.zeros_like(acc)

    d = d_ref[step]
    for e in range(local):
        acc[e] += dot_t(d[e * rows : (e + 1) * rows], w_ref[e])

    @pl.when(step == chunks - 1)
    def _():
        da = acc[...]
        dg_ref[...] = (da * p_ref[...]).astype(BF16)
        du_ref[...] = (da * q_ref[...]).astype(BF16)


def back_kernel(local, rows, half, place_ref, dg_ref, du_ref, back_ref, wg_ref, wu_ref, own_ref, other_ref, o_rows):
    step = pl.program_id(0)
    for e in range(local):
        at = slice(e * rows, (e + 1) * rows)
        o_rows[at] = (dot(dg_ref[e], wg_ref[e]) + dot(du_ref[e], wu_ref[e])).astype(BF16)
    put(step, half, dot(back_ref[...], o_rows[...]).astype(BF16), own_ref, other_ref)


def grads_kernel(local, rows, count, place_ref, *refs):
    lefts, (rows_ref,) = refs[:count], refs[count : count + 1]
    outs, turned = refs[count + 1 : 2 * count + 1], refs[2 * count + 1 :]

    @pl.when(pl.program_id(0) == 0)
    def _():
        for left, turn in zip(lefts, turned):
            for e in range(local):
                turn[e] = jnp.transpose(left[e].astype(F32)).astype(BF16)

    right = rows_ref[0]
    for turn, out in zip(turned, outs):
        for e in range(local):
            out[e] = dot(turn[e], right[e * rows : (e + 1) * rows]).astype(BF16)


def body(tokens, cotangent, expert_ids, gate_values, w_gate, w_up, w_down):
    grid = Grid(lax.axis_size("dp"), lax.axis_size("hst"))
    local, hidden, features = w_gate.shape
    block, width = tokens.shape
    rows = grid.dp * CAP
    total = local * rows
    chunk = 896 if width % 896 == 0 else width
    per = width // chunk
    chunks = features // chunk
    half = chunks // grid.nc
    count = grid.dp * block
    column = grid.nz * block
    shape = (grid, local, rows, block, width, chunk, chunks)

    host = lax.axis_index("hst")
    y, core = host // grid.nc, host % grid.nc
    i = jnp.arange(chunks, dtype=jnp.int32)
    dc, dy, sub = i // (per * grid.ny), i // per % grid.ny, i % per
    source = ((y - dy) % grid.ny) * grid.nc + (core + dc) % grid.nc
    place = jnp.concatenate([source * per + sub, (host * local)[None]]).astype(jnp.int32)

    high = lax.reduce_precision(gate_values, 8, 7)
    rest = gate_values - high
    middle = lax.reduce_precision(rest, 8, 7)
    aux = jnp.concatenate([expert_ids.astype(F32), high, middle, rest - middle], axis=1)
    aux = jnp.pad(aux.astype(BF16), ((0, 0), (0, LANES - aux.shape[1])))
    x_planes = gather(grid, jnp.concatenate([tokens, aux], axis=1))
    d_planes = gather(grid, cotangent)

    def flat(planes):
        return [p[a, b] for p in planes for b in range(grid.ny) for a in range(grid.nx)]

    whole = lambda *dims: pl.BlockSpec(dims, lambda i, place: (0,) * len(dims))
    weight = pl.BlockSpec((local, hidden, chunk), lambda i, place: (0, 0, place[i]))
    hidden_shape = (local, rows, hidden)
    sums = (grid.nx, grid.ny, column, width)
    sum_block = (grid.nx, 1, column, chunk)
    own = pl.BlockSpec(sum_block, lambda i, place: (0, jnp.minimum(i, half - 1) // per, 0, jnp.minimum(i, half - 1) % per))
    other = pl.BlockSpec(sum_block, lambda i, place: (0, jnp.maximum(i - half, 0) // per, 0, jnp.maximum(i - half, 0) % per))
    pass_flops = 2 * total * hidden * features
    pass_bytes = 2 * local * hidden * features

    def call(kernel, name, ins, outs, args, scratch=(), passes=1, limit=40):
        return pl.pallas_call(
            kernel,
            name=name,
            out_shape=[o[0] for o in outs],
            grid_spec=pltpu.PrefetchScalarGridSpec(
                num_scalar_prefetch=1,
                grid=(chunks,),
                in_specs=ins,
                out_specs=[o[1] for o in outs],
                scratch_shapes=list(scratch),
            ),
            compiler_params=pltpu.CompilerParams(
                dimension_semantics=("arbitrary",), vmem_limit_bytes=limit * MIB
            ),
            cost_estimate=pl.CostEstimate(
                flops=passes * pass_flops, bytes_accessed=passes * pass_bytes, transcendentals=0
            ),
        )(place, *args)

    def full(dtype, *dims):
        return (jax.ShapeDtypeStruct(dims, dtype), whole(*dims))

    x_blocks, d_blocks = flat(x_planes), flat(d_planes)
    routed = full(BF16, chunks, total, chunk)
    x_rows, select, back, gate, act, p, q = call(
        functools.partial(first_kernel, shape),
        "gate_up",
        [whole(column, width + LANES)] * len(x_blocks) + [weight, weight],
        [
            routed,
            full(BF16, total, count),
            full(BF16, count, total),
            full(F32, total, LANES),
            full(BF16, *hidden_shape),
            full(F32, *hidden_shape),
            full(F32, *hidden_shape),
        ],
        [*x_blocks, w_gate, w_up],
        [pltpu.VMEM(hidden_shape, F32)] * 2,
        passes=2,
    )
    partial_sums = [(jax.ShapeDtypeStruct(sums, BF16), own), (jax.ShapeDtypeStruct(sums, BF16), other)]
    picked = [pltpu.VMEM((total, chunk), BF16)]
    out_parts = call(
        functools.partial(forward_kernel, local, rows, half),
        "forward",
        [whole(*hidden_shape), whole(total, LANES), whole(count, total), weight],
        partial_sums,
        [act, gate, back, w_down],
        picked,
    )
    mixed = scatter_sum(grid, out_parts, block)
    d_rows, d_gate, d_up = call(
        functools.partial(second_kernel, shape),
        "hidden_grads",
        [whole(column, width)] * len(d_blocks)
        + [whole(total, count), whole(total, LANES), whole(*hidden_shape), whole(*hidden_shape), weight],
        [routed, full(BF16, *hidden_shape), full(BF16, *hidden_shape)],
        [*d_blocks, select, gate, p, q, w_down],
        [pltpu.VMEM(hidden_shape, F32)],
    )
    back_parts = call(
        functools.partial(back_kernel, local, rows, half),
        "backward",
        [whole(*hidden_shape), whole(*hidden_shape), whole(count, total), weight, weight],
        partial_sums,
        [d_gate, d_up, back, w_gate, w_up],
        picked,
        passes=2,
    )
    grad_tokens = scatter_sum(grid, back_parts, block)

    def grads(name, lefts, right):
        return call(
            functools.partial(grads_kernel, local, rows, len(lefts)),
            name,
            [whole(*hidden_shape)] * len(lefts) + [pl.BlockSpec((1, total, chunk), lambda i, place: (i, 0, 0))],
            [(jax.ShapeDtypeStruct(w_gate.shape, BF16), weight)] * len(lefts),
            [*lefts, right],
            [pltpu.VMEM((local, hidden, rows), BF16)] * len(lefts),
            passes=len(lefts),
        )

    (grad_down,) = grads("grad_down", [act], d_rows)
    grad_gate, grad_up = grads("grad_gate_up", [d_gate, d_up], x_rows)
    return mixed, grad_tokens, grad_gate, grad_up, grad_down


def solution(mesh):
    return jax.shard_map(
        body,
        mesh=mesh,
        in_specs=(
            P("dp", "hst"),
            P("dp", "hst"),
            P("dp", None),
            P("dp", None),
            P("hst", "dp", None),
            P("hst", "dp", None),
            P("hst", "dp", None),
        ),
        out_specs=(
            P("dp", "hst"),
            P("dp", "hst"),
            P("hst", "dp", None),
            P("hst", "dp", None),
            P("hst", "dp", None),
        ),
        check_vma=False,
    )
```

```python
import functools
import math

import jax
import jax.numpy as jnp
from jax import lax
from jax.experimental import pallas as pl
from jax.experimental.pallas import tpu as pltpu
from jax.sharding import PartitionSpec as P

CAP = 4
LANES = 128
MIB = 1 << 20
MFLOP = 10**6
F32 = jnp.float32
BF16 = jnp.bfloat16
AXES = ("dp", "hst")


def dot(a, b):
    return lax.dot_general(a, b, (((1,), (0,)), ((), ())), preferred_element_type=F32)


def dot_t(a, b):
    return lax.dot_general(a, b, (((1,), (1,)), ((), ())), preferred_element_type=F32)


def log2(n):
    assert n & (n - 1) == 0
    return n.bit_length() - 1


class Grid:
    def __init__(self, dp, hst):
        self.dp, self.hst = dp, hst
        self.nc = 2 if hst % 2 == 0 else 1
        self.ny = hst // self.nc
        self.nx = self.ny if dp % self.ny == 0 else 1
        self.nz = dp // self.nx
        assert self.nz & (self.nz - 1) == 0
        self.square = [(a, b) for a in range(self.nx) for b in range(self.ny)]

    def shift(self, value, dz=0, dx=0, dy=0, dc=0):
        pairs = []
        for z in range(self.nz):
            for x in range(self.nx):
                for y in range(self.ny):
                    for c in range(self.nc):
                        to_dp = (z ^ dz) * self.nx + (x + dx) % self.nx
                        to_hst = (y + dy) % self.ny * self.nc + (c + dc) % self.nc
                        here = (z * self.nx + x) * self.hst + y * self.nc + c
                        pairs.append((here, to_dp * self.hst + to_hst))
        return lax.ppermute(value, AXES, pairs)

    def along_z(self, mine):
        return [mine] + [self.shift(mine, dz=k) for k in range(1, self.nz)]

    def doubled_along_z(self, mine):
        column, k = mine, 1
        while k < self.nz:
            column = stack([column, self.shift(column, dz=k)], [], "double")
            k *= 2
        return column

    def over_plane(self, column):
        return {(a, b): self.shift(column, dx=a, dy=b) if a or b else column for a, b in self.square}

    def over_cores(self, plane):
        planes = [plane]
        for c in range(1, self.nc):
            planes.append({at: self.shift(block, dc=c) for at, block in plane.items()})
        return [p[a, b] for p in planes for b in range(self.ny) for a in range(self.nx)]

    def source(self, k):
        host = lax.axis_index("hst")
        y, core = host >> log2(self.nc), host & (self.nc - 1)
        return (((y - k % self.ny) & (self.ny - 1)) << log2(self.nc)) + ((core + k // self.ny) & (self.nc - 1))


def call(kernel, name, outs, args, specs=None, out_specs=None, scratch=(), grid=(), limit=16, cost=0):
    specs = specs or [pl.BlockSpec(memory_space=pltpu.VMEM)] * len(args)
    out_specs = out_specs or [pl.BlockSpec(memory_space=pltpu.VMEM)] * len(outs)
    return pl.pallas_call(
        kernel,
        name=name,
        grid=grid,
        out_shape=outs,
        in_specs=specs,
        out_specs=out_specs,
        scratch_shapes=list(scratch),
        compiler_params=pltpu.CompilerParams(vmem_limit_bytes=limit * MIB),
        cost_estimate=pl.CostEstimate(flops=cost * MFLOP, bytes_accessed=0, transcendentals=0),
    )(*args)


def shaped(dtype, *dims):
    return jax.ShapeDtypeStruct(dims, dtype)


VECTORS = pl.BlockSpec(memory_space=pltpu.VMEM)
ANYWHERE = pl.BlockSpec(memory_space=pl.ANY)


def hold_kernel(source, _, held, sems):
    local, pieces = sems.shape
    part = source.shape[1] // pieces
    copies = []
    for e in range(local):
        for k in range(pieces):
            at = (e, pl.ds(k * part, part))
            copies.append(pltpu.make_async_copy(source.at[at], held.at[at], sems.at[e, k]))
    for copy in copies:
        copy.start()
    for copy in copies:
        copy.wait()


def hold(weight, after, name):
    pieces = 2 if weight.shape[1] % 32 == 0 else 1
    (held,) = call(
        hold_kernel,
        name,
        [pltpu.VMEM(weight.shape, BF16)],
        [hbm(weight), after],
        specs=[ANYWHERE] * 2,
        scratch=[pltpu.SemaphoreType.DMA((weight.shape[0], pieces))],
        cost=12000,
    )
    return held


def hbm(weight):
    return pltpu.with_memory_space_constraint(weight, pltpu.HBM)


def pack_kernel(tokens_ref, ids_ref, gates_ref, out_ref):
    rows, width = tokens_ref.shape
    out_ref[:, :width] = tokens_ref[...]
    gates = gates_ref[...]
    high = gates.astype(BF16).astype(F32)
    middle = (gates - high).astype(BF16).astype(F32)
    low = gates - high - middle
    lane = lax.broadcasted_iota(jnp.int32, (rows, LANES), 1)
    aux = jnp.zeros((rows, LANES), F32)
    for k, part in enumerate([ids_ref[...].astype(F32), high, middle, low]):
        for n in range(2):
            aux = jnp.where(lane == 2 * k + n, part[:, n : n + 1], aux)
    out_ref[:, width:] = aux.astype(BF16)


def stack_kernel(count, later, *refs):
    parts, out_ref = refs[:count], refs[-1 - later]
    rows = parts[0].shape[0]
    for k, part in enumerate(parts):
        out_ref[k * rows : (k + 1) * rows] = part[...]
    if later:
        refs[-1][...] = refs[count][...]


def stack(parts, after, name, later=()):
    rows, width = parts[0].shape
    outs = call(
        functools.partial(stack_kernel, len(parts), len(later)),
        name,
        [shaped(BF16, rows * len(parts), width)] + [shaped(BF16, *array.shape) for array in later],
        [*parts, *later, *after],
        specs=[VECTORS] * (len(parts) + len(later)) + [ANYWHERE] * len(after),
        limit=16,
    )
    return outs if later else outs[0]


def add_kernel(count, skip, *refs):
    parts, outs = refs[:count], refs[count + skip :]
    total = parts[0][...].astype(F32)
    for part in parts[1:]:
        total = total + part[...].astype(F32)
    total = total.astype(BF16).reshape((len(outs),) + outs[0].shape)
    for k, out in enumerate(outs):
        out[...] = total[k]


def add(parts, pieces, after, name):
    *lead, rows, width = parts[0].shape
    each = math.prod(lead) * rows // pieces
    return call(
        functools.partial(add_kernel, len(parts), len(after)),
        name,
        [shaped(BF16, each, width)] * pieces,
        [*parts, *after],
        specs=[VECTORS] * len(parts) + [ANYWHERE] * len(after),
        limit=16,
    )


def back_over_cores(grid, parts, after, name):
    got = [grid.shift(parts[c], dc=-c) for c in range(1, grid.nc)]
    return add([parts[0], *got], len(grid.square), after, name)


def back_over_plane(grid, kept, after, name):
    got = [grid.shift(part, dx=-a, dy=-b) for part, (a, b) in zip(kept[1:], grid.square[1:])]
    return add([kept[0], *got], grid.nz, after, name)


def back_along_z(grid, total, after, name):
    got = [grid.shift(total[k], dz=k) for k in range(1, grid.nz)]
    return add([total[0], *got], 1, after, name)[0]


def tables(aux, first, rows, local, block):
    tokens = aux.shape[0]
    across = jnp.transpose(aux.astype(F32))
    ids = [across[k : k + 1] for k in range(2)]
    gates = [across[2 + k : 3 + k] + across[4 + k : 5 + k] + across[6 + k : 7 + k] for k in range(2)]
    total = local * rows
    r = lax.broadcasted_iota(jnp.int32, (total, tokens), 0)
    j = lax.broadcasted_iota(jnp.int32, (total, tokens), 1)
    expert = ((r >> log2(rows)) + first).astype(F32)
    own_block = ((r & (rows - 1)) >> log2(CAP)) == (j >> log2(block))
    slot = (r & (CAP - 1)).astype(F32)
    hits = [(ids[k] == expert).astype(F32) for k in range(2)]
    hit = hits[0] + hits[1]
    up = lax.broadcasted_iota(jnp.int32, (tokens, tokens), 0)
    to = lax.broadcasted_iota(jnp.int32, (tokens, tokens), 1)
    earlier = ((up >> log2(block)) == (to >> log2(block))) & (up < to)
    position = dot(hit.astype(BF16), jnp.where(earlier, 1.0, 0.0).astype(BF16))
    select = jnp.where(own_block & (position == slot), hit, 0.0)
    gate = jnp.sum(select * (hits[0] * gates[0] + hits[1] * gates[1]), axis=1, keepdims=True)
    return select, gate


def streamed(weight, held, sems, starts):
    depth, width = held.shape[0], held.shape[-1]
    copies = [
        pltpu.make_async_copy(weight.at[:, :, pl.ds(start, width)], held.at[k % depth], sems.at[k % depth])
        for k, start in enumerate(starts)
    ]
    for copy in copies[:depth]:
        copy.start()

    def each():
        for k, copy in enumerate(copies):
            copy.wait()
            yield k, held.at[k % depth]
            if k + depth < len(copies):
                copies[k + depth].start()

    return each()


class Sizes:
    def __init__(self, grid, tokens, w_gate):
        self.grid = grid
        self.local, self.hidden, self.features = w_gate.shape
        self.block, self.width = tokens.shape
        self.rows = grid.dp * CAP
        self.total = self.local * self.rows
        self.count = grid.dp * self.block
        self.column = grid.nz * self.block
        self.blocks = grid.nc * grid.ny * grid.nx
        self.slices = grid.nc * grid.ny
        self.chunk = 896 if self.width % 896 == 0 else self.width
        self.per = self.width // self.chunk

    def relative_starts(self):
        return [
            pl.multiple_of(self.grid.source(k // self.per) * self.width + k % self.per * self.chunk, self.chunk)
            for k in range(self.slices * self.per)
        ]

    def at(self, e):
        return slice(e * self.rows, (e + 1) * self.rows)


def routed(s, blocks, select):
    for k in range(s.slices):
        group = blocks[k * s.grid.nx : (k + 1) * s.grid.nx]
        yield k, dot(select, jnp.concatenate([ref[:, : s.width] for ref in group], axis=0))


def gate_up_kernel(s, *refs):
    blocks = refs[: s.blocks]
    wg_ref, wu_ref, _, x_ref, select_ref, back_ref, gate_ref, act_ref, p_ref, q_ref, held, sems = refs[s.blocks :]
    chunks = streamed(wu_ref, held, sems, range(0, s.features, s.chunk))
    aux = jnp.concatenate([ref[:, s.width :] for ref in blocks[: s.grid.nx]], axis=0)
    select, gate = tables(aux, lax.axis_index("hst") * s.local, s.rows, s.local, s.block)
    gate_ref[...] = jnp.broadcast_to(gate, gate_ref.shape)
    select_ref[...] = select.astype(BF16)
    back_ref[...] = jnp.transpose(select).astype(BF16)
    for k, picked in routed(s, blocks, select.astype(BF16)):
        x_ref[s.grid.source(k)] = picked.astype(BF16)
    g, u = [0.0] * s.local, [0.0] * s.local
    for k, weight in chunks:
        at = k % s.per * s.chunk
        columns = slice(k * s.chunk, (k + 1) * s.chunk)
        for e in range(s.local):
            x = x_ref[k // s.per, s.at(e), at : at + s.chunk]
            g[e] += dot_t(x, wg_ref[e, :, columns])
            u[e] += dot_t(x, weight[e])
    for e in range(s.local):
        sigma = jax.nn.sigmoid(g[e])
        act_ref[e] = (g[e] * sigma * u[e]).astype(BF16)
        p_ref[e] = u[e] * sigma * (1.0 + g[e] * (1.0 - sigma))
        q_ref[e] = g[e] * sigma


def hidden_grads_kernel(s, *refs):
    blocks = refs[: s.blocks]
    select_ref, gate_ref, p_ref, q_ref, w_ref, d_ref, dg_ref, du_ref, held, sems = refs[s.blocks :]
    chunks = streamed(w_ref, held, sems, range(0, s.features, s.chunk))
    for k, picked in routed(s, blocks, select_ref[...]):
        d_ref[s.grid.source(k)] = (picked * gate_ref[:, :1]).astype(BF16)
    da = [0.0] * s.local
    for k, weight in chunks:
        at = k % s.per * s.chunk
        for e in range(s.local):
            da[e] += dot_t(d_ref[k // s.per, s.at(e), at : at + s.chunk], weight[e])
    for e in range(s.local):
        dg_ref[e] = (da[e] * p_ref[e]).astype(BF16)
        du_ref[e] = (da[e] * q_ref[e]).astype(BF16)


def to_tokens(s, k, at, found, back_ref, outs):
    each = s.slices // s.grid.nc
    sums = dot(back_ref[...], jnp.concatenate(found, axis=0)).astype(BF16)
    width = sums.shape[-1]
    outs[k // each][:, k % each, :, at : at + width] = sums.reshape(s.grid.nx, s.column, width)


def forward_kernel(s, act_ref, gate_ref, back_ref, w_ref, *refs):
    outs, (held, sems) = refs[:-2], refs[-2:]
    for k, weight in streamed(w_ref, held, sems, s.relative_starts()):
        found = [(dot(act_ref[e], weight[e]) * gate_ref[s.at(e), :1]).astype(BF16) for e in range(s.local)]
        to_tokens(s, k // s.per, k % s.per * s.chunk, found, back_ref, outs)


def backward_kernel(s, dg_ref, du_ref, back_ref, wg_ref, wu_ref, _, *refs):
    outs, (held, sems) = refs[:-2], refs[-2:]
    starts = s.relative_starts()
    for k, weight in streamed(wu_ref, held, sems, starts):
        columns = pl.ds(starts[k], s.chunk)
        found = [
            (dot(dg_ref[e], wg_ref[e, :, columns]) + dot(du_ref[e], weight[e])).astype(BF16)
            for e in range(s.local)
        ]
        to_tokens(s, k // s.per, k % s.per * s.chunk, found, back_ref, outs)


def grads_kernel(s, count, *refs):
    lefts, rows_ref = refs[:count], refs[count]
    outs, marker, turned = refs[count + 2 : 2 * count + 2], refs[2 * count + 2], refs[2 * count + 3 :]

    @pl.when(pl.program_id(0) == 0)
    def _():
        marker[...] = jnp.zeros_like(marker)
        for left, turn in zip(lefts, turned):
            for e in range(s.local):
                turn[e] = jnp.transpose(left[e].astype(F32)).astype(BF16)

    right = rows_ref[0]
    for turn, out in zip(turned, outs):
        for e in range(s.local):
            out[e] = dot(turn[e], right[s.at(e)]).astype(BF16)


def grads(s, name, lefts, right, after):
    chunk, per = s.chunk, s.per
    whole = pl.BlockSpec((s.local, s.rows, s.hidden), lambda i: (0, 0, 0))
    return call(
        functools.partial(grads_kernel, s, len(lefts)),
        name,
        [shaped(BF16, s.local, s.hidden, s.features)] * len(lefts) + [shaped(F32, 8, LANES)],
        [*lefts, right, after],
        specs=[whole] * len(lefts)
        + [pl.BlockSpec((1, s.total, chunk), lambda i: (i // per, 0, i % per)), ANYWHERE],
        out_specs=[pl.BlockSpec((s.local, s.hidden, chunk), lambda i: (0, 0, i))] * len(lefts)
        + [pl.BlockSpec((8, LANES), lambda i: (0, 0))],
        scratch=[pltpu.VMEM((s.local, s.hidden, s.rows), BF16)] * len(lefts),
        grid=(s.features // chunk,),
        limit=8 + 6 * len(lefts),
        cost=46000,
    )


def body(tokens, cotangent, expert_ids, gate_values, w_gate, w_up, w_down):
    grid = Grid(lax.axis_size("dp"), lax.axis_size("hst"))
    s = Sizes(grid, tokens, w_gate)

    (message,) = call(
        pack_kernel, "pack", [shaped(BF16, s.block, s.width + LANES)], [tokens, expert_ids, gate_values]
    )
    x_parts = grid.along_z(message)
    held_gate = hold(w_gate, message, "hold_gate")
    x_column, cotangent = stack(x_parts, [held_gate], "stack_tokens", [cotangent])
    x_plane = grid.over_plane(x_column)
    d_column = grid.doubled_along_z(cotangent)
    last = grid.square[-1]
    x_plane[last] = stack([x_plane[last]], [d_column], "relay")
    x_blocks = grid.over_cores(x_plane)
    d_column = stack([d_column], x_blocks, "stack_cotangents")
    streams = [pltpu.VMEM((3, s.local, s.hidden, s.chunk), BF16), pltpu.SemaphoreType.DMA((3,))]

    hidden_shape = (s.local, s.rows, s.hidden)
    rows_shape = shaped(BF16, s.slices, s.total, s.width)
    x_rows, select, back, gate, act, p, q = call(
        functools.partial(gate_up_kernel, s),
        "gate_up",
        [
            rows_shape,
            shaped(BF16, s.total, s.count),
            shaped(BF16, s.count, s.total),
            shaped(F32, s.total, LANES),
            shaped(BF16, *hidden_shape),
            shaped(F32, *hidden_shape),
            shaped(F32, *hidden_shape),
        ],
        [*x_blocks, held_gate, hbm(w_up), d_column],
        specs=[VECTORS] * (s.blocks + 1) + [ANYWHERE] * 2,
        scratch=streams,
        limit=16,
        cost=46000,
    )
    d_blocks = grid.over_cores(grid.over_plane(d_column))
    sums = shaped(BF16, grid.nx, grid.ny, s.column, s.width)
    out_parts = call(
        functools.partial(forward_kernel, s),
        "forward",
        [sums] * grid.nc,
        [act, gate, back, hbm(w_down)],
        specs=[VECTORS] * 3 + [ANYWHERE],
        scratch=streams,
        limit=16,
        cost=46000,
    )
    d_rows, d_gate, d_up = call(
        functools.partial(hidden_grads_kernel, s),
        "hidden_grads",
        [rows_shape, shaped(BF16, *hidden_shape), shaped(BF16, *hidden_shape)],
        [*d_blocks, select, gate, p, q, hbm(w_down)],
        specs=[VECTORS] * (s.blocks + 4) + [ANYWHERE],
        scratch=streams,
        limit=16,
        cost=46000,
    )
    mixed_kept = back_over_cores(grid, out_parts, [d_gate], "mixed_cores")
    back_parts = call(
        functools.partial(backward_kernel, s),
        "backward",
        [sums] * grid.nc,
        [d_gate, d_up, back, held_gate, hbm(w_up), mixed_kept[0]],
        specs=[VECTORS] * 4 + [ANYWHERE] * 2,
        scratch=streams,
        limit=16,
        cost=46000,
    )
    mixed_total = back_over_plane(grid, mixed_kept, back_parts[:1], "mixed_plane")
    grad_down, down_done = grads(s, "grad_down", [act], d_rows, mixed_total[0])
    mixed = back_along_z(grid, mixed_total, [down_done], "mixed_z")
    token_kept = back_over_cores(grid, back_parts, [down_done], "tokens_cores")
    grad_gate, grad_up, gate_up_done = grads(s, "grad_gate_up", [d_gate, d_up], x_rows, token_kept[0])
    token_total = back_over_plane(grid, token_kept, [gate_up_done], "tokens_plane")
    grad_tokens = back_along_z(grid, token_total, [], "tokens_z")
    return mixed, grad_tokens, grad_gate, grad_up, grad_down


def solution(mesh):
    return jax.shard_map(
        body,
        mesh=mesh,
        in_specs=(
            P("dp", "hst"),
            P("dp", "hst"),
            P("dp", None),
            P("dp", None),
            P("hst", "dp", None),
            P("hst", "dp", None),
            P("hst", "dp", None),
        ),
        out_specs=(
            P("dp", "hst"),
            P("dp", "hst"),
            P("hst", "dp", None),
            P("hst", "dp", None),
            P("hst", "dp", None),
        ),
        check_vma=False,
    )
```

```python
import functools
import math

import jax
import jax.numpy as jnp
from jax import lax
from jax.experimental import pallas as pl
from jax.experimental.pallas import tpu as pltpu
from jax.sharding import PartitionSpec as P

CAP = 4
LANES = 128
MIB = 1 << 20
MFLOP = 10**6
F32 = jnp.float32
BF16 = jnp.bfloat16
AXES = ("dp", "hst")


def dot(a, b):
    return lax.dot_general(a, b, (((1,), (0,)), ((), ())), preferred_element_type=F32)


def dot_t(a, b):
    return lax.dot_general(a, b, (((1,), (1,)), ((), ())), preferred_element_type=F32)


def log2(n):
    assert n & (n - 1) == 0
    return n.bit_length() - 1


class Grid:
    def __init__(self, dp, hst):
        self.dp, self.hst = dp, hst
        self.nc = 2 if hst % 2 == 0 else 1
        self.ny = hst // self.nc
        self.nx = self.ny if dp % self.ny == 0 else 1
        self.nz = dp // self.nx
        assert self.nz & (self.nz - 1) == 0
        self.square = [(a, b) for a in range(self.nx) for b in range(self.ny)]

    def shift(self, value, dz=0, dx=0, dy=0, dc=0):
        pairs = []
        for z in range(self.nz):
            for x in range(self.nx):
                for y in range(self.ny):
                    for c in range(self.nc):
                        to_dp = (z ^ dz) * self.nx + (x + dx) % self.nx
                        to_hst = (y + dy) % self.ny * self.nc + (c + dc) % self.nc
                        here = (z * self.nx + x) * self.hst + y * self.nc + c
                        pairs.append((here, to_dp * self.hst + to_hst))
        return lax.ppermute(value, AXES, pairs)

    def along_z(self, mine):
        return [mine] + [self.shift(mine, dz=k) for k in range(1, self.nz)]

    def doubled_along_z(self, mine):
        columns, k = [mine], 1
        while k < self.nz:
            columns.append(stack([columns[-1], self.shift(columns[-1], dz=k)], [], "double"))
            k *= 2
        return columns

    def over_plane(self, column):
        return {(a, b): self.shift(column, dx=a, dy=b) if a or b else column for a, b in self.square}

    def over_cores(self, plane):
        planes = [plane]
        for c in range(1, self.nc):
            planes.append({at: self.shift(block, dc=c) for at, block in plane.items()})
        return [p[a, b] for p in planes for b in range(self.ny) for a in range(self.nx)]

    def source(self, k):
        host = lax.axis_index("hst")
        y, core = host >> log2(self.nc), host & (self.nc - 1)
        return (((y - k % self.ny) & (self.ny - 1)) << log2(self.nc)) + ((core + k // self.ny) & (self.nc - 1))


def call(kernel, name, outs, args, specs=None, out_specs=None, scratch=(), grid=(), limit=16, cost=0):
    specs = specs or [pl.BlockSpec(memory_space=pltpu.VMEM)] * len(args)
    out_specs = out_specs or [pl.BlockSpec(memory_space=pltpu.VMEM)] * len(outs)
    return pl.pallas_call(
        kernel,
        name=name,
        grid=grid,
        out_shape=outs,
        in_specs=specs,
        out_specs=out_specs,
        scratch_shapes=list(scratch),
        compiler_params=pltpu.CompilerParams(vmem_limit_bytes=limit * MIB),
        cost_estimate=pl.CostEstimate(flops=cost * MFLOP, bytes_accessed=0, transcendentals=0),
    )(*args)


def shaped(dtype, *dims):
    return jax.ShapeDtypeStruct(dims, dtype)


VECTORS = pl.BlockSpec(memory_space=pltpu.VMEM)
ANYWHERE = pl.BlockSpec(memory_space=pl.ANY)


def hbm(weight):
    return pltpu.with_memory_space_constraint(weight, pltpu.HBM)


def pack_kernel(tokens_ref, ids_ref, gates_ref, out_ref):
    rows, width = tokens_ref.shape
    out_ref[:, :width] = tokens_ref[...]
    gates = gates_ref[...]
    high = gates.astype(BF16).astype(F32)
    middle = (gates - high).astype(BF16).astype(F32)
    low = gates - high - middle
    fields = jnp.concatenate([ids_ref[...].astype(F32), high, middle, low], axis=0)
    fields = jnp.pad(fields, ((0, LANES - fields.shape[0]), (0, LANES - rows)))
    out_ref[:, width:] = jnp.transpose(fields)[:rows].astype(BF16)


def stack_kernel(count, later, *refs):
    parts, out_ref = refs[:count], refs[-1 - later]
    rows = parts[0].shape[0]
    for k, part in enumerate(parts):
        out_ref[k * rows : (k + 1) * rows] = part[...]
    if later:
        refs[-1][...] = refs[count][...]


def stack(parts, after, name, later=()):
    rows, width = parts[0].shape
    outs = call(
        functools.partial(stack_kernel, len(parts), len(later)),
        name,
        [shaped(BF16, rows * len(parts), width)] + [shaped(BF16, *array.shape) for array in later],
        [*parts, *later, *after],
        specs=[VECTORS] * (len(parts) + len(later)) + [ANYWHERE] * len(after),
        limit=16,
    )
    return outs if later else outs[0]


def add_kernel(count, skip, *refs):
    parts, outs = refs[:count], refs[count + skip :]
    total = parts[0][...].astype(F32)
    for part in parts[1:]:
        total = total + part[...].astype(F32)
    total = total.astype(BF16).reshape((len(outs),) + outs[0].shape)
    for k, out in enumerate(outs):
        out[...] = total[k]


def add(parts, pieces, after, name):
    *lead, rows, width = parts[0].shape
    each = math.prod(lead) * rows // pieces
    return call(
        functools.partial(add_kernel, len(parts), len(after)),
        name,
        [shaped(BF16, each, width)] * pieces,
        [*parts, *after],
        specs=[VECTORS] * len(parts) + [ANYWHERE] * len(after),
        limit=16,
    )


def back_over_cores(grid, parts, after, name):
    got = [grid.shift(parts[c], dc=-c) for c in range(1, grid.nc)]
    return add([parts[0], *got], len(grid.square), after, name)


def back_over_plane(grid, kept, after, name):
    got = [grid.shift(part, dx=-a, dy=-b) for part, (a, b) in zip(kept[1:], grid.square[1:])]
    return add([kept[0], *got], grid.nz, after, name)


def back_along_z(grid, total, after, name):
    got = [grid.shift(total[k], dz=k) for k in range(1, grid.nz)]
    return add([total[0], *got], 1, after, name)[0]


def tables(aux, first, rows, local, block):
    tokens = aux.shape[0]
    across = jnp.transpose(aux.astype(F32))
    ids = [across[k : k + 1] for k in range(2)]
    gates = [across[2 + k : 3 + k] + across[4 + k : 5 + k] + across[6 + k : 7 + k] for k in range(2)]
    total = local * rows
    r = lax.broadcasted_iota(jnp.int32, (total, tokens), 0)
    j = lax.broadcasted_iota(jnp.int32, (total, tokens), 1)
    expert = ((r >> log2(rows)) + first).astype(F32)
    own_block = ((r & (rows - 1)) >> log2(CAP)) == (j >> log2(block))
    slot = (r & (CAP - 1)).astype(F32)
    hits = [(ids[k] == expert).astype(F32) for k in range(2)]
    hit = hits[0] + hits[1]
    up = lax.broadcasted_iota(jnp.int32, (tokens, tokens), 0)
    to = lax.broadcasted_iota(jnp.int32, (tokens, tokens), 1)
    earlier = ((up >> log2(block)) == (to >> log2(block))) & (up < to)
    position = dot(hit.astype(BF16), jnp.where(earlier, 1.0, 0.0).astype(BF16))
    select = jnp.where(own_block & (position == slot), hit, 0.0)
    gate = jnp.sum(select * (hits[0] * gates[0] + hits[1] * gates[1]), axis=1, keepdims=True)
    return select, gate


def streamed(weight, held, sems, columns):
    depth = held.shape[0]
    copies = [
        pltpu.make_async_copy(
            weight.at[:, :, pl.ds(start, size)], held.at[k % depth, :, :, pl.ds(0, size)], sems.at[k % depth]
        )
        for k, (start, size) in enumerate(columns)
    ]
    for copy in copies[:depth]:
        copy.start()

    def each():
        for k, copy in enumerate(copies):
            copy.wait()
            size = columns[k][1]
            yield held[k % depth, :, :, :size].reshape(-1, size)
            if k + depth < len(copies):
                copies[k + depth].start()

    return each()


def kept(weight, held, sems, columns):
    copies = []
    for k, (start, size) in enumerate(columns):
        at = (slice(None), slice(None), pl.ds(start, size))
        copies.append(pltpu.make_async_copy(weight.at[at], held.at[at], sems.at[k]))

    ahead = 4
    for copy in copies[:ahead]:
        copy.start()

    def each():
        for k, copy in enumerate(copies):
            copy.wait()
            start, size = columns[k]
            yield held[:, :, start : start + size].reshape(-1, size)
            if k + ahead < len(copies):
                copies[k + ahead].start()

    return each()


class Sizes:
    def __init__(self, grid, tokens, w_gate):
        self.grid = grid
        self.local, self.hidden, self.features = w_gate.shape
        self.block, self.width = tokens.shape
        self.rows = grid.dp * CAP
        self.total = self.local * self.rows
        self.count = grid.dp * self.block
        self.column = grid.nz * self.block
        self.blocks = grid.nc * grid.ny * grid.nx
        self.slices = grid.nc * grid.ny
        self.merged = self.local * self.hidden
        whole = self.width % 256 == 0 and self.width > 1024
        self.pieces = [(0, 1024), (1024, self.width - 1024)] if whole else [(0, self.width)]

    def walk(self):
        return [(k, at, size) for k in range(self.slices) for at, size in self.pieces]

    def own_expert(self):
        expert = lax.broadcasted_iota(jnp.int32, (self.total, self.merged), 0) >> log2(self.rows)
        unit = lax.broadcasted_iota(jnp.int32, (self.total, self.merged), 1)
        return (unit >= expert * self.hidden) & (unit < (expert + 1) * self.hidden)


def routed(s, blocks, select):
    for k in range(s.slices):
        group = blocks[k * s.grid.nx : (k + 1) * s.grid.nx]
        yield k, dot(select, jnp.concatenate([ref[:, : s.width] for ref in group], axis=0))


def gate_up_kernel(s, *refs):
    blocks = refs[: s.blocks]
    (wg_ref, wu_ref, _, x_ref, select_ref, back_ref, gate_ref, act_ref, p_ref, q_ref, held_ref, room, sems, held_sems) = refs[
        s.blocks :
    ]
    walk = s.walk()
    columns = [(k * s.width + at, size) for k, at, size in walk]
    gates, ups = kept(wg_ref, held_ref, held_sems, columns), streamed(wu_ref, room, sems, columns)
    aux = jnp.concatenate([ref[:, s.width :] for ref in blocks[: s.grid.nx]], axis=0)
    select, gate = tables(aux, lax.axis_index("hst") * s.local, s.rows, s.local, s.block)
    gate_ref[...] = jnp.broadcast_to(gate, gate_ref.shape)
    select_ref[...] = select.astype(BF16)
    back_ref[...] = jnp.transpose(select).astype(BF16)
    for k, picked in routed(s, blocks, select.astype(BF16)):
        x_ref[s.grid.source(k)] = picked.astype(BF16)
    g = u = 0.0
    for (k, at, size), wg, wu in zip(walk, gates, ups):
        x = x_ref[k, :, at : at + size]
        g += dot_t(x, wg)
        u += dot_t(x, wu)
    sigma = jax.nn.sigmoid(g)
    mine = s.own_expert()
    act_ref[...] = jnp.where(mine, g * sigma * u, 0.0).astype(BF16)
    p_ref[...] = jnp.where(mine, u * sigma * (1.0 + g * (1.0 - sigma)), 0.0)
    q_ref[...] = jnp.where(mine, g * sigma, 0.0)


def hidden_grads_kernel(s, *refs):
    blocks = refs[: s.blocks]
    select_ref, gate_ref, p_ref, q_ref, w_ref, d_ref, dg_ref, du_ref, room, sems = refs[s.blocks :]
    walk = s.walk()
    weights = streamed(w_ref, room, sems, [(k * s.width + at, size) for k, at, size in walk])
    for k, picked in routed(s, blocks, select_ref[...]):
        d_ref[s.grid.source(k)] = (picked * gate_ref[:, :1]).astype(BF16)
    da = 0.0
    for (k, at, size), weight in zip(walk, weights):
        da += dot_t(d_ref[k, :, at : at + size], weight)
    dg_ref[...] = (da * p_ref[...]).astype(BF16)
    du_ref[...] = (da * q_ref[...]).astype(BF16)


def to_tokens(s, k, at, found, back_ref, outs):
    each = s.slices // s.grid.nc
    sums = dot(back_ref[...], found.astype(BF16)).astype(BF16)
    size = sums.shape[-1]
    outs[k // each][:, k % each, :, at : at + size] = sums.reshape(s.grid.nx, s.column, size)


def relative(s, walk):
    return [(pl.multiple_of(s.grid.source(k) * s.width + at, LANES), size) for k, at, size in walk]


def forward_kernel(s, act_ref, gate_ref, back_ref, w_ref, *refs):
    outs, (room, sems) = refs[:-2], refs[-2:]
    walk = s.walk()
    for (k, at, _), weight in zip(walk, streamed(w_ref, room, sems, relative(s, walk))):
        to_tokens(s, k, at, dot(act_ref[...], weight) * gate_ref[:, :1], back_ref, outs)


def backward_kernel(s, dg_ref, du_ref, back_ref, held_ref, wu_ref, _, *refs):
    outs, (room, sems) = refs[:-2], refs[-2:]
    walk = s.walk()
    columns = relative(s, walk)
    for (k, at, size), (start, _), up in zip(walk, columns, streamed(wu_ref, room, sems, columns)):
        gate = held_ref[:, :, pl.ds(start, size)].reshape(s.merged, size)
        to_tokens(s, k, at, dot(dg_ref[...], gate) + dot(du_ref[...], up), back_ref, outs)


def grads_kernel(s, count, *refs):
    lefts, rows_ref = refs[:count], refs[count]
    outs, marker, turned = refs[count + 2 : 2 * count + 2], refs[2 * count + 2], refs[2 * count + 3 :]

    @pl.when(pl.program_id(0) == 0)
    def _():
        marker[...] = jnp.zeros_like(marker)
        for left, turn in zip(lefts, turned):
            turn[...] = jnp.transpose(left[...].astype(F32)).astype(BF16)

    for turn, out in zip(turned, outs):
        out[...] = dot(turn[...], rows_ref[0]).astype(BF16).reshape(out.shape)


def grads(s, name, lefts, right, after):
    return call(
        functools.partial(grads_kernel, s, len(lefts)),
        name,
        [shaped(BF16, s.local, s.hidden, s.features)] * len(lefts) + [shaped(F32, 8, LANES)],
        [*lefts, right, after],
        specs=[pl.BlockSpec((s.total, s.merged), lambda i: (0, 0))] * len(lefts)
        + [pl.BlockSpec((1, s.total, s.width), lambda i: (i, 0, 0)), ANYWHERE],
        out_specs=[pl.BlockSpec((s.local, s.hidden, s.width), lambda i: (0, 0, i))] * len(lefts)
        + [pl.BlockSpec((8, LANES), lambda i: (0, 0))],
        scratch=[pltpu.VMEM((s.merged, s.total), BF16)] * len(lefts),
        grid=(s.slices,),
        limit=8 + 12 * len(lefts),
        cost=46000,
    )


def body(tokens, cotangent, expert_ids, gate_values, w_gate, w_up, w_down):
    grid = Grid(lax.axis_size("dp"), lax.axis_size("hst"))
    s = Sizes(grid, tokens, w_gate)

    (message,) = call(
        pack_kernel, "pack", [shaped(BF16, s.block, s.width + LANES)], [tokens, expert_ids.T, gate_values.T]
    )
    x_parts = grid.along_z(message)
    x_column, cotangent = stack(x_parts, [], "stack_tokens", [cotangent])
    x_plane = grid.over_plane(x_column)
    d_halves = grid.doubled_along_z(cotangent)
    d_column = d_halves[-1]
    last = grid.square[-1]
    x_plane[last] = stack([x_plane[last]], [d_halves[-2]], "relay")
    x_blocks = grid.over_cores(x_plane)
    d_column = stack([d_column], x_blocks, "stack_cotangents")
    room = max(size for _, size in s.pieces)
    streams = [pltpu.VMEM((3, s.local, s.hidden, room), BF16), pltpu.SemaphoreType.DMA((3,))]

    hidden_shape = (s.total, s.merged)
    rows_shape = shaped(BF16, s.slices, s.total, s.width)
    x_rows, select, back, gate, act, p, q, held_gate = call(
        functools.partial(gate_up_kernel, s),
        "gate_up",
        [
            rows_shape,
            shaped(BF16, s.total, s.count),
            shaped(BF16, s.count, s.total),
            shaped(F32, s.total, LANES),
            shaped(BF16, *hidden_shape),
            shaped(F32, *hidden_shape),
            shaped(F32, *hidden_shape),
            pltpu.VMEM(w_gate.shape, BF16),
        ],
        [*x_blocks, hbm(w_gate), hbm(w_up), d_column],
        specs=[VECTORS] * s.blocks + [ANYWHERE] * 3,
        scratch=[*streams, pltpu.SemaphoreType.DMA((len(s.walk()),))],
        limit=16,
        cost=46000,
    )
    d_blocks = grid.over_cores(grid.over_plane(d_column))
    sums = shaped(BF16, grid.nx, grid.ny, s.column, s.width)
    out_parts = call(
        functools.partial(forward_kernel, s),
        "forward",
        [sums] * grid.nc,
        [act, gate, back, hbm(w_down)],
        specs=[VECTORS] * 3 + [ANYWHERE],
        scratch=streams,
        limit=16,
        cost=46000,
    )
    d_rows, d_gate, d_up = call(
        functools.partial(hidden_grads_kernel, s),
        "hidden_grads",
        [rows_shape, shaped(BF16, *hidden_shape), shaped(BF16, *hidden_shape)],
        [*d_blocks, select, gate, p, q, hbm(w_down)],
        specs=[VECTORS] * (s.blocks + 4) + [ANYWHERE],
        scratch=streams,
        limit=16,
        cost=46000,
    )
    mixed_kept = back_over_cores(grid, out_parts, [d_gate], "mixed_cores")
    back_parts = call(
        functools.partial(backward_kernel, s),
        "backward",
        [sums] * grid.nc,
        [d_gate, d_up, back, held_gate, hbm(w_up), mixed_kept[0]],
        specs=[VECTORS] * 4 + [ANYWHERE] * 2,
        scratch=streams,
        limit=16,
        cost=46000,
    )
    grad_down, down_done = grads(s, "grad_down", [act], d_rows, back_parts[0])
    token_kept = back_over_cores(grid, back_parts, [down_done], "tokens_cores")
    mixed_total = back_over_plane(grid, mixed_kept, token_kept[:1], "mixed_plane")
    grad_gate, grad_up, gate_up_done = grads(s, "grad_gate_up", [d_gate, d_up], x_rows, mixed_total[0])
    mixed = back_along_z(grid, mixed_total, [gate_up_done], "mixed_z")
    token_total = back_over_plane(grid, token_kept, [gate_up_done], "tokens_plane")
    grad_tokens = back_along_z(grid, token_total, [], "tokens_z")
    return mixed, grad_tokens, grad_gate, grad_up, grad_down


def solution(mesh):
    return jax.shard_map(
        body,
        mesh=mesh,
        in_specs=(
            P("dp", "hst"),
            P("dp", "hst"),
            P("dp", None),
            P("dp", None),
            P("hst", "dp", None),
            P("hst", "dp", None),
            P("hst", "dp", None),
        ),
        out_specs=(
            P("dp", "hst"),
            P("dp", "hst"),
            P("hst", "dp", None),
            P("hst", "dp", None),
            P("hst", "dp", None),
        ),
        check_vma=False,
    )
```

```python
import functools
import math

import jax
import jax.numpy as jnp
from jax import lax
from jax.experimental import pallas as pl
from jax.experimental.pallas import tpu as pltpu
from jax.sharding import PartitionSpec as P

CAP = 4
LANES = 128
AHEAD = 4
MIB = 1 << 20
MFLOP = 10**6
F32 = jnp.float32
BF16 = jnp.bfloat16
AXES = ("dp", "hst")


def dot(a, b):
    return lax.dot_general(a, b, (((1,), (0,)), ((), ())), preferred_element_type=F32)


def dot_t(a, b):
    return lax.dot_general(a, b, (((1,), (1,)), ((), ())), preferred_element_type=F32)


def log2(n):
    assert n & (n - 1) == 0
    return n.bit_length() - 1


class Grid:
    def __init__(self, dp, hst):
        self.dp, self.hst = dp, hst
        self.nc = 2 if hst % 2 == 0 else 1
        self.ny = hst // self.nc
        self.nx = self.ny if dp % self.ny == 0 else 1
        self.nz = dp // self.nx
        assert self.nz & (self.nz - 1) == 0
        self.square = [(a, b) for a in range(self.nx) for b in range(self.ny)]

    def shift(self, value, dz=0, dx=0, dy=0, dc=0):
        pairs = []
        for z in range(self.nz):
            for x in range(self.nx):
                for y in range(self.ny):
                    for c in range(self.nc):
                        to_dp = (z ^ dz) * self.nx + (x + dx) % self.nx
                        to_hst = (y + dy) % self.ny * self.nc + (c + dc) % self.nc
                        here = (z * self.nx + x) * self.hst + y * self.nc + c
                        pairs.append((here, to_dp * self.hst + to_hst))
        return lax.ppermute(value, AXES, pairs)

    def along_z(self, mine):
        return [mine] + [self.shift(mine, dz=k) for k in range(1, self.nz)]

    def doubled_along_z(self, mine):
        columns, k = [mine], 1
        while k < self.nz:
            columns.append(stack([columns[-1], self.shift(columns[-1], dz=k)], [], "double"))
            k *= 2
        return columns

    def over_plane(self, column):
        return {(a, b): self.shift(column, dx=a, dy=b) if a or b else column for a, b in self.square}

    def over_cores(self, plane):
        planes = [plane]
        for c in range(1, self.nc):
            planes.append({at: self.shift(block, dc=c) for at, block in plane.items()})
        return [p[a, b] for p in planes for b in range(self.ny) for a in range(self.nx)]

    def source(self, k):
        host = lax.axis_index("hst")
        y, core = host >> log2(self.nc), host & (self.nc - 1)
        return (((y - k % self.ny) & (self.ny - 1)) << log2(self.nc)) + ((core + k // self.ny) & (self.nc - 1))


def call(kernel, name, outs, args, specs=None, out_specs=None, scratch=(), grid=(), limit=16, cost=0):
    specs = specs or [pl.BlockSpec(memory_space=pltpu.VMEM)] * len(args)
    out_specs = out_specs or [pl.BlockSpec(memory_space=pltpu.VMEM)] * len(outs)
    return pl.pallas_call(
        kernel,
        name=name,
        grid=grid,
        out_shape=outs,
        in_specs=specs,
        out_specs=out_specs,
        scratch_shapes=list(scratch),
        compiler_params=pltpu.CompilerParams(vmem_limit_bytes=limit * MIB),
        cost_estimate=pl.CostEstimate(flops=cost * MFLOP, bytes_accessed=0, transcendentals=0),
    )(*args)


def shaped(dtype, *dims):
    return jax.ShapeDtypeStruct(dims, dtype)


VECTORS = pl.BlockSpec(memory_space=pltpu.VMEM)
ANYWHERE = pl.BlockSpec(memory_space=pl.ANY)


def hbm(weight):
    return pltpu.with_memory_space_constraint(weight, pltpu.HBM)


def pack_kernel(tokens, ids, gates, later, out_ref, later_ref, tokens_ref, ids_ref, gates_ref, sems):
    pairs = [(tokens, tokens_ref), (ids, ids_ref), (gates, gates_ref), (later, later_ref)]
    copies = [pltpu.make_async_copy(a, b, sems.at[k]) for k, (a, b) in enumerate(pairs)]
    for copy in copies:
        copy.start()
    for copy in copies:
        copy.wait()
    rows, width = tokens_ref.shape
    out_ref[:, :width] = tokens_ref[...]
    values = gates_ref[...]
    high = values.astype(BF16).astype(F32)
    middle = (values - high).astype(BF16).astype(F32)
    low = values - high - middle
    fields = jnp.concatenate([ids_ref[...].astype(F32), high, middle, low], axis=0)
    fields = jnp.pad(fields, ((0, LANES - fields.shape[0]), (0, LANES - rows)))
    out_ref[:, width:] = jnp.transpose(fields)[:rows].astype(BF16)


def stack_kernel(count, later, *refs):
    parts, out_ref = refs[:count], refs[-1 - later]
    rows = parts[0].shape[0]
    for k, part in enumerate(parts):
        out_ref[k * rows : (k + 1) * rows] = part[...]
    if later:
        refs[-1][...] = refs[count][...]


def stack(parts, after, name, later=()):
    rows, width = parts[0].shape
    outs = call(
        functools.partial(stack_kernel, len(parts), len(later)),
        name,
        [shaped(BF16, rows * len(parts), width)] + [shaped(BF16, *array.shape) for array in later],
        [*parts, *later, *after],
        specs=[VECTORS] * (len(parts) + len(later)) + [ANYWHERE] * len(after),
        limit=16,
    )
    return outs if later else outs[0]


def add_kernel(count, skip, *refs):
    parts, outs = refs[:count], refs[count + skip :]
    total = parts[0][...].astype(F32)
    for part in parts[1:]:
        total = total + part[...].astype(F32)
    total = total.astype(BF16).reshape((len(outs),) + outs[0].shape)
    for k, out in enumerate(outs):
        out[...] = total[k]


def add(parts, pieces, after, name):
    *lead, rows, width = parts[0].shape
    each = math.prod(lead) * rows // pieces
    return call(
        functools.partial(add_kernel, len(parts), len(after)),
        name,
        [shaped(BF16, each, width)] * pieces,
        [*parts, *after],
        specs=[VECTORS] * len(parts) + [ANYWHERE] * len(after),
        limit=16,
    )


def back_over_cores(grid, parts, after, name):
    got = [grid.shift(parts[c], dc=-c) for c in range(1, grid.nc)]
    return add([parts[0], *got], len(grid.square), after, name)


def back_over_plane(grid, kept, after, name):
    got = [grid.shift(part, dx=-a, dy=-b) for part, (a, b) in zip(kept[1:], grid.square[1:])]
    return add([kept[0], *got], grid.nz, after, name)


def back_along_z(grid, total, after, name):
    got = [grid.shift(total[k], dz=k) for k in range(1, grid.nz)]
    return add([total[0], *got], 1, after, name)[0]


def tables(aux, first, rows, local, block):
    tokens = aux.shape[0]
    across = jnp.transpose(aux.astype(F32))
    ids = [across[k : k + 1] for k in range(2)]
    gates = [across[2 + k : 3 + k] + across[4 + k : 5 + k] + across[6 + k : 7 + k] for k in range(2)]
    total = local * rows
    r = lax.broadcasted_iota(jnp.int32, (total, tokens), 0)
    j = lax.broadcasted_iota(jnp.int32, (total, tokens), 1)
    expert = ((r >> log2(rows)) + first).astype(F32)
    own_block = ((r & (rows - 1)) >> log2(CAP)) == (j >> log2(block))
    slot = (r & (CAP - 1)).astype(F32)
    hits = [(ids[k] == expert).astype(F32) for k in range(2)]
    hit = hits[0] + hits[1]
    up = lax.broadcasted_iota(jnp.int32, (tokens, tokens), 0)
    to = lax.broadcasted_iota(jnp.int32, (tokens, tokens), 1)
    earlier = ((up >> log2(block)) == (to >> log2(block))) & (up < to)
    position = dot(hit.astype(BF16), jnp.where(earlier, 1.0, 0.0).astype(BF16))
    select = jnp.where(own_block & (position == slot), hit, 0.0)
    gate = jnp.sum(select * (hits[0] * gates[0] + hits[1] * gates[1]), axis=1, keepdims=True)
    return select, gate


def streamed(weight, held, sems, columns):
    depth = held.shape[0]
    copies = [
        pltpu.make_async_copy(
            weight.at[:, :, pl.ds(start, size)], held.at[k % depth, :, :, pl.ds(0, size)], sems.at[k % depth]
        )
        for k, (start, size) in enumerate(columns)
    ]
    for copy in copies[:depth]:
        copy.start()

    def each():
        for k, copy in enumerate(copies):
            copy.wait()
            size = columns[k][1]
            yield held.at[k % depth, :, :, pl.ds(0, size)]
            if k + depth < len(copies):
                copies[k + depth].start()

    return each()


def kept(weight, held, sems, columns, ahead=4):
    copies = []
    for k, (start, size) in enumerate(columns):
        at = (slice(None), slice(None), pl.ds(start, size))
        copies.append(pltpu.make_async_copy(weight.at[at], held.at[at], sems.at[k]))

    for copy in copies[:ahead]:
        copy.start()

    def each():
        for k, copy in enumerate(copies):
            copy.wait()
            start, size = columns[k]
            yield held.at[:, :, pl.ds(start, size)]
            if k + ahead < len(copies):
                copies[k + ahead].start()

    return each()


class Sizes:
    def __init__(self, grid, tokens, w_gate):
        self.grid = grid
        self.local, self.hidden, self.features = w_gate.shape
        self.block, self.width = tokens.shape
        self.rows = grid.dp * CAP
        self.total = self.local * self.rows
        self.count = grid.dp * self.block
        self.column = grid.nz * self.block
        self.blocks = grid.nc * grid.ny * grid.nx
        self.slices = grid.nc * grid.ny
        whole = self.width % 256 == 0 and self.width > 1024
        self.pieces = [(0, 1024), (1024, self.width - 1024)] if whole else [(0, self.width)]
        self.parts = [(0, 512), (512, 512), (1024, self.width - 1024)] if whole else [(0, self.width)]

    def walk(self):
        return [(k, at, size) for k in range(self.slices) for at, size in self.pieces]

    def at(self, e):
        return slice(e * self.rows, (e + 1) * self.rows)


def routed(s, block, select):
    for k in range(s.slices):
        group = [block(k // s.grid.ny, a, k % s.grid.ny) for a in range(s.grid.nx)]
        yield k, dot(select, jnp.concatenate(group, axis=0))


def gate_kernel(s, *refs):
    blocks = refs[: s.blocks]
    w_ref, _, x_ref, select_ref, back_ref, gate_ref, g_ref, held_ref, sems = refs[s.blocks :]
    walk = s.walk()
    weights = kept(w_ref, held_ref, sems, [(k * s.width + at, size) for k, at, size in walk])
    aux = jnp.concatenate([ref[:, s.width :] for ref in blocks[: s.grid.nx]], axis=0)
    select, gate = tables(aux, lax.axis_index("hst") * s.local, s.rows, s.local, s.block)
    gate_ref[...] = jnp.broadcast_to(gate, gate_ref.shape)
    select_ref[...] = select.astype(BF16)
    back_ref[...] = jnp.transpose(select).astype(BF16)

    def block(c, a, b):
        return blocks[(c * s.grid.ny + b) * s.grid.nx + a][:, : s.width]

    for k, picked in routed(s, block, select.astype(BF16)):
        x_ref[s.grid.source(k)] = picked.astype(BF16)
    g = [0.0] * s.local
    for (k, at, size), weight in zip(walk, weights):
        for e in range(s.local):
            g[e] += dot_t(x_ref[k, s.at(e), at : at + size], weight[e])
    for e in range(s.local):
        g_ref[e] = g[e]


def up_kernel(s, x_ref, g_ref, w_ref, _, act_ref, p_ref, q_ref, room, sems):
    walk = s.walk()
    weights = streamed(w_ref, room, sems, [(k * s.width + at, size) for k, at, size in walk])
    u = [0.0] * s.local
    for (k, at, size), weight in zip(walk, weights):
        for e in range(s.local):
            u[e] += dot_t(x_ref[k, s.at(e), at : at + size], weight[e])
    for e in range(s.local):
        g = g_ref[e]
        sigma = jax.nn.sigmoid(g)
        act_ref[e] = (g * sigma * u[e]).astype(BF16)
        p_ref[e] = u[e] * sigma * (1.0 + g * (1.0 - sigma))
        q_ref[e] = g * sigma


def to_tokens(s, k, at, found, back_ref, outs):
    each = s.slices // s.grid.nc
    sums = dot(back_ref[...], jnp.concatenate(found, axis=0)).astype(BF16)
    size = sums.shape[-1]
    outs[k // each][:, k % each, :, at : at + size] = sums.reshape(s.grid.nx, s.column, size)


def relative(s, walk):
    return [(pl.multiple_of(s.grid.source(k) * s.width + at, LANES), size) for k, at, size in walk]


def down_kernel(s, *refs):
    first = 2 * s.grid.nc
    blocks = refs[:first]
    select_ref, gate_ref, back_ref, act_ref, p_ref, q_ref, w_ref = refs[first : first + 7]
    outs, (d_ref, dg_ref, du_ref, room, sems) = refs[first + 7 : -5], refs[-5:]
    walk = s.walk()
    weights = streamed(w_ref, room, sems, relative(s, walk))

    def block(c, a, b):
        n = s.grid.square.index((a, b)) - 1
        return blocks[2 * c][...] if n < 0 else blocks[2 * c + 1][n * s.column : (n + 1) * s.column]

    for k, picked in routed(s, block, select_ref[...]):
        d_ref[s.grid.source(k)] = (picked * gate_ref[:, :1]).astype(BF16)
    da = [0.0] * s.local
    for (k, at, size), weight in zip(walk, weights):
        found = []
        for e in range(s.local):
            found.append((dot(act_ref[e], weight[e]) * gate_ref[s.at(e), :1]).astype(BF16))
            da[e] += dot_t(d_ref[s.grid.source(k), s.at(e), at : at + size], weight[e])
        to_tokens(s, k, at, found, back_ref, outs)
    for e in range(s.local):
        dg_ref[e] = (da[e] * p_ref[e]).astype(BF16)
        du_ref[e] = (da[e] * q_ref[e]).astype(BF16)


def backward_kernel(s, dg_ref, du_ref, back_ref, held_ref, w_ref, _, *refs):
    outs, (room, sems) = refs[:-2], refs[-2:]
    walk = s.walk()
    columns = relative(s, walk)
    for (k, at, size), (start, _), weight in zip(walk, columns, streamed(w_ref, room, sems, columns)):
        gate = held_ref.at[:, :, pl.ds(start, size)]
        found = [
            (dot(dg_ref[e], gate[e]) + dot(du_ref[e], weight[e])).astype(BF16)
            for e in range(s.local)
        ]
        to_tokens(s, k, at, found, back_ref, outs)


def grad_kernel(s, left_ref, rows_ref, _, out, marker, turned, room, sems):
    marker[...] = jnp.zeros_like(marker)
    for e in range(s.local):
        turned[e] = jnp.transpose(left_ref[e].astype(F32)).astype(BF16)
    depth = room.shape[0]
    copies = []
    for k in range(s.slices):
        for at, size in s.parts:
            n = len(copies)
            if n >= depth:
                copies[n - depth].wait()
            for e in range(s.local):
                room[n % depth, e, :, :size] = dot(turned[e], rows_ref[k, s.at(e), at : at + size]).astype(BF16)
            copies.append(
                pltpu.make_async_copy(
                    room.at[n % depth, :, :, pl.ds(0, size)],
                    out.at[:, :, pl.ds(k * s.width + at, size)],
                    sems.at[n % depth],
                )
            )
            copies[-1].start()
    for copy in copies[-depth:]:
        copy.wait()


def grad(s, name, left, right, after):
    room = max(size for _, size in s.parts)
    return call(
        functools.partial(grad_kernel, s),
        name,
        [shaped(BF16, s.local, s.hidden, s.features), shaped(F32, 8, LANES)],
        [left, right, after],
        specs=[VECTORS, VECTORS, ANYWHERE],
        out_specs=[ANYWHERE, VECTORS],
        scratch=[
            pltpu.VMEM((s.local, s.hidden, s.rows), BF16),
            pltpu.VMEM((4, s.local, s.hidden, room), BF16),
            pltpu.SemaphoreType.DMA((4,)),
        ],
        cost=46000,
    )


def body(tokens, cotangent, expert_ids, gate_values, w_gate, w_up, w_down):
    grid = Grid(lax.axis_size("dp"), lax.axis_size("hst"))
    s = Sizes(grid, tokens, w_gate)

    sources = [tokens, expert_ids.T, gate_values.T, cotangent]
    message, cotangent = call(
        pack_kernel,
        "pack",
        [shaped(BF16, s.block, s.width + LANES), shaped(BF16, s.block, s.width)],
        [hbm(source) for source in sources],
        specs=[ANYWHERE] * 4,
        scratch=[pltpu.VMEM(a.shape, a.dtype) for a in sources[:3]] + [pltpu.SemaphoreType.DMA((4,))],
    )
    x_parts = grid.along_z(message)
    x_column, cotangent = stack(x_parts, [], "stack_tokens", [cotangent])
    x_plane = grid.over_plane(x_column)
    d_halves = grid.doubled_along_z(cotangent)
    d_column = d_halves[-1]
    last = grid.square[-1]
    x_plane[last] = stack([x_plane[last]], [d_column], "relay")
    x_blocks = grid.over_cores(x_plane)
    d_column = stack([d_column], x_blocks, "stack_cotangents")
    room = max(size for _, size in s.pieces)
    streams = [pltpu.VMEM((3, s.local, s.hidden, room), BF16), pltpu.SemaphoreType.DMA((3,))]

    hidden_shape = (s.local, s.rows, s.hidden)
    rows_shape = shaped(BF16, s.slices, s.total, s.width)
    x_rows, select, back, gate, g, held_gate = call(
        functools.partial(gate_kernel, s),
        "gate",
        [
            rows_shape,
            shaped(BF16, s.total, s.count),
            shaped(BF16, s.count, s.total),
            shaped(F32, s.total, LANES),
            shaped(F32, *hidden_shape),
            pltpu.VMEM(w_gate.shape, BF16),
        ],
        [*x_blocks, hbm(w_gate), d_column],
        specs=[VECTORS] * s.blocks + [ANYWHERE] * 2,
        scratch=[pltpu.SemaphoreType.DMA((len(s.walk()),))],
        cost=46000,
    )
    d_plane = grid.over_plane(d_column)
    d_others = stack([d_plane[at] for at in grid.square[1:]], [gate], "stack_planes")
    act, p, q = call(
        functools.partial(up_kernel, s),
        "up",
        [
            shaped(BF16, *hidden_shape),
            shaped(F32, *hidden_shape),
            shaped(F32, *hidden_shape),
        ],
        [x_rows, g, hbm(w_up), d_others],
        specs=[VECTORS] * 2 + [ANYWHERE] * 2,
        scratch=streams,
        cost=46000,
    )
    d_blocks = [d_column, d_others]
    for c in range(1, grid.nc):
        d_blocks += [grid.shift(d_column, dc=c), grid.shift(d_others, dc=c)]
    sums = shaped(BF16, grid.nx, grid.ny, s.column, s.width)
    *out_parts, d_rows, d_gate, d_up = call(
        functools.partial(down_kernel, s),
        "down",
        [sums] * grid.nc + [rows_shape, shaped(BF16, *hidden_shape), shaped(BF16, *hidden_shape)],
        [*d_blocks, select, gate, back, act, p, q, hbm(w_down)],
        specs=[VECTORS] * (len(d_blocks) + 6) + [ANYWHERE],
        scratch=streams,
        cost=46000,
    )
    back_parts = call(
        functools.partial(backward_kernel, s),
        "backward",
        [sums] * grid.nc,
        [d_gate, d_up, back, held_gate, hbm(w_up), d_rows],
        specs=[VECTORS] * 4 + [ANYWHERE] * 2,
        scratch=streams,
        cost=46000,
    )
    mixed_kept = back_over_cores(grid, out_parts, back_parts[:1], "mixed_cores")
    grad_down, down_done = grad(s, "grad_down", act, d_rows, mixed_kept[0])
    token_kept = back_over_cores(grid, back_parts, [down_done], "tokens_cores")
    mixed_total = back_over_plane(grid, mixed_kept, token_kept[:1], "mixed_plane")
    grad_gate, gate_done = grad(s, "grad_gate", d_gate, x_rows, mixed_total[0])
    mixed = back_along_z(grid, mixed_total, [gate_done], "mixed_z")
    token_total = back_over_plane(grid, token_kept, [gate_done], "tokens_plane")
    grad_up, up_done = grad(s, "grad_up", d_up, x_rows, token_total[0])
    grad_tokens = back_along_z(grid, token_total, [up_done], "tokens_z")
    return mixed, grad_tokens, grad_gate, grad_up, grad_down


def solution(mesh):
    return jax.shard_map(
        body,
        mesh=mesh,
        in_specs=(
            P("dp", "hst"),
            P("dp", "hst"),
            P("dp", None),
            P("dp", None),
            P("hst", "dp", None),
            P("hst", "dp", None),
            P("hst", "dp", None),
        ),
        out_specs=(
            P("dp", "hst"),
            P("dp", "hst"),
            P("hst", "dp", None),
            P("hst", "dp", None),
            P("hst", "dp", None),
        ),
        check_vma=False,
    )
```

```python
import functools
import math

import jax
import jax.numpy as jnp
from jax import lax
from jax.experimental import pallas as pl
from jax.experimental.pallas import tpu as pltpu
from jax.sharding import PartitionSpec as P

CAP = 4
LANES = 128
AHEAD = 4
MIB = 1 << 20
MFLOP = 10**6
F32 = jnp.float32
BF16 = jnp.bfloat16
AXES = ("dp", "hst")


def dot(a, b):
    return lax.dot_general(a, b, (((1,), (0,)), ((), ())), preferred_element_type=F32)


def dot_t(a, b):
    return lax.dot_general(a, b, (((1,), (1,)), ((), ())), preferred_element_type=F32)


def log2(n):
    assert n & (n - 1) == 0
    return n.bit_length() - 1


class Grid:
    def __init__(self, dp, hst):
        self.dp, self.hst = dp, hst
        self.nc = 2 if hst % 2 == 0 else 1
        self.ny = hst // self.nc
        self.nx = self.ny if dp % self.ny == 0 else 1
        self.nz = dp // self.nx
        assert self.nz & (self.nz - 1) == 0
        self.square = [(a, b) for a in range(self.nx) for b in range(self.ny)]

    def shift(self, value, dz=0, dx=0, dy=0, dc=0):
        pairs = []
        for z in range(self.nz):
            for x in range(self.nx):
                for y in range(self.ny):
                    for c in range(self.nc):
                        to_dp = (z ^ dz) * self.nx + (x + dx) % self.nx
                        to_hst = (y + dy) % self.ny * self.nc + (c + dc) % self.nc
                        here = (z * self.nx + x) * self.hst + y * self.nc + c
                        pairs.append((here, to_dp * self.hst + to_hst))
        return lax.ppermute(value, AXES, pairs)

    def along_z(self, mine):
        return [mine] + [self.shift(mine, dz=k) for k in range(1, self.nz)]

    def doubled_along_z(self, mine):
        columns, k = [mine], 1
        while k < self.nz:
            columns.append(stack([columns[-1], self.shift(columns[-1], dz=k)], [], "double"))
            k *= 2
        return columns

    def over_plane(self, column):
        return {(a, b): self.shift(column, dx=a, dy=b) if a or b else column for a, b in self.square}

    def over_cores(self, column, others):
        blocks = [column, others]
        for c in range(1, self.nc):
            blocks += [self.shift(column, dc=c), self.shift(others, dc=c)]
        return blocks

    def source(self, k):
        host = lax.axis_index("hst")
        y, core = host >> log2(self.nc), host & (self.nc - 1)
        return (((y - k % self.ny) & (self.ny - 1)) << log2(self.nc)) + ((core + k // self.ny) & (self.nc - 1))


def call(kernel, name, outs, args, specs=None, out_specs=None, scratch=(), grid=(), limit=16, cost=0, aliases=None):
    specs = specs or [pl.BlockSpec(memory_space=pltpu.VMEM)] * len(args)
    out_specs = out_specs or [pl.BlockSpec(memory_space=pltpu.VMEM)] * len(outs)
    return pl.pallas_call(
        kernel,
        name=name,
        grid=grid,
        out_shape=outs,
        in_specs=specs,
        out_specs=out_specs,
        scratch_shapes=list(scratch),
        input_output_aliases=aliases or {},
        compiler_params=pltpu.CompilerParams(vmem_limit_bytes=limit * MIB),
        cost_estimate=pl.CostEstimate(flops=cost * MFLOP, bytes_accessed=0, transcendentals=0),
    )(*args)


def shaped(dtype, *dims):
    return jax.ShapeDtypeStruct(dims, dtype)


VECTORS = pl.BlockSpec(memory_space=pltpu.VMEM)
ANYWHERE = pl.BlockSpec(memory_space=pl.ANY)


def hbm(weight):
    return pltpu.with_memory_space_constraint(weight, pltpu.HBM)


def pack_kernel(tokens, ids, gates, later, out_ref, later_ref, tokens_ref, ids_ref, gates_ref, sems):
    pairs = [(tokens, tokens_ref), (ids, ids_ref), (gates, gates_ref), (later, later_ref)]
    copies = [pltpu.make_async_copy(a, b, sems.at[k]) for k, (a, b) in enumerate(pairs)]
    for copy in copies:
        copy.start()
    for copy in copies:
        copy.wait()
    rows, width = tokens_ref.shape
    out_ref[:, :width] = tokens_ref[...]
    values = gates_ref[...]
    high = values.astype(BF16).astype(F32)
    middle = (values - high).astype(BF16).astype(F32)
    low = values - high - middle
    fields = jnp.concatenate([ids_ref[...].astype(F32), high, middle, low], axis=0)
    fields = jnp.pad(fields, ((0, LANES - fields.shape[0]), (0, LANES - rows)))
    out_ref[:, width:] = jnp.transpose(fields)[:rows].astype(BF16)


def stack_kernel(count, later, *refs):
    parts, out_ref = refs[:count], refs[-1 - later]
    rows = parts[0].shape[0]
    for k, part in enumerate(parts):
        out_ref[k * rows : (k + 1) * rows] = part[...]
    if later:
        refs[-1][...] = refs[count][...]


def stack(parts, after, name, later=()):
    rows, width = parts[0].shape
    outs = call(
        functools.partial(stack_kernel, len(parts), len(later)),
        name,
        [shaped(BF16, rows * len(parts), width)] + [shaped(BF16, *array.shape) for array in later],
        [*parts, *later, *after],
        specs=[VECTORS] * (len(parts) + len(later)) + [ANYWHERE] * len(after),
        limit=16,
    )
    return outs if later else outs[0]


def add_kernel(count, skip, pieces, *refs):
    parts, outs = refs[:count], refs[count + skip : count + skip + pieces]
    total = parts[0][...].astype(F32)
    for part in parts[1:]:
        total = total + part[...].astype(F32)
    total = total.astype(BF16).reshape((pieces,) + outs[0].shape)
    for k, out in enumerate(outs):
        out[...] = total[k]


def add(parts, pieces, after, name, later=()):
    *lead, rows, width = parts[0].shape
    each = math.prod(lead) * rows // pieces
    first = len(parts) + len(after)
    return call(
        functools.partial(add_kernel, len(parts), len(after) + len(later), pieces),
        name,
        [shaped(BF16, each, width)] * pieces + [shaped(BF16, *array.shape) for array in later],
        [*parts, *after, *later],
        specs=[VECTORS] * len(parts) + [ANYWHERE] * (len(after) + len(later)),
        out_specs=[VECTORS] * pieces + [ANYWHERE] * len(later),
        aliases={first + k: pieces + k for k in range(len(later))},
    )


def back_over_cores(grid, parts, after, name):
    got = [grid.shift(parts[c], dc=-c) for c in range(1, grid.nc)]
    return add([parts[0], *got], len(grid.square), after, name)


def back_over_plane(grid, kept, after, name, later=()):
    got = [grid.shift(part, dx=-a, dy=-b) for part, (a, b) in zip(kept[1:], grid.square[1:])]
    return add([kept[0], *got], grid.nz, after, name, later)


def back_along_z(grid, total, after, name):
    got = [grid.shift(total[k], dz=k) for k in range(1, grid.nz)]
    return add([total[0], *got], 1, after, name)[0]


def tables(aux, first, rows, local, block):
    tokens = aux.shape[0]
    across = jnp.transpose(aux.astype(F32))
    ids = [across[k : k + 1] for k in range(2)]
    gates = [across[2 + k : 3 + k] + across[4 + k : 5 + k] + across[6 + k : 7 + k] for k in range(2)]
    total = local * rows
    r = lax.broadcasted_iota(jnp.int32, (total, tokens), 0)
    j = lax.broadcasted_iota(jnp.int32, (total, tokens), 1)
    expert = ((r >> log2(rows)) + first).astype(F32)
    own_block = ((r & (rows - 1)) >> log2(CAP)) == (j >> log2(block))
    slot = (r & (CAP - 1)).astype(F32)
    hits = [(ids[k] == expert).astype(F32) for k in range(2)]
    hit = hits[0] + hits[1]
    up = lax.broadcasted_iota(jnp.int32, (tokens, tokens), 0)
    to = lax.broadcasted_iota(jnp.int32, (tokens, tokens), 1)
    earlier = ((up >> log2(block)) == (to >> log2(block))) & (up < to)
    position = dot(hit.astype(BF16), jnp.where(earlier, 1.0, 0.0).astype(BF16))
    select = jnp.where(own_block & (position == slot), hit, 0.0)
    gate = jnp.sum(select * (hits[0] * gates[0] + hits[1] * gates[1]), axis=1, keepdims=True)
    return select, gate


def streamed(weight, held, sems, columns):
    depth = held.shape[0]
    copies = [
        pltpu.make_async_copy(
            weight.at[:, :, pl.ds(start, size)], held.at[k % depth, :, :, pl.ds(0, size)], sems.at[k % depth]
        )
        for k, (start, size) in enumerate(columns)
    ]
    for copy in copies[:depth]:
        copy.start()

    def each():
        for k, copy in enumerate(copies):
            copy.wait()
            size = columns[k][1]
            yield held.at[k % depth, :, :, pl.ds(0, size)]
            if k + depth < len(copies):
                copies[k + depth].start()

    return each()


def kept(weight, held, sems, columns, ahead=4):
    copies = []
    for k, (start, size) in enumerate(columns):
        at = (slice(None), slice(None), pl.ds(start, size))
        copies.append(pltpu.make_async_copy(weight.at[at], held.at[at], sems.at[k]))

    for copy in copies[:ahead]:
        copy.start()

    def each():
        for k, copy in enumerate(copies):
            copy.wait()
            start, size = columns[k]
            yield held.at[:, :, pl.ds(start, size)]
            if k + ahead < len(copies):
                copies[k + ahead].start()

    return each()


class Sizes:
    def __init__(self, grid, tokens, w_gate):
        self.grid = grid
        self.local, self.hidden, self.features = w_gate.shape
        self.block, self.width = tokens.shape
        self.rows = grid.dp * CAP
        self.total = self.local * self.rows
        self.count = grid.dp * self.block
        self.column = grid.nz * self.block
        self.blocks = grid.nc * grid.ny * grid.nx
        self.slices = grid.nc * grid.ny
        whole = self.width % 256 == 0 and self.width > 1024
        self.pieces = [(0, 1024), (1024, self.width - 1024)] if whole else [(0, self.width)]
        self.parts = [(0, 512), (512, 512), (1024, self.width - 1024)] if whole else [(0, self.width)]

    def walk(self):
        return [(k, at, size) for k in range(self.slices) for at, size in self.pieces]

    def block_of(self, blocks, c, a, b):
        n = self.grid.square.index((a, b)) - 1
        return blocks[2 * c] if n < 0 else blocks[2 * c + 1].at[n * self.column : (n + 1) * self.column]

    def at(self, e):
        return slice(e * self.rows, (e + 1) * self.rows)


def routed(s, blocks, select):
    for k in range(s.slices):
        group = [s.block_of(blocks, k // s.grid.ny, a, k % s.grid.ny)[:, : s.width] for a in range(s.grid.nx)]
        yield k, dot(select, jnp.concatenate(group, axis=0))


def gate_up_kernel(s, *refs):
    blocks, refs = refs[: 2 * s.grid.nc], refs[2 * s.grid.nc :]
    wg_ref, wu_ref, _, x_ref, select_ref, back_ref, gate_ref, act_ref, p_ref, q_ref, held_ref, room, sems, held_sems = refs
    walk = s.walk()
    columns = [(k * s.width + at, size) for k, at, size in walk]
    gates, ups = kept(wg_ref, held_ref, held_sems, columns), streamed(wu_ref, room, sems, columns)
    aux = jnp.concatenate([s.block_of(blocks, 0, a, 0)[:, s.width :] for a in range(s.grid.nx)], axis=0)
    select, gate = tables(aux, lax.axis_index("hst") * s.local, s.rows, s.local, s.block)
    gate_ref[...] = jnp.broadcast_to(gate, gate_ref.shape)
    select_ref[...] = select.astype(BF16)
    back_ref[...] = jnp.transpose(select).astype(BF16)
    for k, picked in routed(s, blocks, select.astype(BF16)):
        x_ref[s.grid.source(k)] = picked.astype(BF16)
    g, u = [0.0] * s.local, [0.0] * s.local
    for (k, at, size), wg, wu in zip(walk, gates, ups):
        for e in range(s.local):
            x = x_ref[k, s.at(e), at : at + size]
            g[e] += dot_t(x, wg[e])
            u[e] += dot_t(x, wu[e])
    for e in range(s.local):
        sigma = jax.nn.sigmoid(g[e])
        act_ref[e] = (g[e] * sigma * u[e]).astype(BF16)
        p_ref[e] = u[e] * sigma * (1.0 + g[e] * (1.0 - sigma))
        q_ref[e] = g[e] * sigma


def to_tokens(s, k, at, found, back_ref, outs):
    each = s.slices // s.grid.nc
    sums = dot(back_ref[...], jnp.concatenate(found, axis=0)).astype(BF16)
    size = sums.shape[-1]
    outs[k // each][:, k % each, :, at : at + size] = sums.reshape(s.grid.nx, s.column, size)


def relative(s, walk):
    return [(pl.multiple_of(s.grid.source(k) * s.width + at, LANES), size) for k, at, size in walk]


def down_kernel(s, *refs):
    first = 2 * s.grid.nc
    blocks = refs[:first]
    select_ref, gate_ref, back_ref, act_ref, p_ref, q_ref, w_ref = refs[first : first + 7]
    outs, (d_ref, dg_ref, du_ref, room, sems) = refs[first + 7 : -5], refs[-5:]
    walk = s.walk()
    weights = streamed(w_ref, room, sems, relative(s, walk))
    for k, picked in routed(s, blocks, select_ref[...]):
        d_ref[s.grid.source(k)] = (picked * gate_ref[:, :1]).astype(BF16)
    da = [0.0] * s.local
    for (k, at, size), weight in zip(walk, weights):
        found = []
        for e in range(s.local):
            found.append((dot(act_ref[e], weight[e]) * gate_ref[s.at(e), :1]).astype(BF16))
            da[e] += dot_t(d_ref[s.grid.source(k), s.at(e), at : at + size], weight[e])
        to_tokens(s, k, at, found, back_ref, outs)
    for e in range(s.local):
        dg_ref[e] = (da[e] * p_ref[e]).astype(BF16)
        du_ref[e] = (da[e] * q_ref[e]).astype(BF16)


def backward_kernel(s, dg_ref, du_ref, back_ref, act_ref, d_ref, held_ref, w_ref, _, *refs):
    outs, (out, room, sems, turned, store, out_sems) = refs[:-6], refs[-6:]
    walk = s.walk()
    columns = relative(s, walk)
    weights = streamed(w_ref, room, sems, columns)
    turn(s, act_ref, turned)
    stores = Stores(out, store, out_sems)
    for (k, at, size), (start, _), weight in zip(walk, columns, weights):
        gate = held_ref.at[:, :, pl.ds(start, size)]
        found = [(dot(dg_ref[e], gate[e]) + dot(du_ref[e], weight[e])).astype(BF16) for e in range(s.local)]
        to_tokens(s, k, at, found, back_ref, outs)
        room_for = stores.next(size)
        for e in range(s.local):
            rows = d_ref[s.grid.source(k), s.at(e), at : at + size]
            room_for[e] = dot(turned[e], rows).astype(BF16)
        stores.send(start, size)
    stores.finish()


def turn(s, left_ref, turned):
    for e in range(s.local):
        turned[e] = jnp.transpose(left_ref[e].astype(F32)).astype(BF16)


class Stores:
    def __init__(self, out, room, sems):
        self.out, self.room, self.sems = out, room, sems
        self.copies = []

    def slot(self, size):
        return self.room.at[len(self.copies) % self.room.shape[0], :, :, pl.ds(0, size)]

    def next(self, size):
        n = len(self.copies) - self.room.shape[0]
        if n >= 0:
            self.copies[n].wait()
        return self.slot(size)

    def send(self, start, size):
        sem = self.sems.at[len(self.copies) % self.room.shape[0]]
        copy = pltpu.make_async_copy(self.slot(size), self.out.at[:, :, pl.ds(start, size)], sem)
        copy.start()
        self.copies.append(copy)

    def finish(self):
        for copy in self.copies[-self.room.shape[0] :]:
            copy.wait()


def grad_kernel(s, left_ref, rows_ref, _, out, marker, turned, store, sems):
    marker[...] = jnp.zeros_like(marker)
    turn(s, left_ref, turned)
    stores = Stores(out, store, sems)
    for k in range(s.slices):
        for at, size in s.parts:
            room_for = stores.next(size)
            for e in range(s.local):
                room_for[e] = dot(turned[e], rows_ref[k, s.at(e), at : at + size]).astype(BF16)
            stores.send(k * s.width + at, size)
    stores.finish()


def grad(s, name, left, right, after):
    room = max(size for _, size in s.parts)
    return call(
        functools.partial(grad_kernel, s),
        name,
        [shaped(BF16, s.local, s.hidden, s.features), shaped(F32, 8, LANES)],
        [left, right, after],
        specs=[VECTORS, VECTORS, ANYWHERE],
        out_specs=[ANYWHERE, VECTORS],
        scratch=[
            pltpu.VMEM((s.local, s.hidden, s.rows), BF16),
            pltpu.VMEM((4, s.local, s.hidden, room), BF16),
            pltpu.SemaphoreType.DMA((4,)),
        ],
        cost=46000,
    )


def body(tokens, cotangent, expert_ids, gate_values, w_gate, w_up, w_down):
    grid = Grid(lax.axis_size("dp"), lax.axis_size("hst"))
    s = Sizes(grid, tokens, w_gate)

    sources = [tokens, expert_ids.T, gate_values.T, cotangent]
    message, cotangent = call(
        pack_kernel,
        "pack",
        [shaped(BF16, s.block, s.width + LANES), shaped(BF16, s.block, s.width)],
        [hbm(source) for source in sources],
        specs=[ANYWHERE] * 4,
        scratch=[pltpu.VMEM(a.shape, a.dtype) for a in sources[:3]] + [pltpu.SemaphoreType.DMA((4,))],
    )
    x_parts = grid.along_z(message)
    x_column, cotangent = stack(x_parts, [], "stack_tokens", [cotangent])
    x_plane = grid.over_plane(x_column)
    d_column = grid.doubled_along_z(cotangent)[-1]
    x_others = stack([x_plane[at] for at in grid.square[1:]], [d_column], "stack_tokens_plane")
    x_blocks = grid.over_cores(x_column, x_others)
    d_column = stack([d_column], [x_others], "stack_cotangents")
    d_plane = grid.over_plane(d_column)
    room = max(size for _, size in s.pieces)
    streams = [pltpu.VMEM((3, s.local, s.hidden, room), BF16), pltpu.SemaphoreType.DMA((3,))]

    hidden_shape = (s.local, s.rows, s.hidden)
    rows_shape = shaped(BF16, s.slices, s.total, s.width)
    x_rows, select, back, gate, act, p, q, held_gate = call(
        functools.partial(gate_up_kernel, s),
        "gate_up",
        [
            rows_shape,
            shaped(BF16, s.total, s.count),
            shaped(BF16, s.count, s.total),
            shaped(F32, s.total, LANES),
            shaped(BF16, *hidden_shape),
            shaped(F32, *hidden_shape),
            shaped(F32, *hidden_shape),
            pltpu.VMEM(w_gate.shape, BF16),
        ],
        [*x_blocks, hbm(w_gate), hbm(w_up), d_column],
        specs=[VECTORS] * len(x_blocks) + [ANYWHERE] * 3,
        scratch=[*streams, pltpu.SemaphoreType.DMA((len(s.walk()),))],
        cost=46000,
    )
    d_others = stack([d_plane[at] for at in grid.square[1:]], [gate], "stack_cotangents_plane")
    d_blocks = grid.over_cores(d_column, d_others)
    sums = shaped(BF16, grid.nx, grid.ny, s.column, s.width)
    *out_parts, d_rows, d_gate, d_up = call(
        functools.partial(down_kernel, s),
        "down",
        [sums] * grid.nc + [rows_shape, shaped(BF16, *hidden_shape), shaped(BF16, *hidden_shape)],
        [*d_blocks, select, gate, back, act, p, q, hbm(w_down)],
        specs=[VECTORS] * (len(d_blocks) + 6) + [ANYWHERE],
        scratch=streams,
        cost=46000,
    )
    mixed_kept = back_over_cores(grid, out_parts, [], "mixed_cores")
    *back_parts, grad_down = call(
        functools.partial(backward_kernel, s),
        "backward",
        [sums] * grid.nc + [shaped(BF16, *w_down.shape)],
        [d_gate, d_up, back, act, d_rows, held_gate, hbm(w_up), mixed_kept[0]],
        specs=[VECTORS] * 6 + [ANYWHERE] * 2,
        out_specs=[VECTORS] * grid.nc + [ANYWHERE],
        scratch=[
            *streams,
            pltpu.VMEM((s.local, s.hidden, s.rows), BF16),
            pltpu.VMEM((2, s.local, s.hidden, room), BF16),
            pltpu.SemaphoreType.DMA((2,)),
        ],
        cost=46000,
    )
    *mixed_total, last = back_over_plane(grid, mixed_kept, back_parts[:1], "mixed_plane", back_parts[-1:])
    token_kept = back_over_cores(grid, [*back_parts[:-1], last], [], "tokens_cores")
    grad_gate, gate_done = grad(s, "grad_gate", d_gate, x_rows, token_kept[0])
    mixed = back_along_z(grid, mixed_total, [gate_done], "mixed_z")
    token_total = back_over_plane(grid, token_kept, [gate_done], "tokens_plane")
    grad_up, up_done = grad(s, "grad_up", d_up, x_rows, token_total[0])
    grad_tokens = back_along_z(grid, token_total, [up_done], "tokens_z")
    return mixed, grad_tokens, grad_gate, grad_up, grad_down


def solution(mesh):
    return jax.shard_map(
        body,
        mesh=mesh,
        in_specs=(
            P("dp", "hst"),
            P("dp", "hst"),
            P("dp", None),
            P("dp", None),
            P("hst", "dp", None),
            P("hst", "dp", None),
            P("hst", "dp", None),
        ),
        out_specs=(
            P("dp", "hst"),
            P("dp", "hst"),
            P("hst", "dp", None),
            P("hst", "dp", None),
            P("hst", "dp", None),
        ),
        check_vma=False,
    )
```

```python
import functools
import math

import jax
import jax.numpy as jnp
from jax import lax
from jax.experimental import pallas as pl
from jax.experimental.pallas import tpu as pltpu
from jax.sharding import PartitionSpec as P

CAP = 4
LANES = 128
AHEAD = 4
MIB = 1 << 20
MFLOP = 10**6
F32 = jnp.float32
BF16 = jnp.bfloat16
AXES = ("dp", "hst")


def dot(a, b):
    return lax.dot_general(a, b, (((1,), (0,)), ((), ())), preferred_element_type=F32)


def dot_t(a, b):
    return lax.dot_general(a, b, (((1,), (1,)), ((), ())), preferred_element_type=F32)


def log2(n):
    assert n & (n - 1) == 0
    return n.bit_length() - 1


class Grid:
    def __init__(self, dp, hst):
        self.dp, self.hst = dp, hst
        self.nc = 2 if hst % 2 == 0 else 1
        self.ny = hst // self.nc
        self.nx = self.ny if dp % self.ny == 0 else 1
        self.nz = dp // self.nx
        assert self.nz & (self.nz - 1) == 0
        self.square = [(a, b) for a in range(self.nx) for b in range(self.ny)]

    def shift(self, value, dz=0, dx=0, dy=0, dc=0):
        pairs = []
        for z in range(self.nz):
            for x in range(self.nx):
                for y in range(self.ny):
                    for c in range(self.nc):
                        to_dp = (z ^ dz) * self.nx + (x + dx) % self.nx
                        to_hst = (y + dy) % self.ny * self.nc + (c + dc) % self.nc
                        here = (z * self.nx + x) * self.hst + y * self.nc + c
                        pairs.append((here, to_dp * self.hst + to_hst))
        return lax.ppermute(value, AXES, pairs)

    def along_z(self, mine):
        return [mine] + [self.shift(mine, dz=k) for k in range(1, self.nz)]

    def doubled_along_z(self, mine):
        columns, k = [mine], 1
        while k < self.nz:
            columns.append(stack([columns[-1], self.shift(columns[-1], dz=k)], [], "double"))
            k *= 2
        return columns

    def over_plane(self, column):
        return {(a, b): self.shift(column, dx=a, dy=b) if a or b else column for a, b in self.square}

    def over_cores(self, column, others):
        blocks = [column, others]
        for c in range(1, self.nc):
            blocks += [self.shift(column, dc=c), self.shift(others, dc=c)]
        return blocks

    def source(self, k):
        host = lax.axis_index("hst")
        y, core = host >> log2(self.nc), host & (self.nc - 1)
        return (((y - k % self.ny) & (self.ny - 1)) << log2(self.nc)) + ((core + k // self.ny) & (self.nc - 1))


def call(kernel, name, outs, args, specs=None, out_specs=None, scratch=(), grid=(), limit=16, cost=0, aliases=None):
    specs = specs or [pl.BlockSpec(memory_space=pltpu.VMEM)] * len(args)
    out_specs = out_specs or [pl.BlockSpec(memory_space=pltpu.VMEM)] * len(outs)
    return pl.pallas_call(
        kernel,
        name=name,
        grid=grid,
        out_shape=outs,
        in_specs=specs,
        out_specs=out_specs,
        scratch_shapes=list(scratch),
        input_output_aliases=aliases or {},
        compiler_params=pltpu.CompilerParams(vmem_limit_bytes=limit * MIB),
        cost_estimate=pl.CostEstimate(flops=cost * MFLOP, bytes_accessed=0, transcendentals=0),
    )(*args)


def shaped(dtype, *dims):
    return jax.ShapeDtypeStruct(dims, dtype)


VECTORS = pl.BlockSpec(memory_space=pltpu.VMEM)
ANYWHERE = pl.BlockSpec(memory_space=pl.ANY)


def hbm(weight):
    return pltpu.with_memory_space_constraint(weight, pltpu.HBM)


def pack_kernel(tokens, ids, gates, later, out_ref, later_ref, tokens_ref, ids_ref, gates_ref, sems):
    pairs = [(tokens, tokens_ref), (ids, ids_ref), (gates, gates_ref), (later, later_ref)]
    copies = [pltpu.make_async_copy(a, b, sems.at[k]) for k, (a, b) in enumerate(pairs)]
    for copy in copies:
        copy.start()
    for copy in copies:
        copy.wait()
    rows, width = tokens_ref.shape
    out_ref[:, :width] = tokens_ref[...]
    values = gates_ref[...]
    high = values.astype(BF16).astype(F32)
    middle = (values - high).astype(BF16).astype(F32)
    low = values - high - middle
    fields = jnp.concatenate([ids_ref[...].astype(F32), high, middle, low], axis=0)
    fields = jnp.pad(fields, ((0, LANES - fields.shape[0]), (0, LANES - rows)))
    out_ref[:, width:] = jnp.transpose(fields)[:rows].astype(BF16)


def stack_kernel(count, later, *refs):
    parts, out_ref = refs[:count], refs[-1 - later]
    rows = parts[0].shape[0]
    for k, part in enumerate(parts):
        out_ref[k * rows : (k + 1) * rows] = part[...]
    if later:
        refs[-1][...] = refs[count][...]


def stack(parts, after, name, later=()):
    rows, width = parts[0].shape
    outs = call(
        functools.partial(stack_kernel, len(parts), len(later)),
        name,
        [shaped(BF16, rows * len(parts), width)] + [shaped(BF16, *array.shape) for array in later],
        [*parts, *later, *after],
        specs=[VECTORS] * (len(parts) + len(later)) + [ANYWHERE] * len(after),
        limit=16,
    )
    return outs if later else outs[0]


def add_kernel(count, skip, pieces, *refs):
    parts, outs = refs[:count], refs[count + skip : count + skip + pieces]
    total = parts[0][...].astype(F32)
    for part in parts[1:]:
        total = total + part[...].astype(F32)
    total = total.astype(BF16).reshape((pieces,) + outs[0].shape)
    for k, out in enumerate(outs):
        out[...] = total[k]


def add(parts, pieces, after, name, later=()):
    *lead, rows, width = parts[0].shape
    each = math.prod(lead) * rows // pieces
    first = len(parts) + len(after)
    return call(
        functools.partial(add_kernel, len(parts), len(after) + len(later), pieces),
        name,
        [shaped(BF16, each, width)] * pieces + [shaped(BF16, *array.shape) for array in later],
        [*parts, *after, *later],
        specs=[VECTORS] * len(parts) + [ANYWHERE] * (len(after) + len(later)),
        out_specs=[VECTORS] * pieces + [ANYWHERE] * len(later),
        aliases={first + k: pieces + k for k in range(len(later))},
    )


def back_over_cores(grid, parts, after, name):
    got = [grid.shift(parts[c], dc=-c) for c in range(1, grid.nc)]
    return add([parts[0], *got], len(grid.square), after, name)


def back_over_plane(grid, kept, after, name, later=()):
    got = [grid.shift(part, dx=-a, dy=-b) for part, (a, b) in zip(kept[1:], grid.square[1:])]
    return add([kept[0], *got], grid.nz, after, name, later)


def back_along_z(grid, total, after, name):
    got = [grid.shift(total[k], dz=k) for k in range(1, grid.nz)]
    return add([total[0], *got], 1, after, name)[0]


def tables(aux, first, rows, local, block):
    tokens = aux.shape[0]
    across = jnp.transpose(aux.astype(F32))
    ids = [across[k : k + 1] for k in range(2)]
    gates = [across[2 + k : 3 + k] + across[4 + k : 5 + k] + across[6 + k : 7 + k] for k in range(2)]
    total = local * rows
    r = lax.broadcasted_iota(jnp.int32, (total, tokens), 0)
    j = lax.broadcasted_iota(jnp.int32, (total, tokens), 1)
    expert = ((r >> log2(rows)) + first).astype(F32)
    own_block = ((r & (rows - 1)) >> log2(CAP)) == (j >> log2(block))
    slot = (r & (CAP - 1)).astype(F32)
    hits = [(ids[k] == expert).astype(F32) for k in range(2)]
    hit = hits[0] + hits[1]
    up = lax.broadcasted_iota(jnp.int32, (tokens, tokens), 0)
    to = lax.broadcasted_iota(jnp.int32, (tokens, tokens), 1)
    earlier = ((up >> log2(block)) == (to >> log2(block))) & (up < to)
    position = dot(hit.astype(BF16), jnp.where(earlier, 1.0, 0.0).astype(BF16))
    select = jnp.where(own_block & (position == slot), hit, 0.0)
    gate = jnp.sum(select * (hits[0] * gates[0] + hits[1] * gates[1]), axis=1, keepdims=True)
    return select, gate


def streamed(weight, held, sems, columns):
    depth = held.shape[0]
    copies = [
        pltpu.make_async_copy(
            weight.at[:, :, pl.ds(start, size)], held.at[k % depth, :, :, pl.ds(0, size)], sems.at[k % depth]
        )
        for k, (start, size) in enumerate(columns)
    ]
    for copy in copies[:depth]:
        copy.start()

    def each():
        for k, copy in enumerate(copies):
            copy.wait()
            size = columns[k][1]
            yield held.at[k % depth, :, :, pl.ds(0, size)]
            if k + depth < len(copies):
                copies[k + depth].start()

    return each()


def kept(weight, held, sems, columns, ahead=4):
    copies = []
    for k, (start, size) in enumerate(columns):
        at = (slice(None), slice(None), pl.ds(start, size))
        copies.append(pltpu.make_async_copy(weight.at[at], held.at[at], sems.at[k]))

    for copy in copies[:ahead]:
        copy.start()

    def each():
        for k, copy in enumerate(copies):
            copy.wait()
            start, size = columns[k]
            yield held.at[:, :, pl.ds(start, size)]
            if k + ahead < len(copies):
                copies[k + ahead].start()

    return each()


class Sizes:
    def __init__(self, grid, tokens, w_gate):
        self.grid = grid
        self.local, self.hidden, self.features = w_gate.shape
        self.block, self.width = tokens.shape
        self.rows = grid.dp * CAP
        self.total = self.local * self.rows
        self.count = grid.dp * self.block
        self.column = grid.nz * self.block
        self.blocks = grid.nc * grid.ny * grid.nx
        self.slices = grid.nc * grid.ny
        whole = self.width % 256 == 0 and self.width > 1024
        self.pieces = [(0, 1024), (1024, self.width - 1024)] if whole else [(0, self.width)]
        self.parts = [(0, 512), (512, 512), (1024, self.width - 1024)] if whole else [(0, self.width)]

    def walk(self):
        return [(k, at, size) for k in range(self.slices) for at, size in self.pieces]

    def block_of(self, blocks, c, a, b):
        n = self.grid.square.index((a, b)) - 1
        return blocks[2 * c] if n < 0 else blocks[2 * c + 1].at[n * self.column : (n + 1) * self.column]

    def at(self, e):
        return slice(e * self.rows, (e + 1) * self.rows)


def routed(s, blocks, select):
    for k in range(s.slices):
        group = [s.block_of(blocks, k // s.grid.ny, a, k % s.grid.ny)[:, : s.width] for a in range(s.grid.nx)]
        yield k, dot(select, jnp.concatenate(group, axis=0))


def gate_up_kernel(s, *refs):
    blocks, refs = refs[: 2 * s.grid.nc], refs[2 * s.grid.nc :]
    wg_ref, wu_ref, _, x_ref, select_ref, back_ref, gate_ref, act_ref, p_ref, q_ref, held_ref, room, sems, held_sems = refs
    walk = s.walk()
    columns = [(k * s.width + at, size) for k, at, size in walk]
    gates, ups = kept(wg_ref, held_ref, held_sems, columns), streamed(wu_ref, room, sems, columns)
    aux = jnp.concatenate([s.block_of(blocks, 0, a, 0)[:, s.width :] for a in range(s.grid.nx)], axis=0)
    select, gate = tables(aux, lax.axis_index("hst") * s.local, s.rows, s.local, s.block)
    gate_ref[...] = jnp.broadcast_to(gate, gate_ref.shape)
    select_ref[...] = select.astype(BF16)
    back_ref[...] = jnp.transpose(select).astype(BF16)
    for k, picked in routed(s, blocks, select.astype(BF16)):
        x_ref[s.grid.source(k)] = picked.astype(BF16)
    g, u = [0.0] * s.local, [0.0] * s.local
    for (k, at, size), wg, wu in zip(walk, gates, ups):
        for e in range(s.local):
            x = x_ref[k, s.at(e), at : at + size]
            g[e] += dot_t(x, wg[e])
            u[e] += dot_t(x, wu[e])
    for e in range(s.local):
        sigma = jax.nn.sigmoid(g[e])
        act_ref[e] = (g[e] * sigma * u[e]).astype(BF16)
        p_ref[e] = u[e] * sigma * (1.0 + g[e] * (1.0 - sigma))
        q_ref[e] = g[e] * sigma


def to_tokens(s, k, at, found, back_ref, outs):
    each = s.slices // s.grid.nc
    sums = dot(back_ref[...], jnp.concatenate(found, axis=0)).astype(BF16)
    size = sums.shape[-1]
    outs[k // each][:, k % each, :, at : at + size] = sums.reshape(s.grid.nx, s.column, size)


def relative(s, walk):
    return [(pl.multiple_of(s.grid.source(k) * s.width + at, LANES), size) for k, at, size in walk]


def down_kernel(s, *refs):
    first = 2 * s.grid.nc
    blocks = refs[:first]
    select_ref, gate_ref, back_ref, act_ref, p_ref, q_ref, w_ref = refs[first : first + 7]
    outs, (d_ref, dg_ref, du_ref, room, sems) = refs[first + 7 : -5], refs[-5:]
    walk = s.walk()
    weights = streamed(w_ref, room, sems, relative(s, walk))
    for k, picked in routed(s, blocks, select_ref[...]):
        d_ref[s.grid.source(k)] = (picked * gate_ref[:, :1]).astype(BF16)
    da = [0.0] * s.local
    for (k, at, size), weight in zip(walk, weights):
        found = []
        for e in range(s.local):
            found.append((dot(act_ref[e], weight[e]) * gate_ref[s.at(e), :1]).astype(BF16))
            da[e] += dot_t(d_ref[s.grid.source(k), s.at(e), at : at + size], weight[e])
        to_tokens(s, k, at, found, back_ref, outs)
    for e in range(s.local):
        dg_ref[e] = (da[e] * p_ref[e]).astype(BF16)
        du_ref[e] = (da[e] * q_ref[e]).astype(BF16)


def backward_kernel(s, dg_ref, du_ref, back_ref, x_ref, held_ref, w_ref, _, *refs):
    outs, (out, room, sems, turned, store, out_sems) = refs[:-6], refs[-6:]
    walk = s.walk()
    columns = relative(s, walk)
    weights = streamed(w_ref, room, sems, columns)
    turn(s, dg_ref, turned)
    stores = Stores(out, store, out_sems)
    for (k, at, size), (start, _), weight in zip(walk, columns, weights):
        gate = held_ref.at[:, :, pl.ds(start, size)]
        found = [(dot(dg_ref[e], gate[e]) + dot(du_ref[e], weight[e])).astype(BF16) for e in range(s.local)]
        to_tokens(s, k, at, found, back_ref, outs)
        room_for = stores.next(size)
        for e in range(s.local):
            rows = x_ref[s.grid.source(k), s.at(e), at : at + size]
            room_for[e] = dot(turned[e], rows).astype(BF16)
        stores.send(start, size)
    stores.finish()


def turn(s, left_ref, turned):
    for e in range(s.local):
        turned[e] = jnp.transpose(left_ref[e].astype(F32)).astype(BF16)


class Stores:
    def __init__(self, out, room, sems):
        self.out, self.room, self.sems = out, room, sems
        self.copies = []

    def slot(self, size):
        return self.room.at[len(self.copies) % self.room.shape[0], :, :, pl.ds(0, size)]

    def next(self, size):
        n = len(self.copies) - self.room.shape[0]
        if n >= 0:
            self.copies[n].wait()
        return self.slot(size)

    def send(self, start, size):
        sem = self.sems.at[len(self.copies) % self.room.shape[0]]
        copy = pltpu.make_async_copy(self.slot(size), self.out.at[:, :, pl.ds(start, size)], sem)
        copy.start()
        self.copies.append(copy)

    def finish(self):
        for copy in self.copies[-self.room.shape[0] :]:
            copy.wait()


def grad_kernel(s, left_ref, rows_ref, _, out, marker, turned, store, sems):
    marker[...] = jnp.zeros_like(marker)
    turn(s, left_ref, turned)
    stores = Stores(out, store, sems)
    for k in range(s.slices):
        for at, size in s.parts:
            room_for = stores.next(size)
            for e in range(s.local):
                room_for[e] = dot(turned[e], rows_ref[k, s.at(e), at : at + size]).astype(BF16)
            stores.send(k * s.width + at, size)
    stores.finish()


def grad(s, name, left, right, after):
    room = max(size for _, size in s.parts)
    return call(
        functools.partial(grad_kernel, s),
        name,
        [shaped(BF16, s.local, s.hidden, s.features), shaped(F32, 8, LANES)],
        [left, right, after],
        specs=[VECTORS, VECTORS, ANYWHERE],
        out_specs=[ANYWHERE, VECTORS],
        scratch=[
            pltpu.VMEM((s.local, s.hidden, s.rows), BF16),
            pltpu.VMEM((4, s.local, s.hidden, room), BF16),
            pltpu.SemaphoreType.DMA((4,)),
        ],
        cost=46000,
    )


def body(tokens, cotangent, expert_ids, gate_values, w_gate, w_up, w_down):
    grid = Grid(lax.axis_size("dp"), lax.axis_size("hst"))
    s = Sizes(grid, tokens, w_gate)

    sources = [tokens, expert_ids.T, gate_values.T, cotangent]
    message, cotangent = call(
        pack_kernel,
        "pack",
        [shaped(BF16, s.block, s.width + LANES), shaped(BF16, s.block, s.width)],
        [hbm(source) for source in sources],
        specs=[ANYWHERE] * 4,
        scratch=[pltpu.VMEM(a.shape, a.dtype) for a in sources[:3]] + [pltpu.SemaphoreType.DMA((4,))],
    )
    x_parts = grid.along_z(message)
    x_column, cotangent = stack(x_parts, [], "stack_tokens", [cotangent])
    x_plane = grid.over_plane(x_column)
    d_column = grid.doubled_along_z(cotangent)[-1]
    x_others = stack([x_plane[at] for at in grid.square[1:]], [d_column], "stack_tokens_plane")
    x_blocks = grid.over_cores(x_column, x_others)
    d_column = stack([d_column], [x_others], "stack_cotangents")
    d_plane = grid.over_plane(d_column)
    room = max(size for _, size in s.pieces)
    streams = [pltpu.VMEM((3, s.local, s.hidden, room), BF16), pltpu.SemaphoreType.DMA((3,))]

    hidden_shape = (s.local, s.rows, s.hidden)
    rows_shape = shaped(BF16, s.slices, s.total, s.width)
    x_rows, select, back, gate, act, p, q, held_gate = call(
        functools.partial(gate_up_kernel, s),
        "gate_up",
        [
            rows_shape,
            shaped(BF16, s.total, s.count),
            shaped(BF16, s.count, s.total),
            shaped(F32, s.total, LANES),
            shaped(BF16, *hidden_shape),
            shaped(F32, *hidden_shape),
            shaped(F32, *hidden_shape),
            pltpu.VMEM(w_gate.shape, BF16),
        ],
        [*x_blocks, hbm(w_gate), hbm(w_up), d_column],
        specs=[VECTORS] * len(x_blocks) + [ANYWHERE] * 3,
        scratch=[*streams, pltpu.SemaphoreType.DMA((len(s.walk()),))],
        cost=46000,
    )
    d_others = stack([d_plane[at] for at in grid.square[1:]], [gate], "stack_cotangents_plane")
    d_blocks = grid.over_cores(d_column, d_others)
    sums = shaped(BF16, grid.nx, grid.ny, s.column, s.width)
    *out_parts, d_rows, d_gate, d_up = call(
        functools.partial(down_kernel, s),
        "down",
        [sums] * grid.nc + [rows_shape, shaped(BF16, *hidden_shape), shaped(BF16, *hidden_shape)],
        [*d_blocks, select, gate, back, act, p, q, hbm(w_down)],
        specs=[VECTORS] * (len(d_blocks) + 6) + [ANYWHERE],
        scratch=streams,
        cost=46000,
    )
    mixed_kept = back_over_cores(grid, out_parts, [], "mixed_cores")
    *back_parts, grad_gate = call(
        functools.partial(backward_kernel, s),
        "backward",
        [sums] * grid.nc + [shaped(BF16, *w_down.shape)],
        [d_gate, d_up, back, x_rows, held_gate, hbm(w_up), mixed_kept[0]],
        specs=[VECTORS] * 5 + [ANYWHERE] * 2,
        out_specs=[VECTORS] * grid.nc + [ANYWHERE],
        scratch=[
            *streams,
            pltpu.VMEM((s.local, s.hidden, s.rows), BF16),
            pltpu.VMEM((2, s.local, s.hidden, room), BF16),
            pltpu.SemaphoreType.DMA((2,)),
        ],
        cost=46000,
    )
    *mixed_total, last = back_over_plane(grid, mixed_kept, back_parts[:1], "mixed_plane", back_parts[-1:])
    token_kept = back_over_cores(grid, [*back_parts[:-1], last], [], "tokens_cores")
    grad_down, down_done = grad(s, "grad_down", act, d_rows, token_kept[0])
    mixed = back_along_z(grid, mixed_total, [down_done], "mixed_z")
    token_total = back_over_plane(grid, token_kept, [down_done], "tokens_plane")
    grad_up, up_done = grad(s, "grad_up", d_up, x_rows, token_total[0])
    grad_tokens = back_along_z(grid, token_total, [up_done], "tokens_z")
    return mixed, grad_tokens, grad_gate, grad_up, grad_down


def solution(mesh):
    return jax.shard_map(
        body,
        mesh=mesh,
        in_specs=(
            P("dp", "hst"),
            P("dp", "hst"),
            P("dp", None),
            P("dp", None),
            P("hst", "dp", None),
            P("hst", "dp", None),
            P("hst", "dp", None),
        ),
        out_specs=(
            P("dp", "hst"),
            P("dp", "hst"),
            P("hst", "dp", None),
            P("hst", "dp", None),
            P("hst", "dp", None),
        ),
        check_vma=False,
    )
```

```python
import functools
import math

import jax
import jax.numpy as jnp
from jax import lax
from jax.experimental import pallas as pl
from jax.experimental.pallas import tpu as pltpu
from jax.sharding import PartitionSpec as P

CAP = 4
LANES = 128
AHEAD = 4
MIB = 1 << 20
MFLOP = 10**6
F32 = jnp.float32
BF16 = jnp.bfloat16
AXES = ("dp", "hst")


def dot(a, b):
    return lax.dot_general(a, b, (((1,), (0,)), ((), ())), preferred_element_type=F32)


def dot_t(a, b):
    return lax.dot_general(a, b, (((1,), (1,)), ((), ())), preferred_element_type=F32)


def log2(n):
    assert n & (n - 1) == 0
    return n.bit_length() - 1


class Grid:
    def __init__(self, dp, hst):
        self.dp, self.hst = dp, hst
        self.nc = 2 if hst % 2 == 0 else 1
        self.ny = hst // self.nc
        self.nx = self.ny if dp % self.ny == 0 else 1
        self.nz = dp // self.nx
        assert self.nz & (self.nz - 1) == 0
        self.square = [(a, b) for a in range(self.nx) for b in range(self.ny)]

    def shift(self, value, dz=0, dx=0, dy=0, dc=0):
        pairs = []
        for z in range(self.nz):
            for x in range(self.nx):
                for y in range(self.ny):
                    for c in range(self.nc):
                        to_dp = (z ^ dz) * self.nx + (x + dx) % self.nx
                        to_hst = (y + dy) % self.ny * self.nc + (c + dc) % self.nc
                        here = (z * self.nx + x) * self.hst + y * self.nc + c
                        pairs.append((here, to_dp * self.hst + to_hst))
        return lax.ppermute(value, AXES, pairs)

    def along_z(self, mine):
        return [mine] + [self.shift(mine, dz=k) for k in range(1, self.nz)]

    def over_plane(self, column):
        return {(a, b): self.shift(column, dx=a, dy=b) if a or b else column for a, b in self.square}

    def over_cores(self, column, others):
        blocks = [column, others]
        for c in range(1, self.nc):
            blocks += [self.shift(column, dc=c), self.shift(others, dc=c)]
        return blocks

    def source(self, k):
        host = lax.axis_index("hst")
        y, core = host >> log2(self.nc), host & (self.nc - 1)
        return (((y - k % self.ny) & (self.ny - 1)) << log2(self.nc)) + ((core + k // self.ny) & (self.nc - 1))


def call(kernel, name, outs, args, specs=None, out_specs=None, scratch=(), grid=(), limit=16, cost=0, aliases=None):
    specs = specs or [pl.BlockSpec(memory_space=pltpu.VMEM)] * len(args)
    out_specs = out_specs or [pl.BlockSpec(memory_space=pltpu.VMEM)] * len(outs)
    return pl.pallas_call(
        kernel,
        name=name,
        grid=grid,
        out_shape=outs,
        in_specs=specs,
        out_specs=out_specs,
        scratch_shapes=list(scratch),
        input_output_aliases=aliases or {},
        compiler_params=pltpu.CompilerParams(vmem_limit_bytes=limit * MIB),
        cost_estimate=pl.CostEstimate(flops=cost * MFLOP, bytes_accessed=0, transcendentals=0),
    )(*args)


def shaped(dtype, *dims):
    return jax.ShapeDtypeStruct(dims, dtype)


VECTORS = pl.BlockSpec(memory_space=pltpu.VMEM)
ANYWHERE = pl.BlockSpec(memory_space=pl.ANY)


def hbm(weight):
    return pltpu.with_memory_space_constraint(weight, pltpu.HBM)


def pack_kernel(tokens, ids, gates, later, out_ref, later_ref, tokens_ref, ids_ref, gates_ref, sems):
    pairs = [(tokens, tokens_ref), (ids, ids_ref), (gates, gates_ref), (later, later_ref)]
    copies = [pltpu.make_async_copy(a, b, sems.at[k]) for k, (a, b) in enumerate(pairs)]
    for copy in copies:
        copy.start()
    for copy in copies:
        copy.wait()
    rows, width = tokens_ref.shape
    out_ref[:, :width] = tokens_ref[...]
    values = gates_ref[...]
    high = values.astype(BF16).astype(F32)
    middle = (values - high).astype(BF16).astype(F32)
    low = values - high - middle
    fields = jnp.concatenate([ids_ref[...].astype(F32), high, middle, low], axis=0)
    fields = jnp.pad(fields, ((0, LANES - fields.shape[0]), (0, LANES - rows)))
    out_ref[:, width:] = jnp.transpose(fields)[:rows].astype(BF16)


def stack_kernel(count, later, *refs):
    parts, out_ref = refs[:count], refs[-1 - later]
    rows = parts[0].shape[0]
    for k, part in enumerate(parts):
        out_ref[k * rows : (k + 1) * rows] = part[...]
    if later:
        refs[-1][...] = refs[count][...]


def stack(parts, after, name, later=()):
    rows, width = parts[0].shape
    outs = call(
        functools.partial(stack_kernel, len(parts), len(later)),
        name,
        [shaped(BF16, rows * len(parts), width)] + [shaped(BF16, *array.shape) for array in later],
        [*parts, *later, *after],
        specs=[VECTORS] * (len(parts) + len(later)) + [ANYWHERE] * len(after),
        limit=16,
    )
    return outs if later else outs[0]


def add_kernel(count, skip, pieces, *refs):
    parts, outs = refs[:count], refs[count + skip : count + skip + pieces]
    total = parts[0][...].astype(F32)
    for part in parts[1:]:
        total = total + part[...].astype(F32)
    total = total.astype(BF16).reshape((pieces,) + outs[0].shape)
    for k, out in enumerate(outs):
        out[...] = total[k]


def add(parts, pieces, after, name, later=()):
    *lead, rows, width = parts[0].shape
    each = math.prod(lead) * rows // pieces
    first = len(parts) + len(after)
    return call(
        functools.partial(add_kernel, len(parts), len(after) + len(later), pieces),
        name,
        [shaped(BF16, each, width)] * pieces + [shaped(BF16, *array.shape) for array in later],
        [*parts, *after, *later],
        specs=[VECTORS] * len(parts) + [ANYWHERE] * (len(after) + len(later)),
        out_specs=[VECTORS] * pieces + [ANYWHERE] * len(later),
        aliases={first + k: pieces + k for k in range(len(later))},
    )


def doubled_along_z(grid, mine, meanwhile):
    column, k, done = mine, 1, None
    while k < grid.nz:
        got = grid.shift(column, dz=k)
        if 2 * k >= grid.nz:
            done = meanwhile(column)
        column = stack([column, got], [] if done is None else [done], "double")
        k *= 2
    return column, meanwhile(column) if done is None else done


def back_over_cores(grid, parts, after, name):
    got = [grid.shift(parts[c], dc=-c) for c in range(1, grid.nc)]
    return add([parts[0], *got], len(grid.square), after, name)


def back_over_plane(grid, kept, after, name, later=()):
    got = [grid.shift(part, dx=-a, dy=-b) for part, (a, b) in zip(kept[1:], grid.square[1:])]
    return add([kept[0], *got], grid.nz, after, name, later)


def back_along_z(grid, total):
    return [total[0]] + [grid.shift(total[k], dz=k) for k in range(1, grid.nz)]


def finish_kernel(count, *refs):
    for n, out in enumerate(refs[-2:]):
        total = refs[n * count][...].astype(F32)
        for part in refs[n * count + 1 : (n + 1) * count]:
            total = total + part[...].astype(F32)
        out[...] = total.astype(BF16)


def finish(first, second, after):
    return call(
        functools.partial(finish_kernel, len(first)),
        "finish",
        [shaped(BF16, *first[0].shape)] * 2,
        [*first, *second, *after],
        specs=[VECTORS] * (2 * len(first)) + [ANYWHERE] * len(after),
    )


def tables(aux, first, rows, local, block):
    tokens = aux.shape[0]
    across = jnp.transpose(aux.astype(F32))
    ids = [across[k : k + 1] for k in range(2)]
    gates = [across[2 + k : 3 + k] + across[4 + k : 5 + k] + across[6 + k : 7 + k] for k in range(2)]
    total = local * rows
    r = lax.broadcasted_iota(jnp.int32, (total, tokens), 0)
    j = lax.broadcasted_iota(jnp.int32, (total, tokens), 1)
    expert = ((r >> log2(rows)) + first).astype(F32)
    own_block = ((r & (rows - 1)) >> log2(CAP)) == (j >> log2(block))
    slot = (r & (CAP - 1)).astype(F32)
    hits = [(ids[k] == expert).astype(F32) for k in range(2)]
    hit = hits[0] + hits[1]
    up = lax.broadcasted_iota(jnp.int32, (tokens, tokens), 0)
    to = lax.broadcasted_iota(jnp.int32, (tokens, tokens), 1)
    earlier = ((up >> log2(block)) == (to >> log2(block))) & (up < to)
    position = dot(hit.astype(BF16), jnp.where(earlier, 1.0, 0.0).astype(BF16))
    select = jnp.where(own_block & (position == slot), hit, 0.0)
    gate = jnp.sum(select * (hits[0] * gates[0] + hits[1] * gates[1]), axis=1, keepdims=True)
    return select, gate


def streamed(weight, held, sems, columns):
    depth = held.shape[0]
    copies = [
        pltpu.make_async_copy(
            weight.at[:, :, pl.ds(start, size)], held.at[k % depth, :, :, pl.ds(0, size)], sems.at[k % depth]
        )
        for k, (start, size) in enumerate(columns)
    ]
    for copy in copies[:depth]:
        copy.start()

    def each():
        for k, copy in enumerate(copies):
            copy.wait()
            size = columns[k][1]
            yield held.at[k % depth, :, :, pl.ds(0, size)]
            if k + depth < len(copies):
                copies[k + depth].start()

    return each()


def kept(weight, held, sems, columns, ready=0, ahead=4):
    copies = []
    for k, (start, size) in enumerate(columns):
        at = (slice(None), slice(None), pl.ds(start, size))
        copies.append(pltpu.make_async_copy(weight.at[at], held.at[at], sems.at[k]))
    for copy in copies[ready : ready + ahead]:
        copy.start()

    def each():
        for k, (start, size) in enumerate(columns):
            if k >= ready:
                copies[k].wait()
            yield held.at[:, :, pl.ds(start, size)]
            if k >= ready and k + ahead < len(copies):
                copies[k + ahead].start()

    return each()


def hold_kernel(s, weight, _, held, sems):
    copies = []
    for k, (start, size) in enumerate(s.columns()[: s.early]):
        at = (slice(None), slice(None), pl.ds(start, size))
        copies.append(pltpu.make_async_copy(weight.at[at], held.at[at], sems.at[k]))
        copies[-1].start()
    for copy in copies:
        copy.wait()


def hold(s, weight, after):
    (held,) = call(
        functools.partial(hold_kernel, s),
        "hold_gate",
        [pltpu.VMEM(weight.shape, BF16)],
        [hbm(weight), after],
        specs=[ANYWHERE] * 2,
        scratch=[pltpu.SemaphoreType.DMA((s.early,))],
        cost=12000,
    )
    return held


class Sizes:
    def __init__(self, grid, tokens, w_gate):
        self.grid = grid
        self.local, self.hidden, self.features = w_gate.shape
        self.block, self.width = tokens.shape
        self.rows = grid.dp * CAP
        self.total = self.local * self.rows
        self.count = grid.dp * self.block
        self.column = grid.nz * self.block
        self.blocks = grid.nc * grid.ny * grid.nx
        self.slices = grid.nc * grid.ny
        whole = self.width % 256 == 0 and self.width > 1024
        self.pieces = [(0, 1024), (1024, self.width - 1024)] if whole else [(0, self.width)]
        self.early = self.slices * len(self.pieces) // 2
        self.parts = [(0, 512), (512, 512), (1024, self.width - 1024)] if whole else [(0, self.width)]

    def columns(self):
        return [(k * self.width + at, size) for k, at, size in self.walk()]

    def walk(self):
        return [(k, at, size) for k in range(self.slices) for at, size in self.pieces]

    def block_of(self, blocks, c, a, b):
        n = self.grid.square.index((a, b)) - 1
        return blocks[2 * c] if n < 0 else blocks[2 * c + 1].at[n * self.column : (n + 1) * self.column]

    def at(self, e):
        return slice(e * self.rows, (e + 1) * self.rows)


def routed(s, blocks, select):
    for k in range(s.slices):
        group = [s.block_of(blocks, k // s.grid.ny, a, k % s.grid.ny)[:, : s.width] for a in range(s.grid.nx)]
        yield k, dot(select, jnp.concatenate(group, axis=0))


def gate_up_kernel(s, *refs):
    blocks, refs = refs[: 2 * s.grid.nc], refs[2 * s.grid.nc :]
    _, wg_ref, wu_ref, _, x_ref, select_ref, back_ref, gate_ref, act_ref, p_ref, q_ref, held_ref = refs[:12]
    room, sems, held_sems = refs[12:]
    walk = s.walk()
    columns = s.columns()
    gates, ups = kept(wg_ref, held_ref, held_sems, columns, s.early), streamed(wu_ref, room, sems, columns)
    aux = jnp.concatenate([s.block_of(blocks, 0, a, 0)[:, s.width :] for a in range(s.grid.nx)], axis=0)
    select, gate = tables(aux, lax.axis_index("hst") * s.local, s.rows, s.local, s.block)
    gate_ref[...] = jnp.broadcast_to(gate, gate_ref.shape)
    select_ref[...] = select.astype(BF16)
    back_ref[...] = jnp.transpose(select).astype(BF16)
    for k, picked in routed(s, blocks, select.astype(BF16)):
        x_ref[s.grid.source(k)] = picked.astype(BF16)
    g, u = [0.0] * s.local, [0.0] * s.local
    for (k, at, size), wg, wu in zip(walk, gates, ups):
        for e in range(s.local):
            x = x_ref[k, s.at(e), at : at + size]
            g[e] += dot_t(x, wg[e])
            u[e] += dot_t(x, wu[e])
    for e in range(s.local):
        sigma = jax.nn.sigmoid(g[e])
        act_ref[e] = (g[e] * sigma * u[e]).astype(BF16)
        p_ref[e] = u[e] * sigma * (1.0 + g[e] * (1.0 - sigma))
        q_ref[e] = g[e] * sigma


def to_tokens(s, k, at, found, back_ref, outs):
    each = s.slices // s.grid.nc
    sums = dot(back_ref[...], jnp.concatenate(found, axis=0)).astype(BF16)
    size = sums.shape[-1]
    outs[k // each][:, k % each, :, at : at + size] = sums.reshape(s.grid.nx, s.column, size)


def relative(s, walk):
    return [(pl.multiple_of(s.grid.source(k) * s.width + at, LANES), size) for k, at, size in walk]


def down_kernel(s, *refs):
    first = 2 * s.grid.nc
    blocks = refs[:first]
    select_ref, gate_ref, back_ref, act_ref, p_ref, q_ref, w_ref = refs[first : first + 7]
    outs, (d_ref, dg_ref, du_ref, room, sems) = refs[first + 7 : -5], refs[-5:]
    walk = s.walk()
    weights = streamed(w_ref, room, sems, relative(s, walk))
    for k, picked in routed(s, blocks, select_ref[...]):
        d_ref[s.grid.source(k)] = (picked * gate_ref[:, :1]).astype(BF16)
    da = [0.0] * s.local
    for (k, at, size), weight in zip(walk, weights):
        found = []
        for e in range(s.local):
            found.append((dot(act_ref[e], weight[e]) * gate_ref[s.at(e), :1]).astype(BF16))
            da[e] += dot_t(d_ref[s.grid.source(k), s.at(e), at : at + size], weight[e])
        to_tokens(s, k, at, found, back_ref, outs)
    for e in range(s.local):
        dg_ref[e] = (da[e] * p_ref[e]).astype(BF16)
        du_ref[e] = (da[e] * q_ref[e]).astype(BF16)


def backward_kernel(s, dg_ref, du_ref, back_ref, held_ref, w_ref, _, *refs):
    outs, (room, sems) = refs[:-2], refs[-2:]
    walk = s.walk()
    columns = relative(s, walk)
    for (k, at, size), (start, _), weight in zip(walk, columns, streamed(w_ref, room, sems, columns)):
        gate = held_ref.at[:, :, pl.ds(start, size)]
        found = [(dot(dg_ref[e], gate[e]) + dot(du_ref[e], weight[e])).astype(BF16) for e in range(s.local)]
        to_tokens(s, k, at, found, back_ref, outs)


def turn(s, left_ref, turned):
    for e in range(s.local):
        turned[e] = jnp.transpose(left_ref[e].astype(F32)).astype(BF16)


class Stores:
    def __init__(self, room, sems):
        self.room, self.sems = room, sems
        self.copies = []

    def slot(self, size):
        return self.room.at[len(self.copies) % self.room.shape[0], :, :, pl.ds(0, size)]

    def next(self, size):
        n = len(self.copies) - self.room.shape[0]
        if n >= 0:
            self.copies[n].wait()
        return self.slot(size)

    def send(self, out, start, size):
        sem = self.sems.at[len(self.copies) % self.room.shape[0]]
        copy = pltpu.make_async_copy(self.slot(size), out.at[:, :, pl.ds(start, size)], sem)
        copy.start()
        self.copies.append(copy)

    def finish(self):
        for copy in self.copies[-self.room.shape[0] :]:
            copy.wait()


def grads_kernel(s, count, *refs):
    lefts, rows_refs = refs[:count], refs[count : 2 * count]
    outs, (marker, turned, store, sems) = refs[2 * count + 1 : -4], refs[-4:]
    marker[...] = jnp.zeros_like(marker)
    stores = Stores(store, sems)
    for left_ref, rows_ref, out in zip(lefts, rows_refs, outs):
        turn(s, left_ref, turned)
        for k in range(s.slices):
            for at, size in s.parts:
                room_for = stores.next(size)
                for e in range(s.local):
                    room_for[e] = dot(turned[e], rows_ref[k, s.at(e), at : at + size]).astype(BF16)
                stores.send(out, k * s.width + at, size)
    stores.finish()


def grads(s, name, lefts, rights, after):
    room = max(size for _, size in s.parts)
    count = len(lefts)
    return call(
        functools.partial(grads_kernel, s, count),
        name,
        [shaped(BF16, s.local, s.hidden, s.features)] * count + [shaped(F32, 8, LANES)],
        [*lefts, *rights, after],
        specs=[VECTORS] * (2 * count) + [ANYWHERE],
        out_specs=[ANYWHERE] * count + [VECTORS],
        scratch=[
            pltpu.VMEM((s.local, s.hidden, s.rows), BF16),
            pltpu.VMEM((4, s.local, s.hidden, room), BF16),
            pltpu.SemaphoreType.DMA((4,)),
        ],
        cost=46000,
    )


def body(tokens, cotangent, expert_ids, gate_values, w_gate, w_up, w_down):
    grid = Grid(lax.axis_size("dp"), lax.axis_size("hst"))
    s = Sizes(grid, tokens, w_gate)

    sources = [tokens, expert_ids.T, gate_values.T, cotangent]
    message, cotangent = call(
        pack_kernel,
        "pack",
        [shaped(BF16, s.block, s.width + LANES), shaped(BF16, s.block, s.width)],
        [hbm(source) for source in sources],
        specs=[ANYWHERE] * 4,
        scratch=[pltpu.VMEM(a.shape, a.dtype) for a in sources[:3]] + [pltpu.SemaphoreType.DMA((4,))],
    )
    x_parts = grid.along_z(message)
    x_column, cotangent = stack(x_parts, [], "stack_tokens", [cotangent])
    x_plane = grid.over_plane(x_column)
    d_column, held_gate = doubled_along_z(grid, cotangent, lambda after: hold(s, w_gate, after))
    x_others = stack([x_plane[at] for at in grid.square[1:]], [d_column], "stack_tokens_plane")
    x_blocks = grid.over_cores(x_column, x_others)
    d_column = stack([d_column], [x_others], "stack_cotangents")
    d_plane = grid.over_plane(d_column)
    room = max(size for _, size in s.pieces)
    streams = [pltpu.VMEM((3, s.local, s.hidden, room), BF16), pltpu.SemaphoreType.DMA((3,))]

    hidden_shape = (s.local, s.rows, s.hidden)
    rows_shape = shaped(BF16, s.slices, s.total, s.width)
    x_rows, select, back, gate, act, p, q, held_gate = call(
        functools.partial(gate_up_kernel, s),
        "gate_up",
        [
            rows_shape,
            shaped(BF16, s.total, s.count),
            shaped(BF16, s.count, s.total),
            shaped(F32, s.total, LANES),
            shaped(BF16, *hidden_shape),
            shaped(F32, *hidden_shape),
            shaped(F32, *hidden_shape),
            pltpu.VMEM(w_gate.shape, BF16),
        ],
        [*x_blocks, held_gate, hbm(w_gate), hbm(w_up), d_column],
        specs=[VECTORS] * (len(x_blocks) + 1) + [ANYWHERE] * 3,
        aliases={len(x_blocks): 7},
        scratch=[*streams, pltpu.SemaphoreType.DMA((len(s.walk()),))],
        cost=46000,
    )
    d_others = stack([d_plane[at] for at in grid.square[1:]], [gate], "stack_cotangents_plane")
    d_blocks = grid.over_cores(d_column, d_others)
    sums = shaped(BF16, grid.nx, grid.ny, s.column, s.width)
    *out_parts, d_rows, d_gate, d_up = call(
        functools.partial(down_kernel, s),
        "down",
        [sums] * grid.nc + [rows_shape, shaped(BF16, *hidden_shape), shaped(BF16, *hidden_shape)],
        [*d_blocks, select, gate, back, act, p, q, hbm(w_down)],
        specs=[VECTORS] * (len(d_blocks) + 6) + [ANYWHERE],
        scratch=streams,
        cost=46000,
    )
    mixed_kept = back_over_cores(grid, out_parts, [], "mixed_cores")
    back_parts = call(
        functools.partial(backward_kernel, s),
        "backward",
        [sums] * grid.nc,
        [d_gate, d_up, back, held_gate, hbm(w_up), mixed_kept[0]],
        specs=[VECTORS] * 4 + [ANYWHERE] * 2,
        scratch=streams,
        cost=46000,
    )
    *mixed_total, last = back_over_plane(grid, mixed_kept, back_parts[:1], "mixed_plane", back_parts[-1:])
    token_kept = back_over_cores(grid, [*back_parts[:-1], last], [], "tokens_cores")
    grad_gate, grad_down, done = grads(s, "grad_gate_down", [d_gate, act], [x_rows, d_rows], token_kept[0])
    token_total = back_over_plane(grid, token_kept, [done], "tokens_plane")
    grad_up, done = grads(s, "grad_up", [d_up], [x_rows], token_total[0])
    mixed, grad_tokens = finish(back_along_z(grid, mixed_total), back_along_z(grid, token_total), [done])
    return mixed, grad_tokens, grad_gate, grad_up, grad_down


def solution(mesh):
    return jax.shard_map(
        body,
        mesh=mesh,
        in_specs=(
            P("dp", "hst"),
            P("dp", "hst"),
            P("dp", None),
            P("dp", None),
            P("hst", "dp", None),
            P("hst", "dp", None),
            P("hst", "dp", None),
        ),
        out_specs=(
            P("dp", "hst"),
            P("dp", "hst"),
            P("hst", "dp", None),
            P("hst", "dp", None),
            P("hst", "dp", None),
        ),
        check_vma=False,
    )
```

```python
import functools
import math

import jax
import jax.numpy as jnp
from jax import lax
from jax.experimental import pallas as pl
from jax.experimental.pallas import tpu as pltpu
from jax.sharding import PartitionSpec as P

CAP = 4
LANES = 128
MIB = 1 << 20
MFLOP = 10**6
F32 = jnp.float32
BF16 = jnp.bfloat16
AXES = ("dp", "hst")


def dot(a, b):
    return lax.dot_general(a, b, (((1,), (0,)), ((), ())), preferred_element_type=F32)


def dot_t(a, b):
    return lax.dot_general(a, b, (((1,), (1,)), ((), ())), preferred_element_type=F32)


def log2(n):
    assert n & (n - 1) == 0
    return n.bit_length() - 1


class Grid:
    def __init__(self, dp, hst):
        self.dp, self.hst = dp, hst
        self.nc = 2 if hst % 2 == 0 else 1
        self.ny = hst // self.nc
        self.nx = self.ny if dp % self.ny == 0 else 1
        self.nz = dp // self.nx
        assert self.nz & (self.nz - 1) == 0
        self.square = [(a, b) for a in range(self.nx) for b in range(self.ny)]

    def shift(self, value, dz=0, dx=0, dy=0, dc=0):
        pairs = []
        for z in range(self.nz):
            for x in range(self.nx):
                for y in range(self.ny):
                    for c in range(self.nc):
                        to_dp = (z ^ dz) * self.nx + (x + dx) % self.nx
                        to_hst = (y + dy) % self.ny * self.nc + (c + dc) % self.nc
                        here = (z * self.nx + x) * self.hst + y * self.nc + c
                        pairs.append((here, to_dp * self.hst + to_hst))
        return lax.ppermute(value, AXES, pairs)

    def along_z(self, mine):
        return [mine] + [self.shift(mine, dz=k) for k in range(1, self.nz)]

    def over_plane(self, column):
        return {(a, b): self.shift(column, dx=a, dy=b) if a or b else column for a, b in self.square}

    def over_cores(self, column, others):
        blocks = [column, others]
        for c in range(1, self.nc):
            blocks += [self.shift(column, dc=c), self.shift(others, dc=c)]
        return blocks

    def source(self, k):
        host = lax.axis_index("hst")
        y, core = host >> log2(self.nc), host & (self.nc - 1)
        from_y = (y - (k & (self.ny - 1))) & (self.ny - 1)
        return (from_y << log2(self.nc)) + ((core + (k >> log2(self.ny))) & (self.nc - 1))


def call(kernel, name, outs, args, specs=None, out_specs=None, scratch=(), grid=(), limit=16, cost=0, aliases=None):
    specs = specs or [pl.BlockSpec(memory_space=pltpu.VMEM)] * len(args)
    out_specs = out_specs or [pl.BlockSpec(memory_space=pltpu.VMEM)] * len(outs)
    return pl.pallas_call(
        kernel,
        name=name,
        grid=grid,
        out_shape=outs,
        in_specs=specs,
        out_specs=out_specs,
        scratch_shapes=list(scratch),
        input_output_aliases=aliases or {},
        compiler_params=pltpu.CompilerParams(vmem_limit_bytes=limit * MIB),
        cost_estimate=pl.CostEstimate(flops=cost * MFLOP, bytes_accessed=0, transcendentals=0),
    )(*args)


def shaped(dtype, *dims):
    return jax.ShapeDtypeStruct(dims, dtype)


VECTORS = pl.BlockSpec(memory_space=pltpu.VMEM)
ANYWHERE = pl.BlockSpec(memory_space=pl.ANY)


def hbm(weight):
    return pltpu.with_memory_space_constraint(weight, pltpu.HBM)


def pack_kernel(tokens, ids, gates, later, out_ref, later_ref, tokens_ref, ids_ref, gates_ref, sems):
    pairs = [(tokens, tokens_ref), (ids, ids_ref), (gates, gates_ref), (later, later_ref)]
    copies = [pltpu.make_async_copy(a, b, sems.at[k]) for k, (a, b) in enumerate(pairs)]
    for copy in copies:
        copy.start()
    for copy in copies:
        copy.wait()
    rows, width = tokens_ref.shape
    out_ref[:, :width] = tokens_ref[...]
    values = gates_ref[...]
    high = values.astype(BF16).astype(F32)
    middle = (values - high).astype(BF16).astype(F32)
    low = values - high - middle
    fields = jnp.concatenate([ids_ref[...].astype(F32), high, middle, low], axis=0)
    fields = jnp.pad(fields, ((0, LANES - fields.shape[0]), (0, LANES - rows)))
    out_ref[:, width:] = jnp.transpose(fields)[:rows].astype(BF16)


def stack_kernel(count, later, *refs):
    parts, out_ref = refs[:count], refs[-1 - later]
    rows = parts[0].shape[0]
    for k, part in enumerate(parts):
        out_ref[k * rows : (k + 1) * rows] = part[...]
    if later:
        refs[-1][...] = refs[count][...]


def stack(parts, after, name, later=()):
    rows, width = parts[0].shape
    outs = call(
        functools.partial(stack_kernel, len(parts), len(later)),
        name,
        [shaped(BF16, rows * len(parts), width)] + [shaped(BF16, *array.shape) for array in later],
        [*parts, *later, *after],
        specs=[VECTORS] * (len(parts) + len(later)) + [ANYWHERE] * len(after),
        limit=16,
    )
    return outs if later else outs[0]


def add_kernel(count, skip, pieces, *refs):
    parts, outs = refs[:count], refs[count + skip : count + skip + pieces]
    total = parts[0][...].astype(F32)
    for part in parts[1:]:
        total = total + part[...].astype(F32)
    total = total.astype(BF16).reshape((pieces,) + outs[0].shape)
    for k, out in enumerate(outs):
        out[...] = total[k]


def add(parts, pieces, after, name, later=()):
    *lead, rows, width = parts[0].shape
    each = math.prod(lead) * rows // pieces
    first = len(parts) + len(after)
    return call(
        functools.partial(add_kernel, len(parts), len(after) + len(later), pieces),
        name,
        [shaped(BF16, each, width)] * pieces + [shaped(BF16, *array.shape) for array in later],
        [*parts, *after, *later],
        specs=[VECTORS] * len(parts) + [ANYWHERE] * (len(after) + len(later)),
        out_specs=[VECTORS] * pieces + [ANYWHERE] * len(later),
        aliases={first + k: pieces + k for k in range(len(later))},
    )


def doubled_along_z(grid, mine, meanwhile):
    column, k, done = mine, 1, None
    while k < grid.nz:
        got = grid.shift(column, dz=k)
        if 2 * k >= grid.nz:
            done = meanwhile(column)
        column = stack([column, got], [] if done is None else [done], "double")
        k *= 2
    return column, meanwhile(column) if done is None else done


def back_over_cores(grid, parts, after, name):
    got = [grid.shift(parts[c], dc=-c) for c in range(1, grid.nc)]
    return add([parts[0], *got], len(grid.square), after, name)


def back_over_plane(grid, kept, after, name, later=()):
    got = [grid.shift(part, dx=-a, dy=-b) for part, (a, b) in zip(kept[1:], grid.square[1:])]
    return add([kept[0], *got], grid.nz, after, name, later)


def back_along_z(grid, total):
    return [total[0]] + [grid.shift(total[k], dz=k) for k in range(1, grid.nz)]


def finish_kernel(count, *refs):
    for n, out in enumerate(refs[-2:]):
        total = refs[n * count][...].astype(F32)
        for part in refs[n * count + 1 : (n + 1) * count]:
            total = total + part[...].astype(F32)
        out[...] = total.astype(BF16)


def finish(first, second, after):
    return call(
        functools.partial(finish_kernel, len(first)),
        "finish",
        [shaped(BF16, *first[0].shape)] * 2,
        [*first, *second, *after],
        specs=[VECTORS] * (2 * len(first)) + [ANYWHERE] * len(after),
    )


def tables(aux, first, rows, local, block):
    tokens = aux.shape[0]
    across = jnp.transpose(aux.astype(F32))
    ids = [across[k : k + 1] for k in range(2)]
    gates = [across[2 + k : 3 + k] + across[4 + k : 5 + k] + across[6 + k : 7 + k] for k in range(2)]
    total = local * rows
    r = lax.broadcasted_iota(jnp.int32, (total, tokens), 0)
    j = lax.broadcasted_iota(jnp.int32, (total, tokens), 1)
    expert = ((r >> log2(rows)) + first).astype(F32)
    own_block = ((r & (rows - 1)) >> log2(CAP)) == (j >> log2(block))
    slot = (r & (CAP - 1)).astype(F32)
    hits = [(ids[k] == expert).astype(F32) for k in range(2)]
    hit = hits[0] + hits[1]
    up = lax.broadcasted_iota(jnp.int32, (tokens, tokens), 0)
    to = lax.broadcasted_iota(jnp.int32, (tokens, tokens), 1)
    earlier = ((up >> log2(block)) == (to >> log2(block))) & (up < to)
    position = dot(hit.astype(BF16), jnp.where(earlier, 1.0, 0.0).astype(BF16))
    select = jnp.where(own_block & (position == slot), hit, 0.0)
    gate = jnp.sum(select * (hits[0] * gates[0] + hits[1] * gates[1]), axis=1, keepdims=True)
    return select, gate


class Stream:
    def __init__(self, s, weight, room, sems, place):
        self.s, self.weight, self.room, self.sems, self.place = s, weight, room, sems, place
        for k in range(min(2, s.slices)):
            for p in range(len(s.pieces)):
                self.copy(k, p).start()

    def slot(self, k, p):
        return lax.rem(k, 2) * len(self.s.pieces) + p

    def copy(self, k, p):
        at, size = self.s.pieces[p]
        start = pl.multiple_of(self.place(k) * self.s.width + at, LANES)
        slot = self.slot(k, p)
        return pltpu.make_async_copy(
            self.weight.at[:, :, pl.ds(start, size)], self.room.at[slot, :, :, pl.ds(0, size)], self.sems.at[slot]
        )

    def get(self, k, p):
        self.copy(k, p).wait()
        return self.room.at[self.slot(k, p), :, :, pl.ds(0, self.s.pieces[p][1])]

    def free(self, k, p):
        @pl.when(k + 2 < self.s.slices)
        def _():
            self.copy(k + 2, p).start()


def held_copy(s, weight, held, sems, k, p):
    at, size = s.pieces[p]
    columns = (slice(None), slice(None), pl.ds(pl.multiple_of(k * s.width + at, LANES), size))
    return pltpu.make_async_copy(weight.at[columns], held.at[columns], sems.at[k * len(s.pieces) + p])


def hold_kernel(s, weight, _, held, sems):
    copies = [held_copy(s, weight, held, sems, k, p) for k in range(s.early) for p in range(len(s.pieces))]
    for copy in copies:
        copy.start()
    for copy in copies:
        copy.wait()


def hold(s, weight, after):
    (held,) = call(
        functools.partial(hold_kernel, s),
        "hold_gate",
        [pltpu.VMEM(weight.shape, BF16)],
        [hbm(weight), after],
        specs=[ANYWHERE] * 2,
        scratch=[pltpu.SemaphoreType.DMA((s.early * len(s.pieces),))],
        cost=12000,
    )
    return held


class Sizes:
    def __init__(self, grid, tokens, w_gate):
        self.grid = grid
        self.local, self.hidden, self.features = w_gate.shape
        self.block, self.width = tokens.shape
        self.rows = grid.dp * CAP
        self.total = self.local * self.rows
        self.count = grid.dp * self.block
        self.column = grid.nz * self.block
        self.blocks = grid.nc * grid.ny * grid.nx
        self.slices = grid.nc * grid.ny
        whole = self.width % 256 == 0 and self.width > 1024
        self.pieces = [(0, 1024), (1024, self.width - 1024)] if whole else [(0, self.width)]
        self.early = self.slices // 2

    def block_of(self, blocks, c, a, b):
        n = self.grid.square.index((a, b)) - 1
        return blocks[2 * c] if n < 0 else blocks[2 * c + 1].at[n * self.column : (n + 1) * self.column]

    def at(self, e):
        return slice(e * self.rows, (e + 1) * self.rows)


def routed(s, blocks, select):
    for k in range(s.slices):
        group = [s.block_of(blocks, k // s.grid.ny, a, k % s.grid.ny)[:, : s.width] for a in range(s.grid.nx)]
        yield k, dot(select, jnp.concatenate(group, axis=0))


def gate_up_kernel(s, *refs):
    blocks, refs = refs[: 2 * s.grid.nc], refs[2 * s.grid.nc :]
    _, wg_ref, wu_ref, _, x_ref, select_ref, back_ref, gate_ref, act_ref, p_ref, q_ref, held_ref = refs[:12]
    room, sems, held_sems, g_acc, u_acc = refs[12:]
    ups = Stream(s, wu_ref, room, sems, lambda k: k)
    for k in range(s.early, min(2, s.slices)):
        for p in range(len(s.pieces)):
            held_copy(s, wg_ref, held_ref, held_sems, k, p).start()
    aux = jnp.concatenate([s.block_of(blocks, 0, a, 0)[:, s.width :] for a in range(s.grid.nx)], axis=0)
    select, gate = tables(aux, lax.axis_index("hst") * s.local, s.rows, s.local, s.block)
    gate_ref[...] = jnp.broadcast_to(gate, gate_ref.shape)
    select_ref[...] = select.astype(BF16)
    back_ref[...] = jnp.transpose(select).astype(BF16)
    for k, picked in routed(s, blocks, select.astype(BF16)):
        x_ref[s.grid.source(k)] = picked.astype(BF16)
    g_acc[...] = jnp.zeros_like(g_acc)
    u_acc[...] = jnp.zeros_like(u_acc)

    def step(k, _):
        for p, (at, size) in enumerate(s.pieces):

            @pl.when((k + 2 >= s.early) & (k + 2 < s.slices))
            def _():
                held_copy(s, wg_ref, held_ref, held_sems, k + 2, p).start()

            @pl.when(k >= s.early)
            def _():
                held_copy(s, wg_ref, held_ref, held_sems, k, p).wait()

            up = ups.get(k, p)
            gate = held_ref.at[:, :, pl.ds(pl.multiple_of(k * s.width + at, LANES), size)]
            for e in range(s.local):
                x = x_ref[k, s.at(e), at : at + size]
                g_acc[e] += dot_t(x, gate[e])
                u_acc[e] += dot_t(x, up[e])
            ups.free(k, p)
        return 0

    lax.fori_loop(0, s.slices, step, 0)
    for e in range(s.local):
        g, u = g_acc[e], u_acc[e]
        sigma = jax.nn.sigmoid(g)
        act_ref[e] = (g * sigma * u).astype(BF16)
        p_ref[e] = u * sigma * (1.0 + g * (1.0 - sigma))
        q_ref[e] = g * sigma


def to_tokens(s, k, at, found, back_ref, outs):
    sums = dot(back_ref[...], jnp.concatenate(found, axis=0)).astype(BF16)
    size = sums.shape[-1]
    sums = sums.reshape(s.grid.nx, s.column, size)
    for c, out in enumerate(outs):

        @pl.when(k >> log2(s.grid.ny) == c)
        def _():
            out[:, k & (s.grid.ny - 1), :, at : at + size] = sums


def down_kernel(s, *refs):
    first = 2 * s.grid.nc
    blocks = refs[:first]
    select_ref, gate_ref, back_ref, act_ref, p_ref, q_ref, w_ref = refs[first : first + 7]
    outs, (d_ref, dg_ref, du_ref, room, sems, acc) = refs[first + 7 : -6], refs[-6:]
    weights = Stream(s, w_ref, room, sems, s.grid.source)
    for k, picked in routed(s, blocks, select_ref[...]):
        d_ref[s.grid.source(k)] = (picked * gate_ref[:, :1]).astype(BF16)
    acc[...] = jnp.zeros_like(acc)

    def step(k, _):
        for p, (at, size) in enumerate(s.pieces):
            weight = weights.get(k, p)
            found = []
            for e in range(s.local):
                found.append((dot(act_ref[e], weight[e]) * gate_ref[s.at(e), :1]).astype(BF16))
                acc[e] += dot_t(d_ref[s.grid.source(k), s.at(e), at : at + size], weight[e])
            to_tokens(s, k, at, found, back_ref, outs)
            weights.free(k, p)
        return 0

    lax.fori_loop(0, s.slices, step, 0)
    for e in range(s.local):
        dg_ref[e] = (acc[e] * p_ref[e]).astype(BF16)
        du_ref[e] = (acc[e] * q_ref[e]).astype(BF16)


def backward_kernel(s, dg_ref, du_ref, back_ref, held_ref, w_ref, _, *refs):
    outs, (room, sems) = refs[:-2], refs[-2:]
    weights = Stream(s, w_ref, room, sems, s.grid.source)

    def step(k, _):
        for p, (at, size) in enumerate(s.pieces):
            gate = held_ref.at[:, :, pl.ds(pl.multiple_of(s.grid.source(k) * s.width + at, LANES), size)]
            up = weights.get(k, p)
            found = [(dot(dg_ref[e], gate[e]) + dot(du_ref[e], up[e])).astype(BF16) for e in range(s.local)]
            to_tokens(s, k, at, found, back_ref, outs)
            weights.free(k, p)
        return 0

    lax.fori_loop(0, s.slices, step, 0)


def turn(s, left_ref, turned):
    for e in range(s.local):
        turned[e] = jnp.transpose(left_ref[e].astype(F32)).astype(BF16)


def grads_kernel(s, count, *refs):
    lefts, rows_refs = refs[:count], refs[count : 2 * count]
    outs, (marker, turned, store, sems) = refs[2 * count + 1 : -4], refs[-4:]
    marker[...] = jnp.zeros_like(marker)
    pieces = len(s.pieces)

    def copy(out, k, p):
        at, size = s.pieces[p]
        slot = lax.rem(k, 2) * pieces + p
        start = pl.multiple_of(k * s.width + at, LANES)
        return pltpu.make_async_copy(
            store.at[slot, :, :, pl.ds(0, size)], out.at[:, :, pl.ds(start, size)], sems.at[slot]
        )

    for left_ref, rows_ref, out in zip(lefts, rows_refs, outs):
        turn(s, left_ref, turned)

        def step(k, _):
            for p, (at, size) in enumerate(s.pieces):

                @pl.when(k >= 2)
                def _():
                    copy(out, k - 2, p).wait()

                for e in range(s.local):
                    rows = rows_ref[k, s.at(e), at : at + size]
                    store[lax.rem(k, 2) * pieces + p, e, :, :size] = dot(turned[e], rows).astype(BF16)
                copy(out, k, p).start()
            return 0

        lax.fori_loop(0, s.slices, step, 0)
        for k in range(max(0, s.slices - 2), s.slices):
            for p in range(pieces):
                copy(out, k, p).wait()


def grads(s, name, lefts, rights, after):
    room = max(size for _, size in s.pieces)
    count = len(lefts)
    slots = 2 * len(s.pieces)
    return call(
        functools.partial(grads_kernel, s, count),
        name,
        [shaped(BF16, s.local, s.hidden, s.features)] * count + [shaped(F32, 8, LANES)],
        [*lefts, *rights, after],
        specs=[VECTORS] * (2 * count) + [ANYWHERE],
        out_specs=[ANYWHERE] * count + [VECTORS],
        scratch=[
            pltpu.VMEM((s.local, s.hidden, s.rows), BF16),
            pltpu.VMEM((slots, s.local, s.hidden, room), BF16),
            pltpu.SemaphoreType.DMA((slots,)),
        ],
        cost=46000,
    )


def body(tokens, cotangent, expert_ids, gate_values, w_gate, w_up, w_down):
    grid = Grid(lax.axis_size("dp"), lax.axis_size("hst"))
    s = Sizes(grid, tokens, w_gate)

    sources = [tokens, expert_ids.T, gate_values.T, cotangent]
    message, cotangent = call(
        pack_kernel,
        "pack",
        [shaped(BF16, s.block, s.width + LANES), shaped(BF16, s.block, s.width)],
        [hbm(source) for source in sources],
        specs=[ANYWHERE] * 4,
        scratch=[pltpu.VMEM(a.shape, a.dtype) for a in sources[:3]] + [pltpu.SemaphoreType.DMA((4,))],
    )
    x_parts = grid.along_z(message)
    x_column, cotangent = stack(x_parts, [], "stack_tokens", [cotangent])
    x_plane = grid.over_plane(x_column)
    d_column, held_gate = doubled_along_z(grid, cotangent, lambda after: hold(s, w_gate, after))
    x_others = stack([x_plane[at] for at in grid.square[1:]], [d_column], "stack_tokens_plane")
    x_blocks = grid.over_cores(x_column, x_others)
    d_column = stack([d_column], [x_others], "stack_cotangents")
    d_plane = grid.over_plane(d_column)
    room = max(size for _, size in s.pieces)
    slots = 2 * len(s.pieces)
    streams = [pltpu.VMEM((slots, s.local, s.hidden, room), BF16), pltpu.SemaphoreType.DMA((slots,))]

    hidden_shape = (s.local, s.rows, s.hidden)
    sums_room = pltpu.VMEM(hidden_shape, F32)
    rows_shape = shaped(BF16, s.slices, s.total, s.width)
    x_rows, select, back, gate, act, p, q, held_gate = call(
        functools.partial(gate_up_kernel, s),
        "gate_up",
        [
            rows_shape,
            shaped(BF16, s.total, s.count),
            shaped(BF16, s.count, s.total),
            shaped(F32, s.total, LANES),
            shaped(BF16, *hidden_shape),
            shaped(F32, *hidden_shape),
            shaped(F32, *hidden_shape),
            pltpu.VMEM(w_gate.shape, BF16),
        ],
        [*x_blocks, held_gate, hbm(w_gate), hbm(w_up), d_column],
        specs=[VECTORS] * (len(x_blocks) + 1) + [ANYWHERE] * 3,
        aliases={len(x_blocks): 7},
        scratch=[*streams, pltpu.SemaphoreType.DMA((s.slices * len(s.pieces),)), sums_room, sums_room],
        cost=46000,
    )
    d_others = stack([d_plane[at] for at in grid.square[1:]], [gate], "stack_cotangents_plane")
    d_blocks = grid.over_cores(d_column, d_others)
    sums = shaped(BF16, grid.nx, grid.ny, s.column, s.width)
    *out_parts, d_rows, d_gate, d_up = call(
        functools.partial(down_kernel, s),
        "down",
        [sums] * grid.nc + [rows_shape, shaped(BF16, *hidden_shape), shaped(BF16, *hidden_shape)],
        [*d_blocks, select, gate, back, act, p, q, hbm(w_down)],
        specs=[VECTORS] * (len(d_blocks) + 6) + [ANYWHERE],
        scratch=[*streams, sums_room],
        cost=46000,
    )
    mixed_kept = back_over_cores(grid, out_parts, [], "mixed_cores")
    back_parts = call(
        functools.partial(backward_kernel, s),
        "backward",
        [sums] * grid.nc,
        [d_gate, d_up, back, held_gate, hbm(w_up), mixed_kept[0]],
        specs=[VECTORS] * 4 + [ANYWHERE] * 2,
        scratch=streams,
        cost=46000,
    )
    *mixed_total, last = back_over_plane(grid, mixed_kept, back_parts[:1], "mixed_plane", back_parts[-1:])
    token_kept = back_over_cores(grid, [*back_parts[:-1], last], [], "tokens_cores")
    grad_gate, grad_down, done = grads(s, "grad_gate_down", [d_gate, act], [x_rows, d_rows], token_kept[0])
    token_total = back_over_plane(grid, token_kept, [done], "tokens_plane")
    grad_up, done = grads(s, "grad_up", [d_up], [x_rows], token_total[0])
    mixed, grad_tokens = finish(back_along_z(grid, mixed_total), back_along_z(grid, token_total), [done])
    return mixed, grad_tokens, grad_gate, grad_up, grad_down


def solution(mesh):
    return jax.shard_map(
        body,
        mesh=mesh,
        in_specs=(
            P("dp", "hst"),
            P("dp", "hst"),
            P("dp", None),
            P("dp", None),
            P("hst", "dp", None),
            P("hst", "dp", None),
            P("hst", "dp", None),
        ),
        out_specs=(
            P("dp", "hst"),
            P("dp", "hst"),
            P("hst", "dp", None),
            P("hst", "dp", None),
            P("hst", "dp", None),
        ),
        check_vma=False,
    )
```

```python
import functools
import math

import jax
import jax.numpy as jnp
from jax import lax
from jax.experimental import pallas as pl
from jax.experimental.pallas import tpu as pltpu
from jax.sharding import PartitionSpec as P

CAP = 4
LANES = 128
MIB = 1 << 20
MFLOP = 10**6
EARLY = 2
F32 = jnp.float32
BF16 = jnp.bfloat16
AXES = ("dp", "hst")


def dot(a, b):
    return lax.dot_general(a, b, (((1,), (0,)), ((), ())), preferred_element_type=F32)


def dot_t(a, b):
    return lax.dot_general(a, b, (((1,), (1,)), ((), ())), preferred_element_type=F32)


def log2(n):
    assert n & (n - 1) == 0
    return n.bit_length() - 1


class Grid:
    def __init__(self, dp, hst):
        self.dp, self.hst = dp, hst
        self.nc = 2 if hst % 2 == 0 else 1
        self.ny = hst // self.nc
        self.nx = self.ny if dp % self.ny == 0 else 1
        self.nz = dp // self.nx
        assert self.nz & (self.nz - 1) == 0
        self.square = [(a, b) for a in range(self.nx) for b in range(self.ny)]

    def shift(self, value, dz=0, dx=0, dy=0, dc=0):
        pairs = []
        for z in range(self.nz):
            for x in range(self.nx):
                for y in range(self.ny):
                    for c in range(self.nc):
                        to_dp = (z ^ dz) * self.nx + (x + dx) % self.nx
                        to_hst = (y + dy) % self.ny * self.nc + (c + dc) % self.nc
                        here = (z * self.nx + x) * self.hst + y * self.nc + c
                        pairs.append((here, to_dp * self.hst + to_hst))
        return lax.ppermute(value, AXES, pairs)

    def along_z(self, mine):
        return [mine] + [self.shift(mine, dz=k) for k in range(1, self.nz)]

    def over_plane(self, column):
        return {(a, b): self.shift(column, dx=a, dy=b) if a or b else column for a, b in self.square}

    def over_cores(self, column, others):
        blocks = [column, others]
        for c in range(1, self.nc):
            blocks += [self.shift(column, dc=c), self.shift(others, dc=c)]
        return blocks

    def source(self, k):
        host = lax.axis_index("hst")
        y, core = host >> log2(self.nc), host & (self.nc - 1)
        from_y = (y - (k & (self.ny - 1))) & (self.ny - 1)
        return (from_y << log2(self.nc)) + ((core + (k >> log2(self.ny))) & (self.nc - 1))


def call(kernel, name, outs, args, specs=None, out_specs=None, scratch=(), grid=(), limit=16, cost=0, aliases=None):
    specs = specs or [pl.BlockSpec(memory_space=pltpu.VMEM)] * len(args)
    out_specs = out_specs or [pl.BlockSpec(memory_space=pltpu.VMEM)] * len(outs)
    return pl.pallas_call(
        kernel,
        name=name,
        grid=grid,
        out_shape=outs,
        in_specs=specs,
        out_specs=out_specs,
        scratch_shapes=list(scratch),
        input_output_aliases=aliases or {},
        compiler_params=pltpu.CompilerParams(vmem_limit_bytes=limit * MIB),
        cost_estimate=pl.CostEstimate(flops=cost * MFLOP, bytes_accessed=0, transcendentals=0),
    )(*args)


def shaped(dtype, *dims):
    return jax.ShapeDtypeStruct(dims, dtype)


VECTORS = pl.BlockSpec(memory_space=pltpu.VMEM)
ANYWHERE = pl.BlockSpec(memory_space=pl.ANY)


def hbm(weight):
    return pltpu.with_memory_space_constraint(weight, pltpu.HBM)


def pack_kernel(tokens, ids, gates, later, out_ref, later_ref, tokens_ref, ids_ref, gates_ref, sems):
    pairs = [(tokens, tokens_ref), (ids, ids_ref), (gates, gates_ref), (later, later_ref)]
    copies = [pltpu.make_async_copy(a, b, sems.at[k]) for k, (a, b) in enumerate(pairs)]
    for copy in copies:
        copy.start()
    for copy in copies:
        copy.wait()
    rows, width = tokens_ref.shape
    out_ref[:, :width] = tokens_ref[...]
    values = gates_ref[...]
    high = values.astype(BF16).astype(F32)
    middle = (values - high).astype(BF16).astype(F32)
    low = values - high - middle
    fields = jnp.concatenate([ids_ref[...].astype(F32), high, middle, low], axis=0)
    fields = jnp.pad(fields, ((0, LANES - fields.shape[0]), (0, LANES - rows)))
    out_ref[:, width:] = jnp.transpose(fields)[:rows].astype(BF16)


def stack_kernel(count, later, *refs):
    parts, out_ref = refs[:count], refs[-1 - later]
    rows = parts[0].shape[0]
    for k, part in enumerate(parts):
        out_ref[k * rows : (k + 1) * rows] = part[...]
    if later:
        refs[-1][...] = refs[count][...]


def stack(parts, after, name, later=()):
    rows, width = parts[0].shape
    outs = call(
        functools.partial(stack_kernel, len(parts), len(later)),
        name,
        [shaped(BF16, rows * len(parts), width)] + [shaped(BF16, *array.shape) for array in later],
        [*parts, *later, *after],
        specs=[VECTORS] * (len(parts) + len(later)) + [ANYWHERE] * len(after),
        limit=16,
    )
    return outs if later else outs[0]


def add_kernel(count, skip, pieces, *refs):
    parts, outs = refs[:count], refs[count + skip : count + skip + pieces]
    total = parts[0][...].astype(F32)
    for part in parts[1:]:
        total = total + part[...].astype(F32)
    total = total.astype(BF16).reshape((pieces,) + outs[0].shape)
    for k, out in enumerate(outs):
        out[...] = total[k]


def add(parts, pieces, after, name, later=()):
    *lead, rows, width = parts[0].shape
    each = math.prod(lead) * rows // pieces
    first = len(parts) + len(after)
    return call(
        functools.partial(add_kernel, len(parts), len(after) + len(later), pieces),
        name,
        [shaped(BF16, each, width)] * pieces + [shaped(BF16, *array.shape) for array in later],
        [*parts, *after, *later],
        specs=[VECTORS] * len(parts) + [ANYWHERE] * (len(after) + len(later)),
        out_specs=[VECTORS] * pieces + [ANYWHERE] * len(later),
        aliases={first + k: pieces + k for k in range(len(later))},
    )


def doubled_along_z(grid, mine, meanwhile):
    column, k, done = mine, 1, None
    while k < grid.nz:
        got = grid.shift(column, dz=k)
        if 2 * k >= grid.nz:
            done = meanwhile(column)
        column = stack([column, got], [] if done is None else [done], "double")
        k *= 2
    return column, meanwhile(column) if done is None else done


def back_over_cores(grid, parts, after, name):
    got = [grid.shift(parts[c], dc=-c) for c in range(1, grid.nc)]
    return add([parts[0], *got], len(grid.square), after, name)


def back_over_plane(grid, kept, after, name, later=()):
    got = [grid.shift(part, dx=-a, dy=-b) for part, (a, b) in zip(kept[1:], grid.square[1:])]
    return add([kept[0], *got], grid.nz, after, name, later)


def back_along_z(grid, total):
    return [total[0]] + [grid.shift(total[k], dz=k) for k in range(1, grid.nz)]


def finish_kernel(count, *refs):
    for n, out in enumerate(refs[-2:]):
        total = refs[n * count][...].astype(F32)
        for part in refs[n * count + 1 : (n + 1) * count]:
            total = total + part[...].astype(F32)
        out[...] = total.astype(BF16)


def finish(first, second, after):
    return call(
        functools.partial(finish_kernel, len(first)),
        "finish",
        [shaped(BF16, *first[0].shape)] * 2,
        [*first, *second, *after],
        specs=[VECTORS] * (2 * len(first)) + [ANYWHERE] * len(after),
    )


def tables(aux, first, rows, local, block):
    tokens = aux.shape[0]
    across = jnp.transpose(aux.astype(F32))
    ids = [across[k : k + 1] for k in range(2)]
    gates = [across[2 + k : 3 + k] + across[4 + k : 5 + k] + across[6 + k : 7 + k] for k in range(2)]
    total = local * rows
    r = lax.broadcasted_iota(jnp.int32, (total, tokens), 0)
    j = lax.broadcasted_iota(jnp.int32, (total, tokens), 1)
    expert = ((r >> log2(rows)) + first).astype(F32)
    own_block = ((r & (rows - 1)) >> log2(CAP)) == (j >> log2(block))
    slot = (r & (CAP - 1)).astype(F32)
    hits = [(ids[k] == expert).astype(F32) for k in range(2)]
    hit = hits[0] + hits[1]
    up = lax.broadcasted_iota(jnp.int32, (tokens, tokens), 0)
    to = lax.broadcasted_iota(jnp.int32, (tokens, tokens), 1)
    earlier = ((up >> log2(block)) == (to >> log2(block))) & (up < to)
    position = dot(hit.astype(BF16), jnp.where(earlier, 1.0, 0.0).astype(BF16))
    select = jnp.where(own_block & (position == slot), hit, 0.0)
    gate = jnp.sum(select * (hits[0] * gates[0] + hits[1] * gates[1]), axis=1, keepdims=True)
    return select, gate


class Stream:
    def __init__(self, s, weight, room, sems, place, first=0):
        self.s, self.weight, self.room, self.sems, self.place = s, weight, room, sems, place
        for k in range(first, min(first + 2, s.slices)):
            for p in range(len(s.pieces)):
                self.copy(k, p).start()

    def slot(self, k, p):
        return lax.rem(k, 2) * len(self.s.pieces) + p

    def copy(self, k, p):
        at, size = self.s.pieces[p]
        start = pl.multiple_of(self.place(k) * self.s.width + at, LANES)
        slot = self.slot(k, p)
        return pltpu.make_async_copy(
            self.weight.at[:, :, pl.ds(start, size)], self.room.at[slot, :, :, pl.ds(0, size)], self.sems.at[slot]
        )

    def get(self, k, p):
        self.copy(k, p).wait()
        return self.room.at[self.slot(k, p), :, :, pl.ds(0, self.s.pieces[p][1])]

    def free(self, k, p):
        @pl.when(k + 2 < self.s.slices)
        def _():
            self.copy(k + 2, p).start()


def held_copy(s, weight, held, sems, k, p):
    at, size = s.pieces[p]
    columns = (slice(None), slice(None), pl.ds(pl.multiple_of(k * s.width + at, LANES), size))
    return pltpu.make_async_copy(weight.at[columns], held.at[columns], sems.at[k * len(s.pieces) + p])


def hold_kernel(s, weight, _, held, sems):
    copies = []
    for k in range(s.early):
        for at, size in s.pieces:
            source = pl.ds(pl.multiple_of(s.grid.source(k) * s.width + at, LANES), size)
            target = pl.ds(k * s.width + at, size)
            copies.append(
                pltpu.make_async_copy(weight.at[:, :, source], held.at[:, :, target], sems.at[len(copies)])
            )
            copies[-1].start()
    for copy in copies:
        copy.wait()


def hold(s, weight, after):
    (held,) = call(
        functools.partial(hold_kernel, s),
        "hold_down",
        [pltpu.VMEM((s.local, s.hidden, s.early * s.width), BF16)],
        [hbm(weight), after],
        specs=[ANYWHERE] * 2,
        scratch=[pltpu.SemaphoreType.DMA((s.early * len(s.pieces),))],
        cost=12000,
    )
    return held


class Sizes:
    def __init__(self, grid, tokens, w_gate):
        self.grid = grid
        self.local, self.hidden, self.features = w_gate.shape
        self.block, self.width = tokens.shape
        self.rows = grid.dp * CAP
        self.total = self.local * self.rows
        self.count = grid.dp * self.block
        self.column = grid.nz * self.block
        self.blocks = grid.nc * grid.ny * grid.nx
        self.slices = grid.nc * grid.ny
        whole = self.width % 256 == 0 and self.width > 1024
        self.pieces = [(0, 1024), (1024, self.width - 1024)] if whole else [(0, self.width)]
        self.early = self.slices // EARLY

    def block_of(self, blocks, c, a, b):
        n = self.grid.square.index((a, b)) - 1
        return blocks[2 * c] if n < 0 else blocks[2 * c + 1].at[n * self.column : (n + 1) * self.column]

    def at(self, e):
        return slice(e * self.rows, (e + 1) * self.rows)


def routed(s, blocks, select):
    for k in range(s.slices):
        group = [s.block_of(blocks, k // s.grid.ny, a, k % s.grid.ny)[:, : s.width] for a in range(s.grid.nx)]
        yield k, dot(select, jnp.concatenate(group, axis=0))


def gate_up_kernel(s, *refs):
    blocks, refs = refs[: 2 * s.grid.nc], refs[2 * s.grid.nc :]
    wg_ref, wu_ref, _, x_ref, select_ref, back_ref, gate_ref, act_ref, p_ref, q_ref, held_ref = refs[:11]
    room, sems, held_sems, g_acc, u_acc = refs[11:]
    ups = Stream(s, wu_ref, room, sems, lambda k: k)
    for k in range(min(2, s.slices)):
        for p in range(len(s.pieces)):
            held_copy(s, wg_ref, held_ref, held_sems, k, p).start()
    aux = jnp.concatenate([s.block_of(blocks, 0, a, 0)[:, s.width :] for a in range(s.grid.nx)], axis=0)
    select, gate = tables(aux, lax.axis_index("hst") * s.local, s.rows, s.local, s.block)
    gate_ref[...] = jnp.broadcast_to(gate, gate_ref.shape)
    select_ref[...] = select.astype(BF16)
    back_ref[...] = jnp.transpose(select).astype(BF16)
    for k, picked in routed(s, blocks, select.astype(BF16)):
        x_ref[s.grid.source(k)] = picked.astype(BF16)
    g_acc[...] = jnp.zeros_like(g_acc)
    u_acc[...] = jnp.zeros_like(u_acc)

    def step(k, _):
        for p, (at, size) in enumerate(s.pieces):

            @pl.when(k + 2 < s.slices)
            def _():
                held_copy(s, wg_ref, held_ref, held_sems, k + 2, p).start()

            held_copy(s, wg_ref, held_ref, held_sems, k, p).wait()
            up = ups.get(k, p)
            gate = held_ref.at[:, :, pl.ds(pl.multiple_of(k * s.width + at, LANES), size)]
            for e in range(s.local):
                x = x_ref[k, s.at(e), at : at + size]
                g_acc[e] += dot_t(x, gate[e])
                u_acc[e] += dot_t(x, up[e])
            ups.free(k, p)
        return 0

    lax.fori_loop(0, s.slices, step, 0)
    for e in range(s.local):
        g, u = g_acc[e], u_acc[e]
        sigma = jax.nn.sigmoid(g)
        act_ref[e] = (g * sigma * u).astype(BF16)
        p_ref[e] = u * sigma * (1.0 + g * (1.0 - sigma))
        q_ref[e] = g * sigma


def to_tokens(s, k, at, found, back_ref, outs):
    sums = dot(back_ref[...], jnp.concatenate(found, axis=0)).astype(BF16)
    size = sums.shape[-1]
    sums = sums.reshape(s.grid.nx, s.column, size)
    for c, out in enumerate(outs):

        @pl.when(k >> log2(s.grid.ny) == c)
        def _():
            out[:, k & (s.grid.ny - 1), :, at : at + size] = sums


def forward_kernel(s, act_ref, gate_ref, back_ref, held_ref, w_ref, _, *refs):
    outs, (room, sems) = refs[:-2], refs[-2:]
    weights = Stream(s, w_ref, room, sems, s.grid.source, s.early)

    def step(k, _):
        for p, (at, size) in enumerate(s.pieces):
            use(k, p, at, weights.get(k, p))
            weights.free(k, p)
        return 0

    def use(k, p, at, weight):
        found = [(dot(act_ref[e], weight[e]) * gate_ref[s.at(e), :1]).astype(BF16) for e in range(s.local)]
        to_tokens(s, k, at, found, back_ref, outs)

    def early(k, _):
        for p, (at, size) in enumerate(s.pieces):
            use(k, p, at, held_ref.at[:, :, pl.ds(pl.multiple_of(k * s.width + at, LANES), size)])
        return 0

    lax.fori_loop(0, s.early, early, 0)
    lax.fori_loop(s.early, s.slices, step, 0)


def hidden_grads_kernel(s, *refs):
    blocks, refs = refs[: 2 * s.grid.nc], refs[2 * s.grid.nc :]
    select_ref, gate_ref, p_ref, q_ref, w_ref, _, d_ref, dg_ref, du_ref, room, sems, acc = refs
    weights = Stream(s, w_ref, room, sems, lambda k: k)
    for k, picked in routed(s, blocks, select_ref[...]):
        d_ref[s.grid.source(k)] = (picked * gate_ref[:, :1]).astype(BF16)
    acc[...] = jnp.zeros_like(acc)

    def step(k, _):
        for p, (at, size) in enumerate(s.pieces):
            weight = weights.get(k, p)
            for e in range(s.local):
                acc[e] += dot_t(d_ref[k, s.at(e), at : at + size], weight[e])
            weights.free(k, p)
        return 0

    lax.fori_loop(0, s.slices, step, 0)
    for e in range(s.local):
        dg_ref[e] = (acc[e] * p_ref[e]).astype(BF16)
        du_ref[e] = (acc[e] * q_ref[e]).astype(BF16)


def backward_kernel(s, dg_ref, du_ref, back_ref, held_ref, w_ref, _, *refs):
    outs, (room, sems) = refs[:-2], refs[-2:]
    weights = Stream(s, w_ref, room, sems, s.grid.source)

    def step(k, _):
        for p, (at, size) in enumerate(s.pieces):
            gate = held_ref.at[:, :, pl.ds(pl.multiple_of(s.grid.source(k) * s.width + at, LANES), size)]
            up = weights.get(k, p)
            found = [(dot(dg_ref[e], gate[e]) + dot(du_ref[e], up[e])).astype(BF16) for e in range(s.local)]
            to_tokens(s, k, at, found, back_ref, outs)
            weights.free(k, p)
        return 0

    lax.fori_loop(0, s.slices, step, 0)


def turn(s, left_ref, turned):
    for e in range(s.local):
        turned[e] = jnp.transpose(left_ref[e].astype(F32)).astype(BF16)


def grads_kernel(s, count, *refs):
    lefts, rows_refs = refs[:count], refs[count : 2 * count]
    outs, (marker, turned, store, sems) = refs[2 * count + 1 : -4], refs[-4:]
    marker[...] = jnp.zeros_like(marker)
    pieces = len(s.pieces)

    def copy(out, k, p):
        at, size = s.pieces[p]
        slot = lax.rem(k, 2) * pieces + p
        start = pl.multiple_of(k * s.width + at, LANES)
        return pltpu.make_async_copy(
            store.at[slot, :, :, pl.ds(0, size)], out.at[:, :, pl.ds(start, size)], sems.at[slot]
        )

    for left_ref, rows_ref, out in zip(lefts, rows_refs, outs):
        turn(s, left_ref, turned)

        def step(k, _):
            for p, (at, size) in enumerate(s.pieces):

                @pl.when(k >= 2)
                def _():
                    copy(out, k - 2, p).wait()

                for e in range(s.local):
                    rows = rows_ref[k, s.at(e), at : at + size]
                    store[lax.rem(k, 2) * pieces + p, e, :, :size] = dot(turned[e], rows).astype(BF16)
                copy(out, k, p).start()
            return 0

        lax.fori_loop(0, s.slices, step, 0)
        for k in range(max(0, s.slices - 2), s.slices):
            for p in range(pieces):
                copy(out, k, p).wait()


def grads(s, name, lefts, rights, after):
    room = max(size for _, size in s.pieces)
    count = len(lefts)
    slots = 2 * len(s.pieces)
    return call(
        functools.partial(grads_kernel, s, count),
        name,
        [shaped(BF16, s.local, s.hidden, s.features)] * count + [shaped(F32, 8, LANES)],
        [*lefts, *rights, after],
        specs=[VECTORS] * (2 * count) + [ANYWHERE],
        out_specs=[ANYWHERE] * count + [VECTORS],
        scratch=[
            pltpu.VMEM((s.local, s.hidden, s.rows), BF16),
            pltpu.VMEM((slots, s.local, s.hidden, room), BF16),
            pltpu.SemaphoreType.DMA((slots,)),
        ],
        cost=46000,
    )


def body(tokens, cotangent, expert_ids, gate_values, w_gate, w_up, w_down):
    grid = Grid(lax.axis_size("dp"), lax.axis_size("hst"))
    s = Sizes(grid, tokens, w_gate)

    sources = [tokens, expert_ids.T, gate_values.T, cotangent]
    message, cotangent = call(
        pack_kernel,
        "pack",
        [shaped(BF16, s.block, s.width + LANES), shaped(BF16, s.block, s.width)],
        [hbm(source) for source in sources],
        specs=[ANYWHERE] * 4,
        scratch=[pltpu.VMEM(a.shape, a.dtype) for a in sources[:3]] + [pltpu.SemaphoreType.DMA((4,))],
    )
    x_parts = grid.along_z(message)
    x_column, cotangent = stack(x_parts, [], "stack_tokens", [cotangent])
    x_plane = grid.over_plane(x_column)
    d_column, held_down = doubled_along_z(grid, cotangent, lambda after: hold(s, w_down, after))
    x_others = stack([x_plane[at] for at in grid.square[1:]], [d_column], "stack_tokens_plane")
    x_blocks = grid.over_cores(x_column, x_others)
    d_column = stack([d_column], [x_others], "stack_cotangents")
    d_plane = grid.over_plane(d_column)
    room = max(size for _, size in s.pieces)
    slots = 2 * len(s.pieces)
    streams = [pltpu.VMEM((slots, s.local, s.hidden, room), BF16), pltpu.SemaphoreType.DMA((slots,))]

    hidden_shape = (s.local, s.rows, s.hidden)
    sums_room = pltpu.VMEM(hidden_shape, F32)
    rows_shape = shaped(BF16, s.slices, s.total, s.width)
    x_rows, select, back, gate, act, p, q, held_gate = call(
        functools.partial(gate_up_kernel, s),
        "gate_up",
        [
            rows_shape,
            shaped(BF16, s.total, s.count),
            shaped(BF16, s.count, s.total),
            shaped(F32, s.total, LANES),
            shaped(BF16, *hidden_shape),
            shaped(F32, *hidden_shape),
            shaped(F32, *hidden_shape),
            pltpu.VMEM(w_gate.shape, BF16),
        ],
        [*x_blocks, hbm(w_gate), hbm(w_up), d_column],
        specs=[VECTORS] * len(x_blocks) + [ANYWHERE] * 3,
        scratch=[*streams, pltpu.SemaphoreType.DMA((s.slices * len(s.pieces),)), sums_room, sums_room],
        cost=46000,
    )
    d_others = stack([d_plane[at] for at in grid.square[1:]], [gate], "stack_cotangents_plane")
    d_blocks = grid.over_cores(d_column, d_others)
    sums = shaped(BF16, grid.nx, grid.ny, s.column, s.width)
    out_parts = call(
        functools.partial(forward_kernel, s),
        "forward",
        [sums] * grid.nc,
        [act, gate, back, held_down, hbm(w_down), d_others],
        specs=[VECTORS] * 4 + [ANYWHERE] * 2,
        scratch=streams,
        cost=46000,
    )
    d_rows, d_gate, d_up = call(
        functools.partial(hidden_grads_kernel, s),
        "hidden_grads",
        [rows_shape, shaped(BF16, *hidden_shape), shaped(BF16, *hidden_shape)],
        [*d_blocks, select, gate, p, q, hbm(w_down), out_parts[0]],
        specs=[VECTORS] * (len(d_blocks) + 4) + [ANYWHERE] * 2,
        scratch=[*streams, sums_room],
        cost=46000,
    )
    mixed_kept = back_over_cores(grid, out_parts, [d_gate], "mixed_cores")
    back_parts = call(
        functools.partial(backward_kernel, s),
        "backward",
        [sums] * grid.nc,
        [d_gate, d_up, back, held_gate, hbm(w_up), mixed_kept[0]],
        specs=[VECTORS] * 4 + [ANYWHERE] * 2,
        scratch=streams,
        cost=46000,
    )
    *mixed_total, last = back_over_plane(grid, mixed_kept, back_parts[:1], "mixed_plane", back_parts[-1:])
    token_kept = back_over_cores(grid, [*back_parts[:-1], last], [], "tokens_cores")
    grad_gate, grad_down, done = grads(s, "grad_gate_down", [d_gate, act], [x_rows, d_rows], token_kept[0])
    token_total = back_over_plane(grid, token_kept, [done], "tokens_plane")
    grad_up, done = grads(s, "grad_up", [d_up], [x_rows], token_total[0])
    mixed, grad_tokens = finish(back_along_z(grid, mixed_total), back_along_z(grid, token_total), [done])
    return mixed, grad_tokens, grad_gate, grad_up, grad_down


def solution(mesh):
    return jax.shard_map(
        body,
        mesh=mesh,
        in_specs=(
            P("dp", "hst"),
            P("dp", "hst"),
            P("dp", None),
            P("dp", None),
            P("hst", "dp", None),
            P("hst", "dp", None),
            P("hst", "dp", None),
        ),
        out_specs=(
            P("dp", "hst"),
            P("dp", "hst"),
            P("hst", "dp", None),
            P("hst", "dp", None),
            P("hst", "dp", None),
        ),
        check_vma=False,
    )
```

```python
import functools
import math

import jax
import jax.numpy as jnp
from jax import lax
from jax.experimental import pallas as pl
from jax.experimental.pallas import tpu as pltpu
from jax.sharding import PartitionSpec as P

CAP = 4
LANES = 128
MIB = 1 << 20
MFLOP = 10**6
EARLY = 2
F32 = jnp.float32
BF16 = jnp.bfloat16
AXES = ("dp", "hst")


def dot(a, b):
    return lax.dot_general(a, b, (((1,), (0,)), ((), ())), preferred_element_type=F32)


def dot_t(a, b):
    return lax.dot_general(a, b, (((1,), (1,)), ((), ())), preferred_element_type=F32)


def log2(n):
    assert n & (n - 1) == 0
    return n.bit_length() - 1


class Grid:
    def __init__(self, dp, hst):
        self.dp, self.hst = dp, hst
        self.nc = 2 if hst % 2 == 0 else 1
        self.ny = hst // self.nc
        self.nx = self.ny if dp % self.ny == 0 else 1
        self.nz = dp // self.nx
        assert self.nz & (self.nz - 1) == 0
        self.square = [(a, b) for a in range(self.nx) for b in range(self.ny)]

    def shift(self, value, dz=0, dx=0, dy=0, dc=0):
        pairs = []
        for z in range(self.nz):
            for x in range(self.nx):
                for y in range(self.ny):
                    for c in range(self.nc):
                        to_dp = (z ^ dz) * self.nx + (x + dx) % self.nx
                        to_hst = (y + dy) % self.ny * self.nc + (c + dc) % self.nc
                        here = (z * self.nx + x) * self.hst + y * self.nc + c
                        pairs.append((here, to_dp * self.hst + to_hst))
        return lax.ppermute(value, AXES, pairs)

    def along_z(self, mine):
        return [mine] + [self.shift(mine, dz=k) for k in range(1, self.nz)]

    def over_plane(self, column):
        return {(a, b): self.shift(column, dx=a, dy=b) if a or b else column for a, b in self.square}

    def over_cores(self, column, others):
        blocks = [column, others]
        for c in range(1, self.nc):
            blocks += [self.shift(column, dc=c), self.shift(others, dc=c)]
        return blocks

    def source(self, k):
        host = lax.axis_index("hst")
        y, core = host >> log2(self.nc), host & (self.nc - 1)
        from_y = (y - (k & (self.ny - 1))) & (self.ny - 1)
        return (from_y << log2(self.nc)) + ((core + (k >> log2(self.ny))) & (self.nc - 1))


def call(kernel, name, outs, args, specs=None, out_specs=None, scratch=(), grid=(), limit=16, cost=0, aliases=None):
    specs = specs or [pl.BlockSpec(memory_space=pltpu.VMEM)] * len(args)
    out_specs = out_specs or [pl.BlockSpec(memory_space=pltpu.VMEM)] * len(outs)
    return pl.pallas_call(
        kernel,
        name=name,
        grid=grid,
        out_shape=outs,
        in_specs=specs,
        out_specs=out_specs,
        scratch_shapes=list(scratch),
        input_output_aliases=aliases or {},
        compiler_params=pltpu.CompilerParams(vmem_limit_bytes=limit * MIB),
        cost_estimate=pl.CostEstimate(flops=cost * MFLOP, bytes_accessed=0, transcendentals=0),
    )(*args)


def shaped(dtype, *dims):
    return jax.ShapeDtypeStruct(dims, dtype)


VECTORS = pl.BlockSpec(memory_space=pltpu.VMEM)
ANYWHERE = pl.BlockSpec(memory_space=pl.ANY)


def hbm(weight):
    return pltpu.with_memory_space_constraint(weight, pltpu.HBM)


def pack_kernel(tokens, ids, gates, later, out_ref, later_ref, tokens_ref, ids_ref, gates_ref, sems):
    pairs = [(tokens, tokens_ref), (ids, ids_ref), (gates, gates_ref), (later, later_ref)]
    copies = [pltpu.make_async_copy(a, b, sems.at[k]) for k, (a, b) in enumerate(pairs)]
    for copy in copies:
        copy.start()
    for copy in copies:
        copy.wait()
    rows, width = tokens_ref.shape
    out_ref[:, :width] = tokens_ref[...]
    values = gates_ref[...]
    high = values.astype(BF16).astype(F32)
    middle = (values - high).astype(BF16).astype(F32)
    low = values - high - middle
    fields = jnp.concatenate([ids_ref[...].astype(F32), high, middle, low], axis=0)
    fields = jnp.pad(fields, ((0, LANES - fields.shape[0]), (0, LANES - rows)))
    out_ref[:, width:] = jnp.transpose(fields)[:rows].astype(BF16)


def stack_kernel(count, later, *refs):
    parts, out_ref = refs[:count], refs[-1 - later]
    rows = parts[0].shape[0]
    for k, part in enumerate(parts):
        out_ref[k * rows : (k + 1) * rows] = part[...]
    if later:
        refs[-1][...] = refs[count][...]


def stack(parts, after, name, later=()):
    rows, width = parts[0].shape
    outs = call(
        functools.partial(stack_kernel, len(parts), len(later)),
        name,
        [shaped(BF16, rows * len(parts), width)] + [shaped(BF16, *array.shape) for array in later],
        [*parts, *later, *after],
        specs=[VECTORS] * (len(parts) + len(later)) + [ANYWHERE] * len(after),
        limit=16,
    )
    return outs if later else outs[0]


def add_kernel(count, skip, pieces, *refs):
    parts, outs = refs[:count], refs[count + skip : count + skip + pieces]
    total = parts[0][...].astype(F32)
    for part in parts[1:]:
        total = total + part[...].astype(F32)
    total = total.astype(BF16).reshape((pieces,) + outs[0].shape)
    for k, out in enumerate(outs):
        out[...] = total[k]


def add(parts, pieces, after, name, later=()):
    *lead, rows, width = parts[0].shape
    each = math.prod(lead) * rows // pieces
    first = len(parts) + len(after)
    return call(
        functools.partial(add_kernel, len(parts), len(after) + len(later), pieces),
        name,
        [shaped(BF16, each, width)] * pieces + [shaped(BF16, *array.shape) for array in later],
        [*parts, *after, *later],
        specs=[VECTORS] * len(parts) + [ANYWHERE] * (len(after) + len(later)),
        out_specs=[VECTORS] * pieces + [ANYWHERE] * len(later),
        aliases={first + k: pieces + k for k in range(len(later))},
    )


def doubled_along_z(grid, mine, meanwhile):
    column, k, done = mine, 1, None
    while k < grid.nz:
        got = grid.shift(column, dz=k)
        if 2 * k >= grid.nz:
            done = meanwhile(column)
        column = stack([column, got], [] if done is None else [done], "double")
        k *= 2
    return column, meanwhile(column) if done is None else done


def back_over_cores(grid, parts, after, name):
    got = [grid.shift(parts[c], dc=-c) for c in range(1, grid.nc)]
    return add([parts[0], *got], len(grid.square), after, name)


def back_over_plane(grid, kept, after, name, later=()):
    got = [grid.shift(part, dx=-a, dy=-b) for part, (a, b) in zip(kept[1:], grid.square[1:])]
    return add([kept[0], *got], grid.nz, after, name, later)


def back_along_z(grid, total):
    return [total[0]] + [grid.shift(total[k], dz=k) for k in range(1, grid.nz)]


def finish_kernel(count, *refs):
    for n, out in enumerate(refs[-2:]):
        total = refs[n * count][...].astype(F32)
        for part in refs[n * count + 1 : (n + 1) * count]:
            total = total + part[...].astype(F32)
        out[...] = total.astype(BF16)


def finish(first, second, after):
    return call(
        functools.partial(finish_kernel, len(first)),
        "finish",
        [shaped(BF16, *first[0].shape)] * 2,
        [*first, *second, *after],
        specs=[VECTORS] * (2 * len(first)) + [ANYWHERE] * len(after),
    )


def tables(aux, first, rows, local, block):
    tokens = aux.shape[0]
    across = jnp.transpose(aux.astype(F32))
    ids = [across[k : k + 1] for k in range(2)]
    gates = [across[2 + k : 3 + k] + across[4 + k : 5 + k] + across[6 + k : 7 + k] for k in range(2)]
    total = local * rows
    r = lax.broadcasted_iota(jnp.int32, (total, tokens), 0)
    j = lax.broadcasted_iota(jnp.int32, (total, tokens), 1)
    expert = ((r >> log2(rows)) + first).astype(F32)
    own_block = ((r & (rows - 1)) >> log2(CAP)) == (j >> log2(block))
    slot = (r & (CAP - 1)).astype(F32)
    hits = [(ids[k] == expert).astype(F32) for k in range(2)]
    hit = hits[0] + hits[1]
    up = lax.broadcasted_iota(jnp.int32, (tokens, tokens), 0)
    to = lax.broadcasted_iota(jnp.int32, (tokens, tokens), 1)
    earlier = ((up >> log2(block)) == (to >> log2(block))) & (up < to)
    position = dot(hit.astype(BF16), jnp.where(earlier, 1.0, 0.0).astype(BF16))
    select = jnp.where(own_block & (position == slot), hit, 0.0)
    gate = jnp.sum(select * (hits[0] * gates[0] + hits[1] * gates[1]), axis=1, keepdims=True)
    return select, gate


class Stream:
    def __init__(self, s, weight, room, sems, place, first=0):
        self.s, self.weight, self.room, self.sems, self.place = s, weight, room, sems, place
        for k in range(first, min(first + 2, s.slices)):
            for p in range(len(s.pieces)):
                self.copy(k, p).start()

    def slot(self, k, p):
        return lax.rem(k, 2) * len(self.s.pieces) + p

    def copy(self, k, p):
        at, size = self.s.pieces[p]
        start = pl.multiple_of(self.place(k) * self.s.width + at, LANES)
        slot = self.slot(k, p)
        return pltpu.make_async_copy(
            self.weight.at[:, :, pl.ds(start, size)], self.room.at[slot, :, :, pl.ds(0, size)], self.sems.at[slot]
        )

    def get(self, k, p):
        self.copy(k, p).wait()
        return self.room.at[self.slot(k, p), :, :, pl.ds(0, self.s.pieces[p][1])]

    def free(self, k, p):
        @pl.when(k + 2 < self.s.slices)
        def _():
            self.copy(k + 2, p).start()


def held_copy(s, weight, held, sems, k, p):
    at, size = s.pieces[p]
    columns = (slice(None), slice(None), pl.ds(pl.multiple_of(k * s.width + at, LANES), size))
    return pltpu.make_async_copy(weight.at[columns], held.at[columns], sems.at[k * len(s.pieces) + p])


def hold_kernel(s, weight, _, held, sems):
    copies = []
    for k in range(s.early):
        for at, size in s.pieces:
            source = pl.ds(pl.multiple_of(s.grid.source(k) * s.width + at, LANES), size)
            target = pl.ds(k * s.width + at, size)
            copies.append(
                pltpu.make_async_copy(weight.at[:, :, source], held.at[:, :, target], sems.at[len(copies)])
            )
            copies[-1].start()
    for copy in copies:
        copy.wait()


def hold_gate_kernel(s, weight, _, held, sems):
    copies = [held_copy(s, weight, held, sems, k, p) for k in range(s.early) for p in range(len(s.pieces))]
    for copy in copies:
        copy.start()
    for copy in copies:
        copy.wait()


def hold_gate(s, weight, after):
    (held,) = call(
        functools.partial(hold_gate_kernel, s),
        "hold_gate",
        [pltpu.VMEM(weight.shape, BF16)],
        [hbm(weight), after],
        specs=[ANYWHERE] * 2,
        scratch=[pltpu.SemaphoreType.DMA((s.early * len(s.pieces),))],
        cost=12000,
    )
    return held


def hold(s, weight, after):
    (held,) = call(
        functools.partial(hold_kernel, s),
        "hold_down",
        [pltpu.VMEM((s.local, s.hidden, s.early * s.width), BF16)],
        [hbm(weight), after],
        specs=[ANYWHERE] * 2,
        scratch=[pltpu.SemaphoreType.DMA((s.early * len(s.pieces),))],
        cost=12000,
    )
    return held


class Sizes:
    def __init__(self, grid, tokens, w_gate):
        self.grid = grid
        self.local, self.hidden, self.features = w_gate.shape
        self.block, self.width = tokens.shape
        self.rows = grid.dp * CAP
        self.total = self.local * self.rows
        self.count = grid.dp * self.block
        self.column = grid.nz * self.block
        self.blocks = grid.nc * grid.ny * grid.nx
        self.slices = grid.nc * grid.ny
        whole = self.width % 256 == 0 and self.width > 1024
        self.pieces = [(0, 1024), (1024, self.width - 1024)] if whole else [(0, self.width)]
        self.early = self.slices // EARLY

    def block_of(self, blocks, c, a, b):
        n = self.grid.square.index((a, b)) - 1
        return blocks[2 * c] if n < 0 else blocks[2 * c + 1].at[n * self.column : (n + 1) * self.column]

    def at(self, e):
        return slice(e * self.rows, (e + 1) * self.rows)


def routed(s, blocks, select):
    for k in range(s.slices):
        group = [s.block_of(blocks, k // s.grid.ny, a, k % s.grid.ny)[:, : s.width] for a in range(s.grid.nx)]
        yield k, dot(select, jnp.concatenate(group, axis=0))


def gate_up_kernel(s, *refs):
    blocks, refs = refs[: 2 * s.grid.nc], refs[2 * s.grid.nc :]
    _, wg_ref, wu_ref, _, x_ref, select_ref, back_ref, gate_ref, act_ref, p_ref, q_ref, held_ref = refs[:12]
    room, sems, held_sems, g_acc, u_acc = refs[12:]
    ups = Stream(s, wu_ref, room, sems, lambda k: k)
    for k in range(s.early, min(2, s.slices)):
        for p in range(len(s.pieces)):
            held_copy(s, wg_ref, held_ref, held_sems, k, p).start()
    aux = jnp.concatenate([s.block_of(blocks, 0, a, 0)[:, s.width :] for a in range(s.grid.nx)], axis=0)
    select, gate = tables(aux, lax.axis_index("hst") * s.local, s.rows, s.local, s.block)
    gate_ref[...] = jnp.broadcast_to(gate, gate_ref.shape)
    select_ref[...] = select.astype(BF16)
    back_ref[...] = jnp.transpose(select).astype(BF16)
    for k, picked in routed(s, blocks, select.astype(BF16)):
        x_ref[s.grid.source(k)] = picked.astype(BF16)
    g_acc[...] = jnp.zeros_like(g_acc)
    u_acc[...] = jnp.zeros_like(u_acc)

    def step(k, _):
        for p, (at, size) in enumerate(s.pieces):

            @pl.when((k + 2 >= s.early) & (k + 2 < s.slices))
            def _():
                held_copy(s, wg_ref, held_ref, held_sems, k + 2, p).start()

            @pl.when(k >= s.early)
            def _():
                held_copy(s, wg_ref, held_ref, held_sems, k, p).wait()

            up = ups.get(k, p)
            gate = held_ref.at[:, :, pl.ds(pl.multiple_of(k * s.width + at, LANES), size)]
            for e in range(s.local):
                x = x_ref[k, s.at(e), at : at + size]
                g_acc[e] += dot_t(x, gate[e])
                u_acc[e] += dot_t(x, up[e])
            ups.free(k, p)
        return 0

    lax.fori_loop(0, s.slices, step, 0)
    for e in range(s.local):
        g, u = g_acc[e], u_acc[e]
        sigma = jax.nn.sigmoid(g)
        act_ref[e] = (g * sigma * u).astype(BF16)
        p_ref[e] = u * sigma * (1.0 + g * (1.0 - sigma))
        q_ref[e] = g * sigma


def to_tokens(s, k, at, found, back_ref, outs):
    sums = dot(back_ref[...], jnp.concatenate(found, axis=0)).astype(BF16)
    size = sums.shape[-1]
    sums = sums.reshape(s.grid.nx, s.column, size)
    for c, out in enumerate(outs):

        @pl.when(k >> log2(s.grid.ny) == c)
        def _():
            out[:, k & (s.grid.ny - 1), :, at : at + size] = sums


def forward_kernel(s, act_ref, gate_ref, back_ref, held_ref, w_ref, _, *refs):
    outs, (room, sems) = refs[:-2], refs[-2:]
    weights = Stream(s, w_ref, room, sems, s.grid.source, s.early)

    def step(k, _):
        for p, (at, size) in enumerate(s.pieces):
            use(k, p, at, weights.get(k, p))
            weights.free(k, p)
        return 0

    def use(k, p, at, weight):
        found = [(dot(act_ref[e], weight[e]) * gate_ref[s.at(e), :1]).astype(BF16) for e in range(s.local)]
        to_tokens(s, k, at, found, back_ref, outs)

    def early(k, _):
        for p, (at, size) in enumerate(s.pieces):
            use(k, p, at, held_ref.at[:, :, pl.ds(pl.multiple_of(k * s.width + at, LANES), size)])
        return 0

    lax.fori_loop(0, s.early, early, 0)
    lax.fori_loop(s.early, s.slices, step, 0)


def hidden_grads_kernel(s, *refs):
    blocks, refs = refs[: 2 * s.grid.nc], refs[2 * s.grid.nc :]
    select_ref, gate_ref, p_ref, q_ref, w_ref, _, d_ref, dg_ref, du_ref, room, sems, acc = refs
    weights = Stream(s, w_ref, room, sems, lambda k: k)
    for k, picked in routed(s, blocks, select_ref[...]):
        d_ref[s.grid.source(k)] = (picked * gate_ref[:, :1]).astype(BF16)
    acc[...] = jnp.zeros_like(acc)

    def step(k, _):
        for p, (at, size) in enumerate(s.pieces):
            weight = weights.get(k, p)
            for e in range(s.local):
                acc[e] += dot_t(d_ref[k, s.at(e), at : at + size], weight[e])
            weights.free(k, p)
        return 0

    lax.fori_loop(0, s.slices, step, 0)
    for e in range(s.local):
        dg_ref[e] = (acc[e] * p_ref[e]).astype(BF16)
        du_ref[e] = (acc[e] * q_ref[e]).astype(BF16)


def backward_kernel(s, dg_ref, du_ref, back_ref, held_ref, w_ref, _, *refs):
    outs, (room, sems) = refs[:-2], refs[-2:]
    weights = Stream(s, w_ref, room, sems, s.grid.source)

    def step(k, _):
        for p, (at, size) in enumerate(s.pieces):
            gate = held_ref.at[:, :, pl.ds(pl.multiple_of(s.grid.source(k) * s.width + at, LANES), size)]
            found = [dot(dg_ref[e], gate[e]) for e in range(s.local)]
            up = weights.get(k, p)
            found = [(found[e] + dot(du_ref[e], up[e])).astype(BF16) for e in range(s.local)]
            to_tokens(s, k, at, found, back_ref, outs)
            weights.free(k, p)
        return 0

    lax.fori_loop(0, s.slices, step, 0)


def turn(s, left_ref, turned):
    for e in range(s.local):
        turned[e] = jnp.transpose(left_ref[e].astype(F32)).astype(BF16)


def grads_kernel(s, count, *refs):
    lefts, rows_refs = refs[:count], refs[count : 2 * count]
    outs, (marker, turned, store, sems) = refs[2 * count + 1 : -4], refs[-4:]
    marker[...] = jnp.zeros_like(marker)
    pieces = len(s.pieces)

    def copy(out, k, p):
        at, size = s.pieces[p]
        slot = lax.rem(k, 2) * pieces + p
        start = pl.multiple_of(k * s.width + at, LANES)
        return pltpu.make_async_copy(
            store.at[slot, :, :, pl.ds(0, size)], out.at[:, :, pl.ds(start, size)], sems.at[slot]
        )

    for left_ref, rows_ref, out in zip(lefts, rows_refs, outs):
        turn(s, left_ref, turned)

        def step(k, _):
            for p, (at, size) in enumerate(s.pieces):

                @pl.when(k >= 2)
                def _():
                    copy(out, k - 2, p).wait()

                for e in range(s.local):
                    rows = rows_ref[k, s.at(e), at : at + size]
                    store[lax.rem(k, 2) * pieces + p, e, :, :size] = dot(turned[e], rows).astype(BF16)
                copy(out, k, p).start()
            return 0

        lax.fori_loop(0, s.slices, step, 0)
        for k in range(max(0, s.slices - 2), s.slices):
            for p in range(pieces):
                copy(out, k, p).wait()


def grads(s, name, lefts, rights, after):
    room = max(size for _, size in s.pieces)
    count = len(lefts)
    slots = 2 * len(s.pieces)
    return call(
        functools.partial(grads_kernel, s, count),
        name,
        [shaped(BF16, s.local, s.hidden, s.features)] * count + [shaped(F32, 8, LANES)],
        [*lefts, *rights, after],
        specs=[VECTORS] * (2 * count) + [ANYWHERE],
        out_specs=[ANYWHERE] * count + [VECTORS],
        scratch=[
            pltpu.VMEM((s.local, s.hidden, s.rows), BF16),
            pltpu.VMEM((slots, s.local, s.hidden, room), BF16),
            pltpu.SemaphoreType.DMA((slots,)),
        ],
        cost=46000,
    )


def body(tokens, cotangent, expert_ids, gate_values, w_gate, w_up, w_down):
    grid = Grid(lax.axis_size("dp"), lax.axis_size("hst"))
    s = Sizes(grid, tokens, w_gate)

    sources = [tokens, expert_ids.T, gate_values.T, cotangent]
    message, cotangent = call(
        pack_kernel,
        "pack",
        [shaped(BF16, s.block, s.width + LANES), shaped(BF16, s.block, s.width)],
        [hbm(source) for source in sources],
        specs=[ANYWHERE] * 4,
        scratch=[pltpu.VMEM(a.shape, a.dtype) for a in sources[:3]] + [pltpu.SemaphoreType.DMA((4,))],
    )
    x_parts = grid.along_z(message)
    x_column, cotangent = stack(x_parts, [], "stack_tokens", [cotangent])
    x_plane = grid.over_plane(x_column)
    d_column, held_down = doubled_along_z(grid, cotangent, lambda after: hold(s, w_down, after))
    held_gate = hold_gate(s, w_gate, d_column)
    x_others = stack([x_plane[at] for at in grid.square[1:]], [d_column, held_gate], "stack_tokens_plane")
    x_blocks = grid.over_cores(x_column, x_others)
    d_column = stack([d_column], [x_others], "stack_cotangents")
    d_plane = grid.over_plane(d_column)
    room = max(size for _, size in s.pieces)
    slots = 2 * len(s.pieces)
    streams = [pltpu.VMEM((slots, s.local, s.hidden, room), BF16), pltpu.SemaphoreType.DMA((slots,))]

    hidden_shape = (s.local, s.rows, s.hidden)
    sums_room = pltpu.VMEM(hidden_shape, F32)
    rows_shape = shaped(BF16, s.slices, s.total, s.width)
    x_rows, select, back, gate, act, p, q, held_gate = call(
        functools.partial(gate_up_kernel, s),
        "gate_up",
        [
            rows_shape,
            shaped(BF16, s.total, s.count),
            shaped(BF16, s.count, s.total),
            shaped(F32, s.total, LANES),
            shaped(BF16, *hidden_shape),
            shaped(F32, *hidden_shape),
            shaped(F32, *hidden_shape),
            pltpu.VMEM(w_gate.shape, BF16),
        ],
        [*x_blocks, held_gate, hbm(w_gate), hbm(w_up), d_column],
        specs=[VECTORS] * (len(x_blocks) + 1) + [ANYWHERE] * 3,
        aliases={len(x_blocks): 7},
        scratch=[*streams, pltpu.SemaphoreType.DMA((s.slices * len(s.pieces),)), sums_room, sums_room],
        cost=46000,
    )
    d_others = stack([d_plane[at] for at in grid.square[1:]], [gate], "stack_cotangents_plane")
    d_blocks = grid.over_cores(d_column, d_others)
    sums = shaped(BF16, grid.nx, grid.ny, s.column, s.width)
    out_parts = call(
        functools.partial(forward_kernel, s),
        "forward",
        [sums] * grid.nc,
        [act, gate, back, held_down, hbm(w_down), d_others],
        specs=[VECTORS] * 4 + [ANYWHERE] * 2,
        scratch=streams,
        cost=46000,
    )
    d_rows, d_gate, d_up = call(
        functools.partial(hidden_grads_kernel, s),
        "hidden_grads",
        [rows_shape, shaped(BF16, *hidden_shape), shaped(BF16, *hidden_shape)],
        [*d_blocks, select, gate, p, q, hbm(w_down), out_parts[0]],
        specs=[VECTORS] * (len(d_blocks) + 4) + [ANYWHERE] * 2,
        scratch=[*streams, sums_room],
        cost=46000,
    )
    mixed_kept = back_over_cores(grid, out_parts, [d_gate], "mixed_cores")
    back_parts = call(
        functools.partial(backward_kernel, s),
        "backward",
        [sums] * grid.nc,
        [d_gate, d_up, back, held_gate, hbm(w_up), mixed_kept[0]],
        specs=[VECTORS] * 4 + [ANYWHERE] * 2,
        scratch=streams,
        cost=46000,
    )
    *mixed_total, last = back_over_plane(grid, mixed_kept, back_parts[:1], "mixed_plane", back_parts[-1:])
    token_kept = back_over_cores(grid, [*back_parts[:-1], last], [], "tokens_cores")
    grad_gate, grad_down, done = grads(s, "grad_gate_down", [d_gate, act], [x_rows, d_rows], token_kept[0])
    token_total = back_over_plane(grid, token_kept, [done], "tokens_plane")
    grad_up, done = grads(s, "grad_up", [d_up], [x_rows], token_total[0])
    mixed, grad_tokens = finish(back_along_z(grid, mixed_total), back_along_z(grid, token_total), [done])
    return mixed, grad_tokens, grad_gate, grad_up, grad_down


def solution(mesh):
    return jax.shard_map(
        body,
        mesh=mesh,
        in_specs=(
            P("dp", "hst"),
            P("dp", "hst"),
            P("dp", None),
            P("dp", None),
            P("hst", "dp", None),
            P("hst", "dp", None),
            P("hst", "dp", None),
        ),
        out_specs=(
            P("dp", "hst"),
            P("dp", "hst"),
            P("hst", "dp", None),
            P("hst", "dp", None),
            P("hst", "dp", None),
        ),
        check_vma=False,
    )
```

```python
import functools
import math

import jax
import jax.numpy as jnp
from jax import lax
from jax.experimental import pallas as pl
from jax.experimental.pallas import tpu as pltpu
from jax.sharding import PartitionSpec as P

CAP = 4
LANES = 128
MIB = 1 << 20
MFLOP = 10**6
EARLY = 2
F32 = jnp.float32
BF16 = jnp.bfloat16
AXES = ("dp", "hst")


def dot(a, b):
    return lax.dot_general(a, b, (((1,), (0,)), ((), ())), preferred_element_type=F32)


def dot_t(a, b):
    return lax.dot_general(a, b, (((1,), (1,)), ((), ())), preferred_element_type=F32)


def log2(n):
    assert n & (n - 1) == 0
    return n.bit_length() - 1


class Grid:
    def __init__(self, dp, hst):
        self.dp, self.hst = dp, hst
        self.nc = 2 if hst % 2 == 0 else 1
        self.ny = hst // self.nc
        self.nx = self.ny if dp % self.ny == 0 else 1
        self.nz = dp // self.nx
        assert self.nz & (self.nz - 1) == 0
        self.square = [(a, b) for a in range(self.nx) for b in range(self.ny)]

    def shift(self, value, dz=0, dx=0, dy=0, dc=0):
        pairs = []
        for z in range(self.nz):
            for x in range(self.nx):
                for y in range(self.ny):
                    for c in range(self.nc):
                        to_dp = (z ^ dz) * self.nx + (x + dx) % self.nx
                        to_hst = (y + dy) % self.ny * self.nc + (c + dc) % self.nc
                        here = (z * self.nx + x) * self.hst + y * self.nc + c
                        pairs.append((here, to_dp * self.hst + to_hst))
        return lax.ppermute(value, AXES, pairs)

    def along_z(self, mine):
        return [mine] + [self.shift(mine, dz=k) for k in range(1, self.nz)]

    def over_plane(self, column):
        return {(a, b): self.shift(column, dx=a, dy=b) if a or b else column for a, b in self.square}

    def over_cores(self, column, others):
        blocks = [column, others]
        for c in range(1, self.nc):
            blocks += [self.shift(column, dc=c), self.shift(others, dc=c)]
        return blocks

    def source(self, k):
        host = lax.axis_index("hst")
        y, core = host >> log2(self.nc), host & (self.nc - 1)
        from_y = (y - (k & (self.ny - 1))) & (self.ny - 1)
        return (from_y << log2(self.nc)) + ((core + (k >> log2(self.ny))) & (self.nc - 1))


def call(kernel, name, outs, args, specs=None, out_specs=None, scratch=(), grid=(), limit=16, cost=0, aliases=None):
    specs = specs or [pl.BlockSpec(memory_space=pltpu.VMEM)] * len(args)
    out_specs = out_specs or [pl.BlockSpec(memory_space=pltpu.VMEM)] * len(outs)
    return pl.pallas_call(
        kernel,
        name=name,
        grid=grid,
        out_shape=outs,
        in_specs=specs,
        out_specs=out_specs,
        scratch_shapes=list(scratch),
        input_output_aliases=aliases or {},
        compiler_params=pltpu.CompilerParams(vmem_limit_bytes=limit * MIB),
        cost_estimate=pl.CostEstimate(flops=cost * MFLOP, bytes_accessed=0, transcendentals=0),
    )(*args)


def shaped(dtype, *dims):
    return jax.ShapeDtypeStruct(dims, dtype)


VECTORS = pl.BlockSpec(memory_space=pltpu.VMEM)
ANYWHERE = pl.BlockSpec(memory_space=pl.ANY)


def hbm(weight):
    return pltpu.with_memory_space_constraint(weight, pltpu.HBM)


def pack_kernel(tokens, ids, gates, later, out_ref, later_ref, tokens_ref, ids_ref, gates_ref, sems):
    pairs = [(tokens, tokens_ref), (ids, ids_ref), (gates, gates_ref), (later, later_ref)]
    copies = [pltpu.make_async_copy(a, b, sems.at[k]) for k, (a, b) in enumerate(pairs)]
    for copy in copies:
        copy.start()
    for copy in copies:
        copy.wait()
    rows, width = tokens_ref.shape
    out_ref[:, :width] = tokens_ref[...]
    values = gates_ref[...]
    high = values.astype(BF16).astype(F32)
    middle = (values - high).astype(BF16).astype(F32)
    low = values - high - middle
    fields = jnp.concatenate([ids_ref[...].astype(F32), high, middle, low], axis=0)
    fields = jnp.pad(fields, ((0, LANES - fields.shape[0]), (0, LANES - rows)))
    out_ref[:, width:] = jnp.transpose(fields)[:rows].astype(BF16)


def stack_kernel(count, later, *refs):
    parts, out_ref = refs[:count], refs[-1 - later]
    rows = parts[0].shape[0]
    for k, part in enumerate(parts):
        out_ref[k * rows : (k + 1) * rows] = part[...]
    if later:
        refs[-1][...] = refs[count][...]


def stack(parts, after, name, later=()):
    rows, width = parts[0].shape
    outs = call(
        functools.partial(stack_kernel, len(parts), len(later)),
        name,
        [shaped(BF16, rows * len(parts), width)] + [shaped(BF16, *array.shape) for array in later],
        [*parts, *later, *after],
        specs=[VECTORS] * (len(parts) + len(later)) + [ANYWHERE] * len(after),
        limit=16,
    )
    return outs if later else outs[0]


def add_kernel(count, skip, pieces, *refs):
    parts, outs = refs[:count], refs[count + skip : count + skip + pieces]
    total = parts[0][...].astype(F32)
    for part in parts[1:]:
        total = total + part[...].astype(F32)
    total = total.astype(BF16).reshape((pieces,) + outs[0].shape)
    for k, out in enumerate(outs):
        out[...] = total[k]


def add(parts, pieces, after, name, later=()):
    *lead, rows, width = parts[0].shape
    each = math.prod(lead) * rows // pieces
    first = len(parts) + len(after)
    return call(
        functools.partial(add_kernel, len(parts), len(after) + len(later), pieces),
        name,
        [shaped(BF16, each, width)] * pieces + [shaped(BF16, *array.shape) for array in later],
        [*parts, *after, *later],
        specs=[VECTORS] * len(parts) + [ANYWHERE] * (len(after) + len(later)),
        out_specs=[VECTORS] * pieces + [ANYWHERE] * len(later),
        aliases={first + k: pieces + k for k in range(len(later))},
    )


def doubled_along_z(grid, mine, meanwhile):
    column, k, done = mine, 1, None
    while k < grid.nz:
        got = grid.shift(column, dz=k)
        if 2 * k >= grid.nz:
            done = meanwhile(column)
        column = stack([column, got], [] if done is None else [done], "double")
        k *= 2
    return column, meanwhile(column) if done is None else done


def back_over_cores(grid, parts, after, name):
    got = [grid.shift(parts[c], dc=-c) for c in range(1, grid.nc)]
    return add([parts[0], *got], len(grid.square), after, name)


def back_over_plane(grid, kept, after, name, later=()):
    got = [grid.shift(part, dx=-a, dy=-b) for part, (a, b) in zip(kept[1:], grid.square[1:])]
    return add([kept[0], *got], grid.nz, after, name, later)


def back_along_z(grid, total):
    return [total[0]] + [grid.shift(total[k], dz=k) for k in range(1, grid.nz)]


def finish_kernel(count, *refs):
    for n, out in enumerate(refs[-2:]):
        total = refs[n * count][...].astype(F32)
        for part in refs[n * count + 1 : (n + 1) * count]:
            total = total + part[...].astype(F32)
        out[...] = total.astype(BF16)


def finish(first, second, after):
    return call(
        functools.partial(finish_kernel, len(first)),
        "finish",
        [shaped(BF16, *first[0].shape)] * 2,
        [*first, *second, *after],
        specs=[VECTORS] * (2 * len(first)) + [ANYWHERE] * len(after),
    )


def tables(aux, first, rows, local, block):
    tokens = aux.shape[0]
    across = jnp.transpose(aux.astype(F32))
    ids = [across[k : k + 1] for k in range(2)]
    gates = [across[2 + k : 3 + k] + across[4 + k : 5 + k] + across[6 + k : 7 + k] for k in range(2)]
    total = local * rows
    r = lax.broadcasted_iota(jnp.int32, (total, tokens), 0)
    j = lax.broadcasted_iota(jnp.int32, (total, tokens), 1)
    expert = ((r >> log2(rows)) + first).astype(F32)
    own_block = ((r & (rows - 1)) >> log2(CAP)) == (j >> log2(block))
    slot = (r & (CAP - 1)).astype(F32)
    hits = [(ids[k] == expert).astype(F32) for k in range(2)]
    hit = hits[0] + hits[1]
    up = lax.broadcasted_iota(jnp.int32, (tokens, tokens), 0)
    to = lax.broadcasted_iota(jnp.int32, (tokens, tokens), 1)
    earlier = ((up >> log2(block)) == (to >> log2(block))) & (up < to)
    position = dot(hit.astype(BF16), jnp.where(earlier, 1.0, 0.0).astype(BF16))
    select = jnp.where(own_block & (position == slot), hit, 0.0)
    gate = jnp.sum(select * (hits[0] * gates[0] + hits[1] * gates[1]), axis=1, keepdims=True)
    return select, gate


class Stream:
    def __init__(self, s, weight, room, sems, place, first=0):
        self.s, self.weight, self.room, self.sems, self.place = s, weight, room, sems, place
        for k in range(first, min(first + 2, s.slices)):
            for p in range(len(s.pieces)):
                self.copy(k, p).start()

    def slot(self, k, p):
        return lax.rem(k, 2) * len(self.s.pieces) + p

    def copy(self, k, p):
        at, size = self.s.pieces[p]
        start = pl.multiple_of(self.place(k) * self.s.width + at, LANES)
        slot = self.slot(k, p)
        return pltpu.make_async_copy(
            self.weight.at[:, :, pl.ds(start, size)], self.room.at[slot, :, :, pl.ds(0, size)], self.sems.at[slot]
        )

    def get(self, k, p):
        self.copy(k, p).wait()
        return self.room.at[self.slot(k, p), :, :, pl.ds(0, self.s.pieces[p][1])]

    def free(self, k, p):
        @pl.when(k + 2 < self.s.slices)
        def _():
            self.copy(k + 2, p).start()


def held_copy(s, weight, held, sems, k, p):
    at, size = s.pieces[p]
    columns = (slice(None), slice(None), pl.ds(pl.multiple_of(k * s.width + at, LANES), size))
    return pltpu.make_async_copy(weight.at[columns], held.at[columns], sems.at[k * len(s.pieces) + p])


def hold_kernel(s, weight, _, held, sems):
    copies = []
    for k in range(s.early):
        for at, size in s.pieces:
            source = pl.ds(pl.multiple_of(s.grid.source(k) * s.width + at, LANES), size)
            target = pl.ds(k * s.width + at, size)
            copies.append(
                pltpu.make_async_copy(weight.at[:, :, source], held.at[:, :, target], sems.at[len(copies)])
            )
            copies[-1].start()
    for copy in copies:
        copy.wait()


def hold(s, weight, after):
    (held,) = call(
        functools.partial(hold_kernel, s),
        "hold_down",
        [pltpu.VMEM((s.local, s.hidden, s.early * s.width), BF16)],
        [hbm(weight), after],
        specs=[ANYWHERE] * 2,
        scratch=[pltpu.SemaphoreType.DMA((s.early * len(s.pieces),))],
        cost=12000,
    )
    return held


class Sizes:
    def __init__(self, grid, tokens, w_gate):
        self.grid = grid
        self.local, self.hidden, self.features = w_gate.shape
        self.block, self.width = tokens.shape
        self.rows = grid.dp * CAP
        self.total = self.local * self.rows
        self.count = grid.dp * self.block
        self.column = grid.nz * self.block
        self.blocks = grid.nc * grid.ny * grid.nx
        self.slices = grid.nc * grid.ny
        whole = self.width % 256 == 0 and self.width > 1024
        self.pieces = [(0, 1024), (1024, self.width - 1024)] if whole else [(0, self.width)]
        self.early = self.slices // EARLY

    def block_of(self, blocks, c, a, b):
        n = self.grid.square.index((a, b)) - 1
        return blocks[2 * c] if n < 0 else blocks[2 * c + 1].at[n * self.column : (n + 1) * self.column]

    def at(self, e):
        return slice(e * self.rows, (e + 1) * self.rows)


def routed(s, blocks, select):
    for k in range(s.slices):
        group = [s.block_of(blocks, k // s.grid.ny, a, k % s.grid.ny)[:, : s.width] for a in range(s.grid.nx)]
        yield k, dot(select, jnp.concatenate(group, axis=0))


def gate_up_kernel(s, *refs):
    blocks, refs = refs[: 2 * s.grid.nc], refs[2 * s.grid.nc :]
    wg_ref, wu_ref, _, x_ref, select_ref, back_ref, gate_ref, act_ref, p_ref, q_ref, held_ref = refs[:11]
    room, sems, held_sems, g_acc, u_acc = refs[11:]
    ups = Stream(s, wu_ref, room, sems, lambda k: k)
    for k in range(min(2, s.slices)):
        for p in range(len(s.pieces)):
            held_copy(s, wg_ref, held_ref, held_sems, k, p).start()
    aux = jnp.concatenate([s.block_of(blocks, 0, a, 0)[:, s.width :] for a in range(s.grid.nx)], axis=0)
    select, gate = tables(aux, lax.axis_index("hst") * s.local, s.rows, s.local, s.block)
    gate_ref[...] = jnp.broadcast_to(gate, gate_ref.shape)
    select_ref[...] = select.astype(BF16)
    back_ref[...] = jnp.transpose(select).astype(BF16)
    for k, picked in routed(s, blocks, select.astype(BF16)):
        x_ref[s.grid.source(k)] = picked.astype(BF16)
    g_acc[...] = jnp.zeros_like(g_acc)
    u_acc[...] = jnp.zeros_like(u_acc)

    def step(k, _):
        for p, (at, size) in enumerate(s.pieces):

            @pl.when(k + 2 < s.slices)
            def _():
                held_copy(s, wg_ref, held_ref, held_sems, k + 2, p).start()

            held_copy(s, wg_ref, held_ref, held_sems, k, p).wait()
            up = ups.get(k, p)
            gate = held_ref.at[:, :, pl.ds(pl.multiple_of(k * s.width + at, LANES), size)]
            for e in range(s.local):
                x = x_ref[k, s.at(e), at : at + size]
                g_acc[e] += dot_t(x, gate[e])
                u_acc[e] += dot_t(x, up[e])
            ups.free(k, p)
        return 0

    lax.fori_loop(0, s.slices, step, 0)
    for e in range(s.local):
        g, u = g_acc[e], u_acc[e]
        sigma = jax.nn.sigmoid(g)
        act_ref[e] = (g * sigma * u).astype(BF16)
        p_ref[e] = u * sigma * (1.0 + g * (1.0 - sigma))
        q_ref[e] = g * sigma


def to_tokens(s, k, at, found, back_ref, outs):
    sums = dot(back_ref[...], jnp.concatenate(found, axis=0)).astype(BF16)
    size = sums.shape[-1]
    sums = sums.reshape(s.grid.nx, s.column, size)
    for c, out in enumerate(outs):

        @pl.when(k >> log2(s.grid.ny) == c)
        def _():
            out[:, k & (s.grid.ny - 1), :, at : at + size] = sums


def forward_kernel(s, act_ref, gate_ref, back_ref, held_ref, w_ref, _, *refs):
    outs, (room, sems) = refs[:-2], refs[-2:]
    weights = Stream(s, w_ref, room, sems, s.grid.source, s.early)

    def step(k, _):
        for p, (at, size) in enumerate(s.pieces):
            use(k, p, at, weights.get(k, p))
            weights.free(k, p)
        return 0

    def use(k, p, at, weight):
        found = [(dot(act_ref[e], weight[e]) * gate_ref[s.at(e), :1]).astype(BF16) for e in range(s.local)]
        to_tokens(s, k, at, found, back_ref, outs)

    def early(k, _):
        for p, (at, size) in enumerate(s.pieces):
            use(k, p, at, held_ref.at[:, :, pl.ds(pl.multiple_of(k * s.width + at, LANES), size)])
        return 0

    lax.fori_loop(0, s.early, early, 0)
    lax.fori_loop(s.early, s.slices, step, 0)


def hidden_grads_kernel(s, *refs):
    blocks, refs = refs[: 2 * s.grid.nc], refs[2 * s.grid.nc :]
    select_ref, gate_ref, p_ref, q_ref, w_ref, _, d_ref, dg_ref, du_ref, room, sems, acc = refs
    weights = Stream(s, w_ref, room, sems, lambda k: k)
    for k, picked in routed(s, blocks, select_ref[...]):
        d_ref[s.grid.source(k)] = (picked * gate_ref[:, :1]).astype(BF16)
    acc[...] = jnp.zeros_like(acc)

    def step(k, _):
        for p, (at, size) in enumerate(s.pieces):
            weight = weights.get(k, p)
            for e in range(s.local):
                acc[e] += dot_t(d_ref[k, s.at(e), at : at + size], weight[e])
            weights.free(k, p)
        return 0

    lax.fori_loop(0, s.slices, step, 0)
    for e in range(s.local):
        dg_ref[e] = (acc[e] * p_ref[e]).astype(BF16)
        du_ref[e] = (acc[e] * q_ref[e]).astype(BF16)


def backward_kernel(s, dg_ref, du_ref, back_ref, act_ref, d_ref, held_ref, w_ref, _, *refs):
    outs, (out, room, sems, turned, store, store_sems) = refs[:-6], refs[-6:]
    weights = Stream(s, w_ref, room, sems, s.grid.source)
    turn(s, act_ref, turned)

    def copy(k, p):
        at, size = s.pieces[p]
        start = pl.multiple_of(s.grid.source(k) * s.width + at, LANES)
        return pltpu.make_async_copy(
            store.at[p, :, :, pl.ds(0, size)], out.at[:, :, pl.ds(start, size)], store_sems.at[p]
        )

    def step(k, _):
        for p, (at, size) in enumerate(s.pieces):
            gate = held_ref.at[:, :, pl.ds(pl.multiple_of(s.grid.source(k) * s.width + at, LANES), size)]
            up = weights.get(k, p)
            found = [(dot(dg_ref[e], gate[e]) + dot(du_ref[e], up[e])).astype(BF16) for e in range(s.local)]
            to_tokens(s, k, at, found, back_ref, outs)
            weights.free(k, p)

            @pl.when(k >= 1)
            def _():
                copy(k - 1, p).wait()

            for e in range(s.local):
                rows = d_ref[s.grid.source(k), s.at(e), at : at + size]
                store[p, e, :, :size] = dot(turned[e], rows).astype(BF16)
            copy(k, p).start()
        return 0

    lax.fori_loop(0, s.slices, step, 0)
    for p in range(len(s.pieces)):
        copy(s.slices - 1, p).wait()


def turn(s, left_ref, turned):
    for e in range(s.local):
        turned[e] = jnp.transpose(left_ref[e].astype(F32)).astype(BF16)


def grads_kernel(s, spans, skip, *refs):
    count = len(spans)
    lefts, rows_refs = refs[:count], refs[count : 2 * count]
    outs, (marker, turned, store, sems) = refs[2 * count + skip : -4], refs[-4:]
    marker[...] = jnp.zeros_like(marker)
    pieces = len(s.pieces)

    def copy(out, k, p):
        at, size = s.pieces[p]
        slot = lax.rem(k, 2) * pieces + p
        start = pl.multiple_of(k * s.width + at, LANES)
        return pltpu.make_async_copy(
            store.at[slot, :, :, pl.ds(0, size)], out.at[:, :, pl.ds(start, size)], sems.at[slot]
        )

    for (low, high), left_ref, rows_ref, out in zip(spans, lefts, rows_refs, outs):
        turn(s, left_ref, turned)

        def step(k, _):
            for p, (at, size) in enumerate(s.pieces):

                @pl.when(k >= low + 2)
                def _():
                    copy(out, k - 2, p).wait()

                for e in range(s.local):
                    rows = rows_ref[k, s.at(e), at : at + size]
                    store[lax.rem(k, 2) * pieces + p, e, :, :size] = dot(turned[e], rows).astype(BF16)
                copy(out, k, p).start()
            return 0

        lax.fori_loop(low, high, step, 0)
        for k in range(max(low, high - 2), high):
            for p in range(pieces):
                copy(out, k, p).wait()


def grads(s, name, lefts, rights, spans, after, into=()):
    room = max(size for _, size in s.pieces)
    count = len(lefts)
    slots = 2 * len(s.pieces)
    return call(
        functools.partial(grads_kernel, s, spans, 1 + len(into)),
        name,
        [shaped(BF16, s.local, s.hidden, s.features)] * count + [shaped(F32, 8, LANES)],
        [*lefts, *rights, after, *into],
        specs=[VECTORS] * (2 * count) + [ANYWHERE] * (1 + len(into)),
        out_specs=[ANYWHERE] * count + [VECTORS],
        scratch=[
            pltpu.VMEM((s.local, s.hidden, s.rows), BF16),
            pltpu.VMEM((slots, s.local, s.hidden, room), BF16),
            pltpu.SemaphoreType.DMA((slots,)),
        ],
        aliases={2 * count + 1 + n: n for n in range(len(into))},
        cost=46000,
    )


def body(tokens, cotangent, expert_ids, gate_values, w_gate, w_up, w_down):
    grid = Grid(lax.axis_size("dp"), lax.axis_size("hst"))
    s = Sizes(grid, tokens, w_gate)

    sources = [tokens, expert_ids.T, gate_values.T, cotangent]
    message, cotangent = call(
        pack_kernel,
        "pack",
        [shaped(BF16, s.block, s.width + LANES), shaped(BF16, s.block, s.width)],
        [hbm(source) for source in sources],
        specs=[ANYWHERE] * 4,
        scratch=[pltpu.VMEM(a.shape, a.dtype) for a in sources[:3]] + [pltpu.SemaphoreType.DMA((4,))],
    )
    x_parts = grid.along_z(message)
    x_column, cotangent = stack(x_parts, [], "stack_tokens", [cotangent])
    x_plane = grid.over_plane(x_column)
    d_column, held_down = doubled_along_z(grid, cotangent, lambda after: hold(s, w_down, after))
    x_others = stack([x_plane[at] for at in grid.square[1:]], [d_column], "stack_tokens_plane")
    x_blocks = grid.over_cores(x_column, x_others)
    d_column = stack([d_column], [x_others], "stack_cotangents")
    d_plane = grid.over_plane(d_column)
    room = max(size for _, size in s.pieces)
    slots = 2 * len(s.pieces)
    streams = [pltpu.VMEM((slots, s.local, s.hidden, room), BF16), pltpu.SemaphoreType.DMA((slots,))]

    hidden_shape = (s.local, s.rows, s.hidden)
    sums_room = pltpu.VMEM(hidden_shape, F32)
    rows_shape = shaped(BF16, s.slices, s.total, s.width)
    x_rows, select, back, gate, act, p, q, held_gate = call(
        functools.partial(gate_up_kernel, s),
        "gate_up",
        [
            rows_shape,
            shaped(BF16, s.total, s.count),
            shaped(BF16, s.count, s.total),
            shaped(F32, s.total, LANES),
            shaped(BF16, *hidden_shape),
            shaped(F32, *hidden_shape),
            shaped(F32, *hidden_shape),
            pltpu.VMEM(w_gate.shape, BF16),
        ],
        [*x_blocks, hbm(w_gate), hbm(w_up), d_column],
        specs=[VECTORS] * len(x_blocks) + [ANYWHERE] * 3,
        scratch=[*streams, pltpu.SemaphoreType.DMA((s.slices * len(s.pieces),)), sums_room, sums_room],
        cost=46000,
    )
    d_others = stack([d_plane[at] for at in grid.square[1:]], [gate], "stack_cotangents_plane")
    d_blocks = grid.over_cores(d_column, d_others)
    sums = shaped(BF16, grid.nx, grid.ny, s.column, s.width)
    out_parts = call(
        functools.partial(forward_kernel, s),
        "forward",
        [sums] * grid.nc,
        [act, gate, back, held_down, hbm(w_down), d_others],
        specs=[VECTORS] * 4 + [ANYWHERE] * 2,
        scratch=streams,
        cost=46000,
    )
    d_rows, d_gate, d_up = call(
        functools.partial(hidden_grads_kernel, s),
        "hidden_grads",
        [rows_shape, shaped(BF16, *hidden_shape), shaped(BF16, *hidden_shape)],
        [*d_blocks, select, gate, p, q, hbm(w_down), out_parts[0]],
        specs=[VECTORS] * (len(d_blocks) + 4) + [ANYWHERE] * 2,
        scratch=[*streams, sums_room],
        cost=46000,
    )
    mixed_kept = back_over_cores(grid, out_parts, [d_gate], "mixed_cores")
    *back_parts, grad_down = call(
        functools.partial(backward_kernel, s),
        "backward",
        [sums] * grid.nc + [shaped(BF16, *w_down.shape)],
        [d_gate, d_up, back, act, d_rows, held_gate, hbm(w_up), mixed_kept[0]],
        specs=[VECTORS] * 6 + [ANYWHERE] * 2,
        out_specs=[VECTORS] * grid.nc + [ANYWHERE],
        scratch=[
            *streams,
            pltpu.VMEM((s.local, s.hidden, s.rows), BF16),
            pltpu.VMEM((len(s.pieces), s.local, s.hidden, room), BF16),
            pltpu.SemaphoreType.DMA((len(s.pieces),)),
        ],
        cost=46000,
    )
    *mixed_total, last = back_over_plane(grid, mixed_kept, back_parts[:1], "mixed_plane", back_parts[-1:])
    token_kept = back_over_cores(grid, [*back_parts[:-1], last], [], "tokens_cores")
    spans = [(0, s.slices), (0, s.slices // 2), (s.slices // 2, s.slices)]
    grad_gate, grad_up, done = grads(
        s, "grad_gate_up", [d_gate, d_up], [x_rows, x_rows], spans[:2], token_kept[0]
    )
    token_total = back_over_plane(grid, token_kept, [done], "tokens_plane")
    grad_up, done = grads(s, "grad_up", [d_up], [x_rows], spans[2:], token_total[0], [grad_up])
    mixed, grad_tokens = finish(back_along_z(grid, mixed_total), back_along_z(grid, token_total), [done])
    return mixed, grad_tokens, grad_gate, grad_up, grad_down


def solution(mesh):
    return jax.shard_map(
        body,
        mesh=mesh,
        in_specs=(
            P("dp", "hst"),
            P("dp", "hst"),
            P("dp", None),
            P("dp", None),
            P("hst", "dp", None),
            P("hst", "dp", None),
            P("hst", "dp", None),
        ),
        out_specs=(
            P("dp", "hst"),
            P("dp", "hst"),
            P("hst", "dp", None),
            P("hst", "dp", None),
            P("hst", "dp", None),
        ),
        check_vma=False,
    )
```

```python
import functools
import math

import jax
import jax.numpy as jnp
from jax import lax
from jax.experimental import pallas as pl
from jax.experimental.pallas import tpu as pltpu
from jax.sharding import PartitionSpec as P

CAP = 4
LANES = 128
MIB = 1 << 20
MFLOP = 10**6
EARLY = 2
F32 = jnp.float32
BF16 = jnp.bfloat16
AXES = ("dp", "hst")


def dot(a, b):
    return lax.dot_general(a, b, (((1,), (0,)), ((), ())), preferred_element_type=F32)


def dot_t(a, b):
    return lax.dot_general(a, b, (((1,), (1,)), ((), ())), preferred_element_type=F32)


def log2(n):
    assert n & (n - 1) == 0
    return n.bit_length() - 1


class Grid:
    def __init__(self, dp, hst):
        self.dp, self.hst = dp, hst
        self.nc = 2 if hst % 2 == 0 else 1
        self.ny = hst // self.nc
        self.nx = self.ny if dp % self.ny == 0 else 1
        self.nz = dp // self.nx
        assert self.nz & (self.nz - 1) == 0
        self.square = [(a, b) for a in range(self.nx) for b in range(self.ny)]

    def shift(self, value, dz=0, dx=0, dy=0, dc=0):
        pairs = []
        for z in range(self.nz):
            for x in range(self.nx):
                for y in range(self.ny):
                    for c in range(self.nc):
                        to_dp = (z ^ dz) * self.nx + (x + dx) % self.nx
                        to_hst = (y + dy) % self.ny * self.nc + (c + dc) % self.nc
                        here = (z * self.nx + x) * self.hst + y * self.nc + c
                        pairs.append((here, to_dp * self.hst + to_hst))
        return lax.ppermute(value, AXES, pairs)

    def along_z(self, mine):
        return [mine] + [self.shift(mine, dz=k) for k in range(1, self.nz)]

    def over_plane(self, column):
        return {(a, b): self.shift(column, dx=a, dy=b) if a or b else column for a, b in self.square}

    def over_cores(self, column, others):
        blocks = [column, others]
        for c in range(1, self.nc):
            blocks += [self.shift(column, dc=c), self.shift(others, dc=c)]
        return blocks

    def source(self, k):
        host = lax.axis_index("hst")
        y, core = host >> log2(self.nc), host & (self.nc - 1)
        from_y = (y - (k & (self.ny - 1))) & (self.ny - 1)
        return (from_y << log2(self.nc)) + ((core + (k >> log2(self.ny))) & (self.nc - 1))


def call(kernel, name, outs, args, specs=None, out_specs=None, scratch=(), grid=(), limit=16, cost=0, aliases=None):
    specs = specs or [pl.BlockSpec(memory_space=pltpu.VMEM)] * len(args)
    out_specs = out_specs or [pl.BlockSpec(memory_space=pltpu.VMEM)] * len(outs)
    return pl.pallas_call(
        kernel,
        name=name,
        grid=grid,
        out_shape=outs,
        in_specs=specs,
        out_specs=out_specs,
        scratch_shapes=list(scratch),
        input_output_aliases=aliases or {},
        compiler_params=pltpu.CompilerParams(vmem_limit_bytes=limit * MIB),
        cost_estimate=pl.CostEstimate(flops=cost * MFLOP, bytes_accessed=0, transcendentals=0),
    )(*args)


def shaped(dtype, *dims):
    return jax.ShapeDtypeStruct(dims, dtype)


VECTORS = pl.BlockSpec(memory_space=pltpu.VMEM)
ANYWHERE = pl.BlockSpec(memory_space=pl.ANY)


def hbm(weight):
    return pltpu.with_memory_space_constraint(weight, pltpu.HBM)


def pack_kernel(tokens, ids, gates, later, out_ref, later_ref, tokens_ref, ids_ref, gates_ref, sems):
    pairs = [(tokens, tokens_ref), (ids, ids_ref), (gates, gates_ref), (later, later_ref)]
    copies = [pltpu.make_async_copy(a, b, sems.at[k]) for k, (a, b) in enumerate(pairs)]
    for copy in copies:
        copy.start()
    for copy in copies:
        copy.wait()
    rows, width = tokens_ref.shape
    out_ref[:, :width] = tokens_ref[...]
    values = gates_ref[...]
    high = values.astype(BF16).astype(F32)
    middle = (values - high).astype(BF16).astype(F32)
    low = values - high - middle
    fields = jnp.concatenate([ids_ref[...].astype(F32), high, middle, low], axis=0)
    fields = jnp.pad(fields, ((0, LANES - fields.shape[0]), (0, LANES - rows)))
    out_ref[:, width:] = jnp.transpose(fields)[:rows].astype(BF16)


def stack_kernel(count, later, *refs):
    parts, out_ref = refs[:count], refs[-1 - later]
    rows = parts[0].shape[0]
    for k, part in enumerate(parts):
        out_ref[k * rows : (k + 1) * rows] = part[...]
    if later:
        refs[-1][...] = refs[count][...]


def stack(parts, after, name, later=()):
    rows, width = parts[0].shape
    outs = call(
        functools.partial(stack_kernel, len(parts), len(later)),
        name,
        [shaped(BF16, rows * len(parts), width)] + [shaped(BF16, *array.shape) for array in later],
        [*parts, *later, *after],
        specs=[VECTORS] * (len(parts) + len(later)) + [ANYWHERE] * len(after),
        limit=16,
    )
    return outs if later else outs[0]


def add_kernel(count, skip, pieces, *refs):
    parts, outs = refs[:count], refs[count + skip : count + skip + pieces]
    total = parts[0][...].astype(F32)
    for part in parts[1:]:
        total = total + part[...].astype(F32)
    total = total.astype(BF16).reshape((pieces,) + outs[0].shape)
    for k, out in enumerate(outs):
        out[...] = total[k]


def add(parts, pieces, after, name, later=()):
    *lead, rows, width = parts[0].shape
    each = math.prod(lead) * rows // pieces
    first = len(parts) + len(after)
    return call(
        functools.partial(add_kernel, len(parts), len(after) + len(later), pieces),
        name,
        [shaped(BF16, each, width)] * pieces + [shaped(BF16, *array.shape) for array in later],
        [*parts, *after, *later],
        specs=[VECTORS] * len(parts) + [ANYWHERE] * (len(after) + len(later)),
        out_specs=[VECTORS] * pieces + [ANYWHERE] * len(later),
        aliases={first + k: pieces + k for k in range(len(later))},
    )


def doubled_along_z(grid, mine, meanwhile):
    column, k, done = mine, 1, None
    while k < grid.nz:
        got = grid.shift(column, dz=k)
        if 2 * k >= grid.nz:
            done = meanwhile(column)
        column = stack([column, got], [] if done is None else [done], "double")
        k *= 2
    return column, meanwhile(column) if done is None else done


def back_over_cores(grid, parts, after, name):
    got = [grid.shift(parts[c], dc=-c) for c in range(1, grid.nc)]
    return add([parts[0], *got], len(grid.square), after, name)


def back_over_plane(grid, kept, after, name, later=()):
    got = [grid.shift(part, dx=-a, dy=-b) for part, (a, b) in zip(kept[1:], grid.square[1:])]
    return add([kept[0], *got], grid.nz, after, name, later)


def back_along_z(grid, total):
    return [total[0]] + [grid.shift(total[k], dz=k) for k in range(1, grid.nz)]


def finish_kernel(count, *refs):
    for n, out in enumerate(refs[-2:]):
        total = refs[n * count][...].astype(F32)
        for part in refs[n * count + 1 : (n + 1) * count]:
            total = total + part[...].astype(F32)
        out[...] = total.astype(BF16)


def finish(first, second, after):
    return call(
        functools.partial(finish_kernel, len(first)),
        "finish",
        [shaped(BF16, *first[0].shape)] * 2,
        [*first, *second, *after],
        specs=[VECTORS] * (2 * len(first)) + [ANYWHERE] * len(after),
    )


def tables(aux, first, rows, local, block):
    tokens = aux.shape[0]
    across = jnp.transpose(aux.astype(F32))
    ids = [across[k : k + 1] for k in range(2)]
    gates = [across[2 + k : 3 + k] + across[4 + k : 5 + k] + across[6 + k : 7 + k] for k in range(2)]
    total = local * rows
    r = lax.broadcasted_iota(jnp.int32, (total, tokens), 0)
    j = lax.broadcasted_iota(jnp.int32, (total, tokens), 1)
    expert = ((r >> log2(rows)) + first).astype(F32)
    own_block = ((r & (rows - 1)) >> log2(CAP)) == (j >> log2(block))
    slot = (r & (CAP - 1)).astype(F32)
    hits = [(ids[k] == expert).astype(F32) for k in range(2)]
    hit = hits[0] + hits[1]
    up = lax.broadcasted_iota(jnp.int32, (tokens, tokens), 0)
    to = lax.broadcasted_iota(jnp.int32, (tokens, tokens), 1)
    earlier = ((up >> log2(block)) == (to >> log2(block))) & (up < to)
    position = dot(hit.astype(BF16), jnp.where(earlier, 1.0, 0.0).astype(BF16))
    select = jnp.where(own_block & (position == slot), hit, 0.0)
    gate = jnp.sum(select * (hits[0] * gates[0] + hits[1] * gates[1]), axis=1, keepdims=True)
    return select, gate


class Stream:
    def __init__(self, s, weight, room, sems, place, first=0):
        self.s, self.weight, self.room, self.sems, self.place = s, weight, room, sems, place
        for k in range(first, min(first + 2, s.slices)):
            for p in range(len(s.pieces)):
                self.copy(k, p).start()

    def slot(self, k, p):
        return lax.rem(k, 2) * len(self.s.pieces) + p

    def copy(self, k, p):
        at, size = self.s.pieces[p]
        start = pl.multiple_of(self.place(k) * self.s.width + at, LANES)
        slot = self.slot(k, p)
        return pltpu.make_async_copy(
            self.weight.at[:, :, pl.ds(start, size)], self.room.at[slot, :, :, pl.ds(0, size)], self.sems.at[slot]
        )

    def get(self, k, p):
        self.copy(k, p).wait()
        return self.room.at[self.slot(k, p), :, :, pl.ds(0, self.s.pieces[p][1])]

    def free(self, k, p):
        @pl.when(k + 2 < self.s.slices)
        def _():
            self.copy(k + 2, p).start()


def held_copy(s, weight, held, sems, k, p):
    at, size = s.pieces[p]
    columns = (slice(None), slice(None), pl.ds(pl.multiple_of(k * s.width + at, LANES), size))
    return pltpu.make_async_copy(weight.at[columns], held.at[columns], sems.at[k * len(s.pieces) + p])


def hold_kernel(s, weight, _, held, sems):
    copies = []
    for k in range(s.early):
        for at, size in s.pieces:
            source = pl.ds(pl.multiple_of(s.grid.source(k) * s.width + at, LANES), size)
            target = pl.ds(k * s.width + at, size)
            copies.append(
                pltpu.make_async_copy(weight.at[:, :, source], held.at[:, :, target], sems.at[len(copies)])
            )
            copies[-1].start()
    for copy in copies:
        copy.wait()


def hold(s, weight, after):
    (held,) = call(
        functools.partial(hold_kernel, s),
        "hold_down",
        [pltpu.VMEM((s.local, s.hidden, s.early * s.width), BF16)],
        [hbm(weight), after],
        specs=[ANYWHERE] * 2,
        scratch=[pltpu.SemaphoreType.DMA((s.early * len(s.pieces),))],
        cost=12000,
    )
    return held


class Sizes:
    def __init__(self, grid, tokens, w_gate):
        self.grid = grid
        self.local, self.hidden, self.features = w_gate.shape
        self.block, self.width = tokens.shape
        self.rows = grid.dp * CAP
        self.total = self.local * self.rows
        self.count = grid.dp * self.block
        self.column = grid.nz * self.block
        self.blocks = grid.nc * grid.ny * grid.nx
        self.slices = grid.nc * grid.ny
        whole = self.width % 256 == 0 and self.width > 1024
        self.pieces = [(0, 1024), (1024, self.width - 1024)] if whole else [(0, self.width)]
        self.early = self.slices // EARLY

    def block_of(self, blocks, c, a, b):
        n = self.grid.square.index((a, b)) - 1
        return blocks[2 * c] if n < 0 else blocks[2 * c + 1].at[n * self.column : (n + 1) * self.column]

    def at(self, e):
        return slice(e * self.rows, (e + 1) * self.rows)


def routed(s, blocks, select):
    for k in range(s.slices):
        group = [s.block_of(blocks, k // s.grid.ny, a, k % s.grid.ny)[:, : s.width] for a in range(s.grid.nx)]
        yield k, dot(select, jnp.concatenate(group, axis=0))


def gate_up_kernel(s, *refs):
    blocks, refs = refs[: 2 * s.grid.nc], refs[2 * s.grid.nc :]
    wg_ref, wu_ref, _, x_ref, select_ref, back_ref, gate_ref, act_ref, p_ref, q_ref, held_ref = refs[:11]
    room, sems, held_sems, g_acc, u_acc = refs[11:]
    ups = Stream(s, wu_ref, room, sems, lambda k: k)
    for k in range(min(2, s.slices)):
        for p in range(len(s.pieces)):
            held_copy(s, wg_ref, held_ref, held_sems, k, p).start()
    aux = jnp.concatenate([s.block_of(blocks, 0, a, 0)[:, s.width :] for a in range(s.grid.nx)], axis=0)
    select, gate = tables(aux, lax.axis_index("hst") * s.local, s.rows, s.local, s.block)
    gate_ref[...] = jnp.broadcast_to(gate, gate_ref.shape)
    select_ref[...] = select.astype(BF16)
    back_ref[...] = jnp.transpose(select).astype(BF16)
    for k, picked in routed(s, blocks, select.astype(BF16)):
        x_ref[s.grid.source(k)] = picked.astype(BF16)
    g_acc[...] = jnp.zeros_like(g_acc)
    u_acc[...] = jnp.zeros_like(u_acc)

    def step(k, _):
        for p, (at, size) in enumerate(s.pieces):

            @pl.when(k + 2 < s.slices)
            def _():
                held_copy(s, wg_ref, held_ref, held_sems, k + 2, p).start()

            held_copy(s, wg_ref, held_ref, held_sems, k, p).wait()
            up = ups.get(k, p)
            gate = held_ref.at[:, :, pl.ds(pl.multiple_of(k * s.width + at, LANES), size)]
            for e in range(s.local):
                x = x_ref[k, s.at(e), at : at + size]
                g_acc[e] += dot_t(x, gate[e])
                u_acc[e] += dot_t(x, up[e])
            ups.free(k, p)
        return 0

    lax.fori_loop(0, s.slices, step, 0)
    for e in range(s.local):
        g, u = g_acc[e], u_acc[e]
        sigma = jax.nn.sigmoid(g)
        act_ref[e] = (g * sigma * u).astype(BF16)
        p_ref[e] = u * sigma * (1.0 + g * (1.0 - sigma))
        q_ref[e] = g * sigma


def to_tokens(s, k, at, found, back_ref, outs):
    sums = dot(back_ref[...], jnp.concatenate(found, axis=0)).astype(BF16)
    size = sums.shape[-1]
    sums = sums.reshape(s.grid.nx, s.column, size)
    for c, out in enumerate(outs):

        @pl.when(k >> log2(s.grid.ny) == c)
        def _():
            out[:, k & (s.grid.ny - 1), :, at : at + size] = sums


def forward_kernel(s, act_ref, gate_ref, back_ref, held_ref, w_ref, _, *refs):
    outs, (room, sems) = refs[:-2], refs[-2:]
    weights = Stream(s, w_ref, room, sems, s.grid.source, s.early)

    def step(k, _):
        for p, (at, size) in enumerate(s.pieces):
            use(k, p, at, weights.get(k, p))
            weights.free(k, p)
        return 0

    def use(k, p, at, weight):
        found = [(dot(act_ref[e], weight[e]) * gate_ref[s.at(e), :1]).astype(BF16) for e in range(s.local)]
        to_tokens(s, k, at, found, back_ref, outs)

    def early(k, _):
        for p, (at, size) in enumerate(s.pieces):
            use(k, p, at, held_ref.at[:, :, pl.ds(pl.multiple_of(k * s.width + at, LANES), size)])
        return 0

    lax.fori_loop(0, s.early, early, 0)
    lax.fori_loop(s.early, s.slices, step, 0)


def hidden_grads_kernel(s, *refs):
    blocks, refs = refs[: 2 * s.grid.nc], refs[2 * s.grid.nc :]
    select_ref, gate_ref, p_ref, q_ref, w_ref, _, d_ref, dg_ref, du_ref, room, sems, acc = refs
    weights = Stream(s, w_ref, room, sems, lambda k: k)
    for k, picked in routed(s, blocks, select_ref[...]):
        d_ref[s.grid.source(k)] = (picked * gate_ref[:, :1]).astype(BF16)
    acc[...] = jnp.zeros_like(acc)

    def step(k, _):
        for p, (at, size) in enumerate(s.pieces):
            weight = weights.get(k, p)
            for e in range(s.local):
                acc[e] += dot_t(d_ref[k, s.at(e), at : at + size], weight[e])
            weights.free(k, p)
        return 0

    lax.fori_loop(0, s.slices, step, 0)
    for e in range(s.local):
        dg_ref[e] = (acc[e] * p_ref[e]).astype(BF16)
        du_ref[e] = (acc[e] * q_ref[e]).astype(BF16)


def backward_kernel(s, dg_ref, du_ref, back_ref, held_ref, w_ref, _, *refs):
    outs, (room, sems) = refs[:-2], refs[-2:]
    weights = Stream(s, w_ref, room, sems, s.grid.source)

    def step(k, _):
        for p, (at, size) in enumerate(s.pieces):
            gate = held_ref.at[:, :, pl.ds(pl.multiple_of(s.grid.source(k) * s.width + at, LANES), size)]
            up = weights.get(k, p)
            found = [(dot(dg_ref[e], gate[e]) + dot(du_ref[e], up[e])).astype(BF16) for e in range(s.local)]
            to_tokens(s, k, at, found, back_ref, outs)
            weights.free(k, p)
        return 0

    lax.fori_loop(0, s.slices, step, 0)


def turn(s, left_ref, turned):
    for e in range(s.local):
        zeros = jnp.zeros((s.rows, s.hidden), F32)
        rows = [left_ref[e].astype(F32) if n == e else zeros for n in range(s.local)]
        turned[e] = jnp.transpose(jnp.concatenate(rows, axis=0)).astype(BF16)


def grads_kernel(s, count, *refs):
    lefts, rows_refs = refs[:count], refs[count : 2 * count]
    outs, (marker, turned, store, sems) = refs[2 * count + 1 : -4], refs[-4:]
    marker[...] = jnp.zeros_like(marker)
    pieces = len(s.pieces)

    def copy(out, k, p):
        at, size = s.pieces[p]
        slot = lax.rem(k, 2) * pieces + p
        start = pl.multiple_of(k * s.width + at, LANES)
        return pltpu.make_async_copy(
            store.at[slot, :, :, pl.ds(0, size)], out.at[:, :, pl.ds(start, size)], sems.at[slot]
        )

    for left_ref, rows_ref, out in zip(lefts, rows_refs, outs):
        turn(s, left_ref, turned)

        def step(k, _):
            for p, (at, size) in enumerate(s.pieces):

                @pl.when(k >= 2)
                def _():
                    copy(out, k - 2, p).wait()

                left = turned[...].reshape(s.local * s.hidden, s.total)
                value = dot(left, rows_ref[k, :, at : at + size]).astype(BF16)
                store[lax.rem(k, 2) * pieces + p, :, :, :size] = value.reshape(s.local, s.hidden, size)
                copy(out, k, p).start()
            return 0

        lax.fori_loop(0, s.slices, step, 0)
        for k in range(max(0, s.slices - 2), s.slices):
            for p in range(pieces):
                copy(out, k, p).wait()


def grads(s, name, lefts, rights, after):
    room = max(size for _, size in s.pieces)
    count = len(lefts)
    slots = 2 * len(s.pieces)
    return call(
        functools.partial(grads_kernel, s, count),
        name,
        [shaped(BF16, s.local, s.hidden, s.features)] * count + [shaped(F32, 8, LANES)],
        [*lefts, *rights, after],
        specs=[VECTORS] * (2 * count) + [ANYWHERE],
        out_specs=[ANYWHERE] * count + [VECTORS],
        scratch=[
            pltpu.VMEM((s.local, s.hidden, s.total), BF16),
            pltpu.VMEM((slots, s.local, s.hidden, room), BF16),
            pltpu.SemaphoreType.DMA((slots,)),
        ],
        cost=46000,
    )


def body(tokens, cotangent, expert_ids, gate_values, w_gate, w_up, w_down):
    grid = Grid(lax.axis_size("dp"), lax.axis_size("hst"))
    s = Sizes(grid, tokens, w_gate)

    sources = [tokens, expert_ids.T, gate_values.T, cotangent]
    message, cotangent = call(
        pack_kernel,
        "pack",
        [shaped(BF16, s.block, s.width + LANES), shaped(BF16, s.block, s.width)],
        [hbm(source) for source in sources],
        specs=[ANYWHERE] * 4,
        scratch=[pltpu.VMEM(a.shape, a.dtype) for a in sources[:3]] + [pltpu.SemaphoreType.DMA((4,))],
    )
    x_parts = grid.along_z(message)
    x_column, cotangent = stack(x_parts, [], "stack_tokens", [cotangent])
    x_plane = grid.over_plane(x_column)
    d_column, held_down = doubled_along_z(grid, cotangent, lambda after: hold(s, w_down, after))
    x_others = stack([x_plane[at] for at in grid.square[1:]], [d_column], "stack_tokens_plane")
    x_blocks = grid.over_cores(x_column, x_others)
    d_column = stack([d_column], [x_others], "stack_cotangents")
    d_plane = grid.over_plane(d_column)
    room = max(size for _, size in s.pieces)
    slots = 2 * len(s.pieces)
    streams = [pltpu.VMEM((slots, s.local, s.hidden, room), BF16), pltpu.SemaphoreType.DMA((slots,))]

    hidden_shape = (s.local, s.rows, s.hidden)
    sums_room = pltpu.VMEM(hidden_shape, F32)
    rows_shape = shaped(BF16, s.slices, s.total, s.width)
    x_rows, select, back, gate, act, p, q, held_gate = call(
        functools.partial(gate_up_kernel, s),
        "gate_up",
        [
            rows_shape,
            shaped(BF16, s.total, s.count),
            shaped(BF16, s.count, s.total),
            shaped(F32, s.total, LANES),
            shaped(BF16, *hidden_shape),
            shaped(F32, *hidden_shape),
            shaped(F32, *hidden_shape),
            pltpu.VMEM(w_gate.shape, BF16),
        ],
        [*x_blocks, hbm(w_gate), hbm(w_up), d_column],
        specs=[VECTORS] * len(x_blocks) + [ANYWHERE] * 3,
        scratch=[*streams, pltpu.SemaphoreType.DMA((s.slices * len(s.pieces),)), sums_room, sums_room],
        cost=46000,
    )
    d_others = stack([d_plane[at] for at in grid.square[1:]], [gate], "stack_cotangents_plane")
    d_blocks = grid.over_cores(d_column, d_others)
    sums = shaped(BF16, grid.nx, grid.ny, s.column, s.width)
    out_parts = call(
        functools.partial(forward_kernel, s),
        "forward",
        [sums] * grid.nc,
        [act, gate, back, held_down, hbm(w_down), d_others],
        specs=[VECTORS] * 4 + [ANYWHERE] * 2,
        scratch=streams,
        cost=46000,
    )
    d_rows, d_gate, d_up = call(
        functools.partial(hidden_grads_kernel, s),
        "hidden_grads",
        [rows_shape, shaped(BF16, *hidden_shape), shaped(BF16, *hidden_shape)],
        [*d_blocks, select, gate, p, q, hbm(w_down), out_parts[0]],
        specs=[VECTORS] * (len(d_blocks) + 4) + [ANYWHERE] * 2,
        scratch=[*streams, sums_room],
        cost=46000,
    )
    mixed_kept = back_over_cores(grid, out_parts, [d_gate], "mixed_cores")
    back_parts = call(
        functools.partial(backward_kernel, s),
        "backward",
        [sums] * grid.nc,
        [d_gate, d_up, back, held_gate, hbm(w_up), mixed_kept[0]],
        specs=[VECTORS] * 4 + [ANYWHERE] * 2,
        scratch=streams,
        cost=46000,
    )
    *mixed_total, last = back_over_plane(grid, mixed_kept, back_parts[:1], "mixed_plane", back_parts[-1:])
    token_kept = back_over_cores(grid, [*back_parts[:-1], last], [], "tokens_cores")
    grad_gate, grad_down, done = grads(s, "grad_gate_down", [d_gate, act], [x_rows, d_rows], token_kept[0])
    token_total = back_over_plane(grid, token_kept, [done], "tokens_plane")
    grad_up, done = grads(s, "grad_up", [d_up], [x_rows], token_total[0])
    mixed, grad_tokens = finish(back_along_z(grid, mixed_total), back_along_z(grid, token_total), [done])
    return mixed, grad_tokens, grad_gate, grad_up, grad_down


def solution(mesh):
    return jax.shard_map(
        body,
        mesh=mesh,
        in_specs=(
            P("dp", "hst"),
            P("dp", "hst"),
            P("dp", None),
            P("dp", None),
            P("hst", "dp", None),
            P("hst", "dp", None),
            P("hst", "dp", None),
        ),
        out_specs=(
            P("dp", "hst"),
            P("dp", "hst"),
            P("hst", "dp", None),
            P("hst", "dp", None),
            P("hst", "dp", None),
        ),
        check_vma=False,
    )
```
